32 devices in a mesh: groups: 2 (over y), dp: 4 (over z), nbr: 2 (over x), mp: 2 (over core).
Axes of the slice: x: 2, y: 2, z: 4, core: 2. Of those that a mesh axis runs over, the one named last changes fastest.
Arguments:
- hidden: bfloat16 [2048, 4096], P(('groups', 'dp', 'nbr'), 'mp'), parts along dimension 0, may hold values from -6 to 6
- grad_out: bfloat16 [2048, 4096], P(('groups', 'dp', 'nbr'), 'mp'), parts along dimension 0, may hold values from -6 to 6
- database: bfloat16 [128, 64, 896], P(('groups', 'dp', 'nbr')), parts along dimension 0, may hold values from -6 to 6
- enc_gain: float32 [896], replicated, may hold values from 0.25 to 1.75
- query_weight: bfloat16 [4096, 2048], P('dp', 'mp'), may hold values from -0.1875 to 0.1875
- key_weight: bfloat16 [896, 2048], P('dp', 'mp'), may hold values from -0.1875 to 0.1875
- value_weight: bfloat16 [896, 2048], P('dp', 'mp'), may hold values from -0.1875 to 0.1875
- out_weight: bfloat16 [2048, 4096], P('mp', 'dp'), may hold values from -0.375 to 0.375
- block_ids: int32 [32, 4], P(('groups', 'dp', 'nbr')), parts along dimension 0, may hold values from 0 to 7
- owners: int32 [32, 4], P(('groups', 'dp', 'nbr')), parts along dimension 0, may hold values from 0 to 1, as said below
Outputs:
- output: bfloat16 [2048, 4096], P(('groups', 'dp', 'nbr'), 'mp'), parts along dimension 0
- grad_hidden: bfloat16 [2048, 4096], P(('groups', 'dp', 'nbr'), 'mp'), parts along dimension 0
The draws below stay inside these ranges and needn't reach their ends.
There are 2 independent parts, one for each index of `groups`. The reference program is written for one: setup_inputs(seed, part) draws one part's arguments, and reference() takes and returns one part's arrays. A program takes and returns all parts, laid end to end along the dimension named above; an argument that names none is the same for every part. Nothing has to cross between parts.
Inputs may be any that keep to these rules, and one draw needn't show every extreme that they name: `owners`: of the 8 blocks named by one device's spans, exactly 4 have each owner.
All inputs are finite; a program needn't handle non-finite values.
Results may differ from the reference program's by a relative error of at most 0.0098.
Values may be sent and summed in bfloat16 or wider, within the bound.
No kernel may reach another device: no remote copies, remote signals or barrier semaphores. Data moves between devices by JAX's collectives and lax.ppermute only.
A program may use at most 128 MiB of HBM per device.

```python
import math
import jax
import jax.numpy as jnp
from jax import lax

D = 4096
E = 896
HEADS = 16
HD = 128
SPAN = 64
BLOCK = 64
SPAN_DEV = 2
BANK_DEV = 8
UPC = 4
UNITS = 8
CAP = 4
TOKENS = 1024
SPANS = 16
BANKS = 64
N_NBR = 2


def draw_owners(key, part):
    key = jax.random.fold_in(key, 7)
    devices = SPANS // SPAN_DEV
    subkeys = jax.random.split(key, devices)

    def draw_one(device_key):
        return jax.random.permutation(device_key, UNITS)
    shuffled = jax.vmap(draw_one)(subkeys)
    return (shuffled // CAP).astype(jnp.int32).reshape(SPANS, UPC)


def with_ends(array, stream_key, low, top_value):
    extent = array.shape
    spot = [jax.random.randint(jax.random.fold_in(stream_key, axis), (), 0, extent[axis]) for axis in range(len(extent))]
    array = array.at[tuple(spot)].set(low)
    longest = extent.index(max(extent))
    spot[longest] = (spot[longest] + 1) % extent[longest]
    return array.at[tuple(spot)].set(top_value)


def steps_of(stream_key, dims, cuts, low, high):
    gain, own = 1.0, jax.random.fold_in(stream_key, 6)
    for position, shards_of in cuts:
        draws = jnp.exp(jax.random.uniform(jax.random.fold_in(own, position), (shards_of,), jnp.float32, low / len(cuts), high / len(cuts)))
        gain = gain * jnp.repeat(draws, dims[position] // shards_of).reshape([-1 if axis == position else 1 for axis in range(len(dims))])
    return gain


def centred(key, shape, scale, bound, pieces=(), held_as=jnp.bfloat16):
    drawn = scale * jax.random.normal(key, shape, jnp.float32)
    if pieces:
        drawn = drawn * steps_of(key, shape, pieces, -0.22, 0.18)
    return jnp.clip(drawn, -bound, bound).astype(held_as)


def setup_inputs(seed: int = 0, part: int = 0) -> dict:
    key_list = jax.random.split(jax.random.key(seed), 11)
    part_splits = jax.random.split(jax.random.fold_in(key_list[10], part), 11)
    return {
        "hidden": centred(part_splits[0], (TOKENS, D), 1.0, 6.0, ((0, 8), (1, 2))),
        "grad_out": centred(part_splits[1], (TOKENS, D), 1.0, 6.0, ((0, 8), (1, 2))),
        "database": centred(part_splits[2], (BANKS, BLOCK, E), 1.0, 6.0, ((0, 8),)),
        "enc_gain": jnp.clip(1.0 + 0.15 * jax.random.normal(key_list[3], (E,), jnp.float32), 0.25, 1.75),
        "query_weight": centred(key_list[4], (D, HEADS * HD), (D // 4) ** -0.5, 0.1875, ((0, 4), (1, 2))),
        "key_weight": centred(key_list[5], (E, HEADS * HD), E ** -0.5, 0.1875, ((0, 4), (1, 2))),
        "value_weight": centred(key_list[6], (E, HEADS * HD), E ** -0.5, 0.1875, ((0, 4), (1, 2))),
        "out_weight": centred(key_list[7], (HEADS * HD, D), (HEADS * HD // 8) ** -0.5, 0.375, ((0, 2), (1, 4))),
        "block_ids": with_ends(jax.random.randint(part_splits[8], (SPANS, UPC), 0, BANK_DEV), jax.random.fold_in(part_splits[8], 1), 0, BANK_DEV - 1).astype(jnp.int32),
        "owners": draw_owners(jax.random.fold_in(jax.random.fold_in(key_list[10], part), 71), part),
    }


def neighbour_rows(database, block_ids, owners):
    span_index = jnp.arange(SPANS, dtype=jnp.int32)
    device_row = span_index // SPAN_DEV // N_NBR * N_NBR
    bank_rows = ((device_row[:, None] + owners) * BANK_DEV + block_ids).astype(jnp.int32)
    return database[bank_rows]

def encode_rows(states, enc_gain):
    widened = states.astype(jnp.float32)
    inverse = lax.rsqrt(lax.optimization_barrier(jnp.mean(widened * widened, axis=-1, keepdims=True)) + 1e-06)
    return (widened * inverse * enc_gain).astype(jnp.bfloat16)

def reference(hidden, grad_out, database, enc_gain, query_weight, key_weight, value_weight, out_weight, block_ids, owners):
    states = neighbour_rows(database, block_ids, owners).reshape(SPANS, UPC * BLOCK, E)
    neighbours = encode_rows(states, enc_gain)
    flattened = neighbours.reshape(SPANS * UPC * BLOCK, E)
    key_states = jnp.dot(flattened, key_weight, preferred_element_type=jnp.float32).astype(jnp.bfloat16)
    value_states = jnp.dot(flattened, value_weight, preferred_element_type=jnp.float32).astype(jnp.bfloat16)
    key_states = key_states.reshape(SPANS, UPC * BLOCK, HEADS, HD)
    value_states = value_states.reshape(SPANS, UPC * BLOCK, HEADS, HD)
    queries = jnp.dot(hidden, query_weight, preferred_element_type=jnp.float32).astype(jnp.bfloat16)
    queries = queries.reshape(SPANS, SPAN, HEADS, HD)
    score_scale = 1.0 / math.sqrt(HD)
    scores = jnp.einsum('cthd,cjhd->chtj', queries.astype(jnp.float32), key_states.astype(jnp.float32)) * score_scale
    attention = jax.nn.softmax(scores, axis=-1)
    attention_low = attention.astype(jnp.bfloat16)
    mixture = jnp.einsum('chtj,cjhd->cthd', attention_low.astype(jnp.float32), value_states.astype(jnp.float32))
    mixture = mixture.astype(jnp.bfloat16).reshape(TOKENS, HEADS * HD)
    output = (hidden.astype(jnp.float32) + jnp.dot(mixture, out_weight, preferred_element_type=jnp.float32)).astype(jnp.bfloat16)
    grad_mixture = jnp.dot(grad_out, out_weight.T, preferred_element_type=jnp.float32).astype(jnp.bfloat16)
    grad_mixture = grad_mixture.reshape(SPANS, SPAN, HEADS, HD)
    grad_attention = jnp.einsum('cthd,cjhd->chtj', grad_mixture.astype(jnp.float32), value_states.astype(jnp.float32))
    grad_scores = attention * (grad_attention - lax.optimization_barrier(jnp.sum(attention * grad_attention, axis=-1, keepdims=True))) * score_scale
    grad_scores = grad_scores.astype(jnp.bfloat16)
    grad_queries = jnp.einsum('chtj,cjhd->cthd', grad_scores.astype(jnp.float32), key_states.astype(jnp.float32))
    grad_queries = grad_queries.astype(jnp.bfloat16).reshape(TOKENS, HEADS * HD)
    grad_hidden = (grad_out.astype(jnp.float32) + jnp.dot(grad_queries, query_weight.T, preferred_element_type=jnp.float32)).astype(jnp.bfloat16)
    return (output, grad_hidden)
```

```python
import functools
import math

import jax
import jax.numpy as jnp
from jax import lax
from jax.experimental import pallas as pl
from jax.experimental.pallas import tpu as pltpu
from jax.sharding import PartitionSpec as P

HD = 128
SPAN = 64
BLOCK = 64
UPC = 4
UNITS = 8
AXES = ("groups", "dp", "nbr", "mp")
F32 = jnp.float32
BF16 = jnp.bfloat16


def encode_rows(states, enc_gain):
    widened = states.astype(F32)
    inverse = lax.rsqrt(jnp.mean(widened * widened, axis=-1, keepdims=True) + 1e-06)
    return (widened * inverse * enc_gain).astype(BF16)


def dot(a, b):
    return jnp.dot(a, b, preferred_element_type=F32)


def dot_t(a, b):
    return lax.dot_general(a, b, (((1,), (1,)), ((), ())), preferred_element_type=F32)


def take_blocks(idx_ref, kv_ref, span, cols):
    parts = []
    for u in range(UPC):
        row = pl.multiple_of(idx_ref[span, u] * BLOCK, BLOCK)
        parts.append(kv_ref[pl.ds(row, BLOCK), cols])
    return jnp.concatenate(parts, axis=0)


def forward_kernel(idx_ref, q_ref, kv_ref, mix_ref, att_ref):
    span = pl.program_id(0)
    width = q_ref.shape[1]
    for h in range(width // HD):
        cols = slice(h * HD, (h + 1) * HD)
        keys = take_blocks(idx_ref, kv_ref, span, cols)
        values = take_blocks(idx_ref, kv_ref, span, slice(width + h * HD, width + (h + 1) * HD))
        scores = dot_t(q_ref[:, cols], keys) * (1.0 / math.sqrt(HD))
        scores = jnp.exp(scores - jnp.max(scores, axis=-1, keepdims=True))
        attention = scores / jnp.sum(scores, axis=-1, keepdims=True)
        att_ref[0, h] = attention
        mix_ref[:, cols] = dot(attention.astype(BF16), values).astype(BF16)


def backward_kernel(idx_ref, gm_ref, kv_ref, att_ref, gq_ref):
    span = pl.program_id(0)
    width = gm_ref.shape[1]
    for h in range(width // HD):
        cols = slice(h * HD, (h + 1) * HD)
        keys = take_blocks(idx_ref, kv_ref, span, cols)
        values = take_blocks(idx_ref, kv_ref, span, slice(width + h * HD, width + (h + 1) * HD))
        grad_attention = dot_t(gm_ref[:, cols], values)
        attention = att_ref[0, h]
        inner = jnp.sum(attention * grad_attention, axis=-1, keepdims=True)
        grad_scores = attention * (grad_attention - inner) * (1.0 / math.sqrt(HD))
        gq_ref[:, cols] = dot(grad_scores.astype(BF16), keys).astype(BF16)


def attention_specs(kv, width, heads):
    row = pl.BlockSpec((SPAN, width), lambda i, idx: (i, 0))
    bank = pl.BlockSpec(kv.shape, lambda i, idx: (0, 0))
    att = pl.BlockSpec((1, heads, SPAN, UPC * BLOCK), lambda i, idx: (i, 0, 0, 0))
    return row, bank, att


def attention_forward(idx, q, kv):
    tokens, width = q.shape
    heads, spans = width // HD, tokens // SPAN
    row, bank, att = attention_specs(kv, width, heads)
    return pl.pallas_call(
        forward_kernel,
        grid_spec=pltpu.PrefetchScalarGridSpec(
            num_scalar_prefetch=1, grid=(spans,), in_specs=[row, bank], out_specs=[row, att]
        ),
        out_shape=(
            jax.ShapeDtypeStruct((tokens, width), BF16),
            jax.ShapeDtypeStruct((spans, heads, SPAN, UPC * BLOCK), F32),
        ),
        compiler_params=pltpu.CompilerParams(vmem_limit_bytes=32 << 20),
        name="attention_forward",
    )(idx, q, kv)


def attention_backward(idx, gm, kv, att):
    tokens, width = gm.shape
    heads, spans = width // HD, tokens // SPAN
    row, bank, att_spec = attention_specs(kv, width, heads)
    return pl.pallas_call(
        backward_kernel,
        grid_spec=pltpu.PrefetchScalarGridSpec(
            num_scalar_prefetch=1, grid=(spans,), in_specs=[row, bank, att_spec], out_specs=row
        ),
        out_shape=jax.ShapeDtypeStruct((tokens, width), BF16),
        compiler_params=pltpu.CompilerParams(vmem_limit_bytes=32 << 20),
        name="attention_backward",
    )(idx, gm, kv, att)


def flat(y, z, x, m):
    return ((y * 4 + z) * 2 + x) * 2 + m


def permutation(move):
    pairs = []
    for y in range(2):
        for z in range(4):
            for x in range(2):
                for m in range(2):
                    pairs.append((flat(y, z, x, m), flat(*move(y, z, x, m))))
    return pairs


RING = (0, 1, 3, 2)
NEXT = {RING[i]: RING[(i + 1) % 4] for i in range(4)}
PREV = {RING[i]: RING[(i + 3) % 4] for i in range(4)}
FIRST = permutation(lambda y, z, x, m: (y, z, 1 - x, m) if m == 0 else (1 - y, z, x, m))
SECOND = permutation(lambda y, z, x, m: (1 - y, z, x, m) if m == 0 else (y, z, 1 - x, m))
CORE = permutation(lambda y, z, x, m: (y, z, x, 1 - m))
UP = permutation(lambda y, z, x, m: (y, NEXT[z], x, m))
DOWN = permutation(lambda y, z, x, m: (y, PREV[z], x, m))


def move(array, pairs):
    return lax.ppermute(array, AXES, pairs)


def plane_gather(mine):
    first = move(mine, FIRST)
    far = move(jnp.stack((mine, first)), SECOND)
    return jnp.stack((mine, far[0], first, far[1]))


def core_swap(slots):
    other = move(slots, CORE)
    return jnp.stack((other[0], other[2], other[1], other[3]))


def plane_reduce(own_half, other_half):
    rows = own_half.shape[0] // 4
    total = own_half.reshape(4, rows, -1) + core_swap(
        other_half.astype(BF16).reshape(4, rows, -1)
    ).astype(F32)
    pair = total[:2] + move(total[2:].astype(BF16), FIRST).astype(F32)
    return pair[0] + move(pair[1].astype(BF16), SECOND).astype(F32)


def ring_gather(mine):
    up = move(mine, UP)
    down = move(mine, DOWN)
    far = move(up, UP)
    return up, down, far


def local_plane(
    hidden,
    grad_out,
    database,
    enc_gain,
    query_weight,
    key_weight,
    value_weight,
    out_weight,
    block_ids,
    owners,
):
    y, z, x, m = (lax.axis_index(a) for a in AXES)
    chip = y * 2 + x
    rows, half = hidden.shape
    width = query_weight.shape[1] // 4
    depth = query_weight.shape[0]
    nxt = jnp.array([NEXT[i] for i in range(4)], jnp.int32)[z]
    prv = jnp.array([PREV[i] for i in range(4)], jnp.int32)[z]
    sources = (z, prv, nxt, 3 - z)

    wq = lax.dynamic_slice_in_dim(query_weight, chip * width, width, 1)
    wkv = jnp.concatenate(
        (
            lax.dynamic_slice_in_dim(key_weight, chip * width, width, 1),
            lax.dynamic_slice_in_dim(value_weight, chip * width, width, 1),
        ),
        axis=1,
    )
    wo = lax.dynamic_slice_in_dim(out_weight, chip * width, width, 0)
    wq_parts = (wq,) + ring_gather(wq)
    wkv_parts = (wkv,) + ring_gather(wkv)
    wo_parts = (wo,) + ring_gather(wo)

    blocks = database.shape[0] // 2
    encoded = encode_rows(lax.dynamic_slice_in_dim(database, m * blocks, blocks, 0), enc_gain)
    encoded = encoded.reshape(blocks * BLOCK, -1)
    h_own = plane_gather(hidden)
    h_other = core_swap(h_own).reshape(4 * rows, half)
    h_own = h_own.reshape(4 * rows, half)
    e_own = plane_gather(encoded)
    e_other = core_swap(e_own)
    e_all = jnp.concatenate((e_own, e_other)).reshape(8 * blocks * BLOCK, -1)
    g_own = plane_gather(grad_out)
    g_other = core_swap(g_own).reshape(4 * rows, half)
    g_own = g_own.reshape(4 * rows, half)

    codes = lax.all_gather(jnp.stack((owners, block_ids)), ("groups", "nbr"), axis=0)
    slot = jnp.arange(4, dtype=jnp.int32)
    hi, lo = slot // 2, slot % 2
    slot_y = jnp.where(m == 0, lo, hi)
    slot_x = jnp.where(m == 0, hi, lo)
    codes = codes[(slot_y ^ y) * 2 + (slot_x ^ x)]
    own_of, id_of = codes[:, 0], codes[:, 1]
    rel_x = own_of ^ x
    rel_y = slot_y[:, None, None]
    bank = jnp.where(m == 0, rel_x * 2 + rel_y, rel_y * 2 + rel_x)
    idx = ((id_of // blocks) ^ m) * (4 * blocks) + bank * blocks + id_of % blocks
    idx = idx.reshape(-1, UPC)

    def assemble(parts, axis, places):
        shape = list(parts[0].shape)
        step = shape[axis]
        shape[axis] = 4 * step
        whole = jnp.zeros(shape, BF16)
        for part, place in zip(parts, places):
            whole = lax.dynamic_update_slice_in_dim(whole, part, place * step, axis)
        return whole

    halves = tuple(s ^ (2 * m) for s in sources)
    wq_all = assemble(wq_parts, 0, halves)
    wkv_all = assemble(wkv_parts, 0, sources)
    wo_all = assemble(wo_parts, 1, halves)
    wq_own, wq_other = wq_all[: 2 * depth], wq_all[2 * depth :]
    wo_own, wo_other = wo_all[:, : 2 * depth], wo_all[:, 2 * depth :]

    queries = (dot(h_own, wq_own) + dot(h_other, wq_other)).astype(BF16)
    kv = dot(e_all, wkv_all).astype(BF16)
    mixture, attention = attention_forward(idx, queries, kv)

    summed = plane_reduce(dot(mixture, wo_own), dot(mixture, wo_other))
    output = (hidden.astype(F32) + summed).astype(BF16)

    grad_mixture = (dot_t(g_own, wo_own) + dot_t(g_other, wo_other)).astype(BF16)
    grad_queries = attention_backward(idx, grad_mixture, kv, attention)
    grad_sum = plane_reduce(dot_t(grad_queries, wq_own), dot_t(grad_queries, wq_other))
    grad_hidden = (grad_out.astype(F32) + grad_sum).astype(BF16)
    return (output, grad_hidden)


def local_any(
    hidden,
    grad_out,
    database,
    enc_gain,
    query_weight,
    key_weight,
    value_weight,
    out_weight,
    block_ids,
    owners,
):
    tok_rows = hidden.shape[0]
    span_count = block_ids.shape[0]
    local_width = query_weight.shape[1]
    local_heads = local_width // HD
    owner_count = lax.axis_size("nbr")
    capacity = UNITS // owner_count
    score_scale = 1.0 / math.sqrt(HD)
    full_hidden, full_grad = (
        lax.all_gather(hidden, "mp", axis=1, tiled=True),
        lax.all_gather(grad_out, "mp", axis=1, tiled=True),
    )
    query_full, key_full, value_full, out_full = (
        lax.all_gather(query_weight, "dp", axis=0, tiled=True),
        lax.all_gather(key_weight, "dp", axis=0, tiled=True),
        lax.all_gather(value_weight, "dp", axis=0, tiled=True),
        lax.all_gather(out_weight, "dp", axis=1, tiled=True),
    )
    queries = jnp.dot(full_hidden, query_full, preferred_element_type=jnp.float32)
    queries = queries.astype(jnp.bfloat16).reshape(span_count, SPAN, local_heads, HD)
    owner_flat = owners.reshape(UNITS)
    id_flat = block_ids.reshape(UNITS)
    positions = jnp.arange(UNITS, dtype=jnp.int32)
    send_order = jnp.argsort(owner_flat * UNITS + positions)
    restore = jnp.argsort(send_order)
    requests = id_flat[send_order].reshape(owner_count, capacity)
    fetched = database[lax.all_to_all(requests, "nbr", split_axis=0, concat_axis=0, tiled=True)]
    encoded = encode_rows(fetched, enc_gain)
    key_part = jnp.einsum(
        "osbe,ef->osbf", encoded, key_full, preferred_element_type=jnp.float32
    ).astype(jnp.bfloat16)
    value_part = jnp.einsum(
        "osbe,ef->osbf", encoded, value_full, preferred_element_type=jnp.float32
    ).astype(jnp.bfloat16)
    stacked = jnp.concatenate((key_part, value_part), axis=-1)
    answers = lax.all_to_all(stacked, "nbr", split_axis=0, concat_axis=0, tiled=True)
    gathered = answers.reshape((UNITS,) + answers.shape[2:])[restore]
    kv_rows = gathered.reshape(span_count, UPC * BLOCK, 2 * local_width)
    key_rows = kv_rows[:, :, :local_width]
    value_rows = kv_rows[:, :, local_width:]
    key_rows = key_rows.reshape(span_count, UPC * BLOCK, local_heads, HD)
    value_rows = value_rows.reshape(span_count, UPC * BLOCK, local_heads, HD)
    scores = (
        jnp.einsum("cthd,cjhd->chtj", queries, key_rows, preferred_element_type=jnp.float32)
        * score_scale
    )
    attention = jax.nn.softmax(scores, axis=-1)
    attention_low = attention.astype(jnp.bfloat16)
    mixture = jnp.einsum(
        "chtj,cjhd->cthd", attention_low, value_rows, preferred_element_type=jnp.float32
    )
    mixture = mixture.astype(jnp.bfloat16).reshape(tok_rows, local_width)
    partial_out = jnp.dot(mixture, out_full, preferred_element_type=jnp.float32)
    summed = lax.psum_scatter(partial_out, "mp", scatter_dimension=1, tiled=True)
    output = (hidden.astype(jnp.float32) + summed).astype(jnp.bfloat16)
    grad_mixture = jnp.einsum("td,hd->th", full_grad, out_full, preferred_element_type=jnp.float32)
    grad_mixture = grad_mixture.astype(jnp.bfloat16).reshape(span_count, SPAN, local_heads, HD)
    grad_attention = jnp.einsum(
        "cthd,cjhd->chtj", grad_mixture, value_rows, preferred_element_type=jnp.float32
    )
    grad_scores = (
        attention
        * (grad_attention - jnp.sum(attention * grad_attention, axis=-1, keepdims=True))
        * score_scale
    )
    grad_scores = grad_scores.astype(jnp.bfloat16)
    grad_queries = jnp.einsum(
        "chtj,cjhd->cthd", grad_scores, key_rows, preferred_element_type=jnp.float32
    )
    grad_queries = grad_queries.astype(jnp.bfloat16).reshape(tok_rows, local_width)
    partial_grad = jnp.einsum(
        "th,dh->td", grad_queries, query_full, preferred_element_type=jnp.float32
    )
    grad_sum = lax.psum_scatter(partial_grad, "mp", scatter_dimension=1, tiled=True)
    grad_hidden = (grad_out.astype(jnp.float32) + grad_sum).astype(jnp.bfloat16)
    return (output, grad_hidden)


def solution(mesh):
    in_specs = (
        P(("groups", "dp", "nbr"), "mp"),
        P(("groups", "dp", "nbr"), "mp"),
        P(("groups", "dp", "nbr"), None, None),
        P(),
        P("dp", "mp"),
        P("dp", "mp"),
        P("dp", "mp"),
        P("mp", "dp"),
        P(("groups", "dp", "nbr"), None),
        P(("groups", "dp", "nbr"), None),
    )
    out_specs = (P(("groups", "dp", "nbr"), "mp"), P(("groups", "dp", "nbr"), "mp"))
    sizes = tuple(mesh.shape[a] for a in AXES)
    local = local_plane if sizes == (2, 4, 2, 2) else local_any
    return jax.shard_map(local, mesh=mesh, in_specs=in_specs, out_specs=out_specs, check_vma=False)
```

```python
import math

import jax
import jax.numpy as jnp
from jax import lax
from jax.experimental import pallas as pl
from jax.experimental.pallas import tpu as pltpu
from jax.sharding import PartitionSpec as P

HD = 128
SPAN = 64
BLOCK = 64
UPC = 4
UNITS = 8
AXES = ("groups", "dp", "nbr", "mp")
F32 = jnp.float32
BF16 = jnp.bfloat16


def encode_rows(states, enc_gain):
    widened = states.astype(F32)
    inverse = lax.rsqrt(jnp.mean(widened * widened, axis=-1, keepdims=True) + 1e-06)
    return (widened * inverse * enc_gain).astype(BF16)


def dot(a, b):
    return jnp.dot(a, b, preferred_element_type=F32)


def dot_t(a, b):
    return lax.dot_general(a, b, (((1,), (1,)), ((), ())), preferred_element_type=F32)


CROSSED = (0, 2, 1, 3)
TILE = 16
SCALE = 1.0 / math.sqrt(HD)
LONG = pl.CostEstimate(flops=10**11, bytes_accessed=1024, transcendentals=0)


def shape_of(shape, dtype=BF16):
    return jax.ShapeDtypeStruct(shape, dtype)


def kernel_call(body, name, scalars, operands, out_shapes, in_specs):
    whole = lambda a: pl.BlockSpec(a.shape, lambda i, *_, n=len(a.shape): (0,) * n)
    return pl.pallas_call(
        body,
        grid_spec=pltpu.PrefetchScalarGridSpec(
            num_scalar_prefetch=len(scalars),
            grid=(1,),
            in_specs=[sp or whole(a) for sp, a in zip(in_specs, operands)],
            out_specs=[whole(a) for a in out_shapes],
        ),
        out_shape=tuple(out_shapes),
        compiler_params=pltpu.CompilerParams(vmem_limit_bytes=56 << 20),
        cost_estimate=LONG,
        name=name,
    )(*scalars, *operands)


class Copies:
    def __init__(self, sems):
        self.sems, self.used, self.open = sems, 0, {}

    def start(self, name, source, target):
        copy = pltpu.make_async_copy(source, target, self.sems.at[self.used])
        self.used += 1
        copy.start()
        self.open.setdefault(name, []).append(copy)

    def wait(self, *names):
        for name in names:
            for copy in self.open.pop(name):
                copy.wait()


def copy_call(body, name, scalars, operands, out_shapes, scratch, copies):
    anywhere = pl.BlockSpec(memory_space=pl.ANY)
    smem = pl.BlockSpec(memory_space=pltpu.SMEM)
    need = sum(math.prod(a.shape) * jnp.dtype(a.dtype).itemsize for a in scratch)
    return pl.pallas_call(
        body,
        in_specs=[smem] * len(scalars) + [anywhere] * len(operands),
        out_specs=[anywhere] * len(out_shapes),
        out_shape=tuple(out_shapes),
        scratch_shapes=[pltpu.VMEM(a.shape, a.dtype) for a in scratch] + [pltpu.SemaphoreType.DMA((copies,))],
        compiler_params=pltpu.CompilerParams(vmem_limit_bytes=need + (10 << 20)),
        cost_estimate=LONG,
        name=name,
    )(*scalars, *operands)


def slices_kernel(place, q, k, v, o, out):
    depth, width = q.shape
    rank = k.shape[0]
    out[:rank] = k[...]
    out[rank : 2 * rank] = v[...]
    out[2 * rank : 2 * rank + depth] = q[...]
    for c in range(depth // width):
        at = 2 * rank + depth + c * width
        out[at : at + width] = o[:, c * width : (c + 1) * width]


def projection_slices(chip, qw, kw, vw, ow):
    depth, width, rank = qw.shape[0], qw.shape[1] // 4, kw.shape[0]
    column = lambda i, place: (0, place[0])
    return kernel_call(
        slices_kernel,
        "projection_slices",
        (chip.reshape(1),),
        (qw, kw, vw, ow),
        (shape_of((2 * rank + 2 * depth, width)),),
        [
            pl.BlockSpec((depth, width), column),
            pl.BlockSpec((rank, width), column),
            pl.BlockSpec((rank, width), column),
            pl.BlockSpec((width, depth), lambda i, place: (place[0], 0)),
        ],
    )[0]


def prepare_kernel(core, owners, ids, hid, db, gain, near, far):
    rows, half = hid.shape
    blocks, e = db.shape[0] // 2, db.shape[2]
    per = rows // BLOCK
    near[:, :half] = hid[...]
    for ref, which, start in ((near, core[0], half), (far, 1 - core[0], 0)):
        for part in range(blocks // per):
            states = db[pl.ds(which * blocks + part * per, per)].reshape(rows, e)
            ref[:, start + part * e : start + (part + 1) * e] = encode_rows(states, gain[...])
    lane = lax.broadcasted_iota(jnp.int32, (rows, near.shape[1] - half - blocks // per * e), 1)
    row = jnp.zeros(lane.shape, jnp.int32)
    for u in range(UNITS):
        at = divmod(u, UPC)
        row = jnp.where(lane == u, owners[at] * 2 * blocks + ids[at], row)
    near[:, near.shape[1] - lane.shape[1] :] = row.astype(F32).astype(BF16)


def prepare(core, owners, ids, hidden, db, gain):
    rows, half = hidden.shape
    wide = db.shape[0] // 2 * BLOCK // rows * db.shape[2]
    return kernel_call(
        prepare_kernel,
        "prepare",
        (core.reshape(1), owners, ids),
        (hidden, db, gain),
        (shape_of((rows, half + wide + 128)), shape_of((rows, wide))),
        [None] * 3,
    )


def rows_of(ref, first, count):
    return ref.at[pl.ds(first, count)]


def take_blocks(idx, kv, span, cols):
    parts = []
    for u in range(UPC):
        row = pl.multiple_of(idx[span, u] * TILE, TILE)
        parts.append(kv[pl.ds(row, BLOCK), cols])
    return jnp.concatenate(parts, axis=0)


def head_cols(width, h):
    return slice(h * HD, (h + 1) * HD), slice(width + h * HD, width + (h + 1) * HD)


def stage_tokens(copies, name, arrays, target):
    rows, half = arrays[0].shape[0], target.shape[1]
    for slot, a in enumerate(arrays):
        source = a.at[:, pl.ds(0, half)] if a.shape[1] > half else a
        copies.start(name, source, rows_of(target, slot * rows, rows))


def stage_output(copies, pos, parts, target):
    depth, width = parts[3].shape
    for r, part in enumerate(parts):
        for c in range(depth // width):
            at = part.shape[0] - depth + c * width
            place = pl.multiple_of(pos[r] * depth + c * width, width)
            copies.start("output", rows_of(part, at, width), target.at[:, pl.ds(place, width)])


def forward_kernel(src, idx, pos, *refs):
    banks, own, other, parts = refs[:8], refs[:4], refs[8:12], refs[12:16]
    kv_out, mix_out, att_out = refs[16:19]
    states, kvw, kv, near, far, weights, queries, mix, att, sems = refs[19:]
    e, columns = kvw.shape
    rank, rows, wide = e // 4, banks[0].shape[0], states.shape[1]
    half, width = near.shape[1], weights.shape[1]
    depth = weights.shape[0] // 4
    spans = att.shape[0]
    copies = Copies(sems)
    for r, part in enumerate(parts):
        place = pl.multiple_of(src[r] * rank, TILE)
        for c in range(2):
            target = kvw.at[pl.ds(place, rank), pl.ds(c * width, width)]
            copies.start("kvw", rows_of(part, c * rank, rank), target)
    for b, bank in enumerate(banks):
        start = 0 if b == 4 else bank.shape[1] - 128 - wide
        copies.start(b // 4, bank.at[:, pl.ds(start, wide)], rows_of(states, b * rows, rows))
    for r, part in enumerate(parts):
        place = pl.multiple_of(pos[r] * depth, depth)
        copies.start("query", rows_of(part, 2 * rank, depth), rows_of(weights, place, depth))
    stage_tokens(copies, "near", own, near)
    stage_tokens(copies, "far", other, far)
    copies.wait("kvw")
    for side in range(2):
        copies.wait(side)
        for c in range(wide // e):
            block = states[4 * side * rows : 4 * (side + 1) * rows, c * e : (c + 1) * e]
            at = (8 * c + 4 * side) * rows
            kv[at : at + 4 * rows] = dot(block, kvw[...]).astype(BF16)
    copies.start("out", kv, kv_out)
    copies.wait("query", "near")
    total = dot(near[...], weights[:half])
    copies.wait("far")
    queries[...] = (total + dot(far[...], weights[half:])).astype(BF16)
    for span in range(spans):
        rows = slice(span * SPAN, (span + 1) * SPAN)
        heads = range(width // HD)
        cols = [head_cols(width, h) for h in heads]
        scores = [dot_t(queries[rows, kc], take_blocks(idx, kv, span, kc)) * SCALE for kc, _ in cols]
        scores = [jnp.exp(s - jnp.max(s, axis=-1, keepdims=True)) for s in scores]
        scores = [s * (1.0 / jnp.sum(s, axis=-1, keepdims=True)) for s in scores]
        for h in heads:
            att[span, h] = scores[h]
            kc, vc = cols[h]
            mix[rows, kc] = dot(scores[h].astype(BF16), take_blocks(idx, kv, span, vc)).astype(BF16)
        if span % 2:
            copies.start("out", rows_of(att, span - 1, 2), rows_of(att_out, span - 1, 2))
    copies.start("out", mix, mix_out)
    copies.wait("out")


def forward(src, idx, pos, own, far_states, other, parts, half, e, depth):
    rows, width = own[0].shape[0], parts[0].shape[1]
    tokens = 4 * rows
    spans = tokens // SPAN
    wide = far_states.shape[1]
    kv = shape_of((8 * wide // e * rows, 2 * width))
    mix = shape_of((tokens, width))
    att = shape_of((spans, width // HD, SPAN, UPC * BLOCK), F32)
    side = shape_of((tokens, half))
    return copy_call(
        forward_kernel,
        "forward",
        (src, idx, pos),
        (*own, far_states, *other[1:], *other, *parts),
        (kv, mix, att),
        (
            shape_of((8 * rows, wide)),
            shape_of((e, 2 * width)),
            kv,
            side,
            side,
            shape_of((4 * depth, width)),
            mix,
            mix,
            att,
        ),
        30 + spans // 2,
    )


def output_kernel(pos, *refs):
    mix_in, parts = refs[0], refs[1:5]
    theirs_out, mine_out, mix, weights, theirs, mine, sems = refs[5:]
    tokens, half = mine.shape
    rows = tokens // 4
    copies = Copies(sems)
    copies.start("mix", mix_in, mix)
    stage_output(copies, pos, parts, weights)
    copies.wait("mix", "output")
    crossed = jnp.concatenate([mix[CROSSED[s] * rows : (CROSSED[s] + 1) * rows] for s in range(4)])
    for ref, out, tokens_of, first in ((theirs, theirs_out, crossed, half), (mine, mine_out, mix[...], 0)):
        for c in range(4):
            step = half // 4
            cols = slice(c * step, (c + 1) * step)
            ref[:, cols] = dot(tokens_of, weights[:, first + c * step : first + (c + 1) * step]).astype(BF16)
        copies.start("out", ref, out)
    copies.wait("out")


def output_halves(pos, mix, parts):
    tokens, width = mix.shape
    depth = parts[3].shape[0]
    half = shape_of((tokens, 2 * depth))
    return copy_call(
        output_kernel,
        "output_halves",
        (pos,),
        (mix, *parts),
        (half, half),
        (mix, shape_of((width, 4 * depth)), half, half),
        3 + 4 * depth // width,
    )


def cotangent_kernel(pos, *refs):
    own, other, parts, gm_out = refs[:4], refs[4:8], refs[8:12], refs[12]
    near, far, weights, gm, sems = refs[13:]
    half = near.shape[1]
    copies = Copies(sems)
    stage_output(copies, pos, parts, weights)
    stage_tokens(copies, "near", own, near)
    stage_tokens(copies, "far", other, far)
    copies.wait("output", "near")
    total = dot_t(near[...], weights[:, :half])
    copies.wait("far")
    gm[...] = (total + dot_t(far[...], weights[:, half:])).astype(BF16)
    copies.start("out", gm, gm_out)
    copies.wait("out")


def cotangent(pos, own, other, parts):
    rows, half = own[0].shape
    depth, width = parts[3].shape
    side, gm = shape_of((4 * rows, half)), shape_of((4 * rows, width))
    return copy_call(
        cotangent_kernel,
        "cotangent",
        (pos,),
        (*own, *other, *parts),
        (gm,),
        (side, side, shape_of((width, 4 * depth)), gm),
        9 + 4 * depth // width,
    )[0]


def backward_kernel(idx, pos, *refs):
    gm_in, kv_in, att_in, parts, results = refs[0], refs[1], refs[2], refs[3:7], refs[7:11]
    gm, kv, att, wq, gq, crossed, buffers, sems = refs[11:]
    width, depth = wq.shape[1], wq.shape[0] // 4
    spans = att.shape[0]
    copies = Copies(sems)
    copies.start("in", gm_in, gm)
    copies.start("in", kv_in, kv)
    copies.start("in", att_in, att)
    for r, part in enumerate(parts):
        place = pl.multiple_of(pos[r] * depth, depth)
        first = part.shape[0] - 2 * depth if r < 3 else part.shape[0] - depth
        copies.start("query", rows_of(part, first, depth), rows_of(wq, place, depth))
    copies.wait("in")
    for span in range(spans):
        slot, rest = divmod(span, spans // 4)
        rows = slice(span * SPAN, (span + 1) * SPAN)
        there = (CROSSED[slot] * (spans // 4) + rest) * SPAN
        heads = range(width // HD)
        cols = [head_cols(width, h) for h in heads]
        grads = [dot_t(gm[rows, kc], take_blocks(idx, kv, span, vc)) for kc, vc in cols]
        inner = [jnp.sum(att[span, h] * grads[h], axis=-1, keepdims=True) for h in heads]
        grads = [(att[span, h] * (grads[h] - inner[h]) * SCALE).astype(BF16) for h in heads]
        for h in heads:
            kc, _ = cols[h]
            value = dot(grads[h], take_blocks(idx, kv, span, kc)).astype(BF16)
            gq[rows, kc] = value
            crossed[there : there + SPAN, kc] = value
    copies.wait("query")
    for n, (source, slice_of) in enumerate(((crossed, 2), (crossed, 3), (gq, 0), (gq, 1))):
        for c in range(2):
            step = depth // 2
            at = slice_of * depth + c * step
            buffers[n, :, c * step : (c + 1) * step] = dot_t(source[...], wq[at : at + step]).astype(BF16)
        copies.start("out", buffers.at[n], results[n])
    copies.wait("out")


def backward(idx, pos, gm, kv, att, parts, depth):
    tokens, width = gm.shape
    chunk = shape_of((tokens, depth))
    return copy_call(
        backward_kernel,
        "backward",
        (idx, pos),
        (gm, kv, att, *parts),
        (chunk,) * 4,
        (gm, kv, att, shape_of((4 * depth, width)), gm, gm, shape_of((4, tokens, depth))),
        11,
    )


def flat(y, z, x, m):
    return ((y * 4 + z) * 2 + x) * 2 + m


def permutation(move):
    pairs = []
    for y in range(2):
        for z in range(4):
            for x in range(2):
                for m in range(2):
                    pairs.append((flat(y, z, x, m), flat(*move(y, z, x, m))))
    return pairs


RING = (0, 1, 3, 2)
NEXT = {RING[i]: RING[(i + 1) % 4] for i in range(4)}
PREV = {RING[i]: RING[(i + 3) % 4] for i in range(4)}
FIRST = permutation(lambda y, z, x, m: (y, z, 1 - x, m) if m == 0 else (1 - y, z, x, m))
SECOND = permutation(lambda y, z, x, m: (1 - y, z, x, m) if m == 0 else (y, z, 1 - x, m))
DIAGONAL = permutation(lambda y, z, x, m: (1 - y, z, 1 - x, m))
CORE = permutation(lambda y, z, x, m: (y, z, x, 1 - m))
UP = permutation(lambda y, z, x, m: (y, NEXT[z], x, m))
DOWN = permutation(lambda y, z, x, m: (y, PREV[z], x, m))


def move(array, pairs):
    return lax.ppermute(array, AXES, pairs)


def after(array, *earlier):
    return lax.optimization_barrier((array, *earlier))[0]


def phase(*arrays):
    return lax.optimization_barrier(arrays)


def local_plane(
    hidden,
    grad_out,
    database,
    enc_gain,
    query_weight,
    key_weight,
    value_weight,
    out_weight,
    block_ids,
    owners,
):
    y, z, x, m = (lax.axis_index(a).astype(jnp.int32) for a in AXES)
    depth, width = query_weight.shape[0], query_weight.shape[1] // 4
    rank = key_weight.shape[0]
    blocks, e = database.shape[0] // 2, database.shape[2]
    rows, half = hidden.shape
    nxt = lax.rem(2 * z + 1 - z // 2, 4)
    sources = (z, 3 - nxt, nxt, 3 - z)
    pos = jnp.stack([s ^ (2 * m) for s in sources])
    sources = jnp.stack(sources)

    weights = projection_slices(y * 2 + x, query_weight, key_weight, value_weight, out_weight)
    up, down = move(weights, UP), move(weights, DOWN)
    he, e_far = prepare(m, owners, block_ids, after(hidden, weights), database, enc_gain)
    he_own = (he, move(he, SECOND), move(he, FIRST), move(he, DIAGONAL))
    up, down, pos, sources, *he_own = phase(up, down, pos, sources, *he_own)

    near_far = move(up[: 2 * rank + depth], UP)
    h_zero = move(hidden, CORE)
    he_other = (h_zero,) + tuple(move(he_own[CROSSED[i]], CORE) for i in (1, 2, 3))
    o_far = move(after(up[2 * rank + depth :], *he_other), UP)
    g = after(grad_out, *he_other)
    g_own = (grad_out, move(g, SECOND), move(g, FIRST), move(g, DIAGONAL))

    per = rows // BLOCK
    codes = jnp.stack([after(a, *he_other)[0, a.shape[1] - 128 :][:UNITS] for a in he_own]).astype(jnp.int32)
    own_of, id_of = codes // (2 * blocks), codes % (2 * blocks)
    slot = jnp.arange(4, dtype=jnp.int32)
    rel_x = own_of ^ x
    rel_y = jnp.where(m == 0, slot % 2, slot // 2)[:, None]
    bank = jnp.where(m == 0, rel_x * 2 + rel_y, rel_y * 2 + rel_x)
    holder, block = id_of // blocks, id_of % blocks
    idx = (block // per * 8 + (holder ^ m) * 4 + bank) * per + block % per
    idx = (idx * (BLOCK // TILE)).reshape(-1, UPC).astype(jnp.int32)

    parts = (weights, up, down, near_far)
    kv, mixture, attention = forward(sources, idx, pos, he_own, e_far, he_other, parts, half, e, depth)
    mixture, o_far, *g_own = phase(mixture, o_far, *g_own[1:])
    g_own = (grad_out, *g_own)

    def begin(mine, theirs):
        return move((mine[2:].astype(F32) + theirs[2:].astype(F32)).astype(BF16), FIRST)

    def carry_on(mine, theirs, first):
        total = mine[1].astype(F32) + theirs[1].astype(F32) + first[1].astype(F32)
        return move(total.astype(BF16), SECOND)

    def finish(mine, theirs, first, second):
        return sum(a.astype(F32) for a in (mine[0], theirs[0], first[0], second))

    def slots(array):
        return array.reshape(4, rows, -1)

    g_other = tuple(move(g_own[CROSSED[i]], CORE) for i in range(4))
    outs = (weights, up, down, o_far)
    o_theirs, o_mine = output_halves(pos, mixture, outs)
    o_theirs, o_mine = slots(move(o_theirs, CORE)), slots(o_mine)
    gm = cotangent(pos, g_own, (g_other[0], after(g_other[1], o_mine), *g_other[2:]), outs)
    o_theirs = after(o_theirs, gm)
    o_first = begin(o_mine, o_theirs)
    t0, t1, m0, m1 = backward(idx, pos, after(gm, o_theirs), kv, attention, parts, depth)
    t0, t1 = after(t0, o_first), after(t1, o_first)
    t0, t1 = slots(move(t0, CORE)), slots(move(t1, CORE))
    m0, m1 = slots(m0), slots(m1)
    first0, first1 = begin(m0, t0), begin(m1, t1)
    o_second = carry_on(o_mine, o_theirs, o_first)
    second0, second1 = carry_on(m0, t0, first0), carry_on(m1, t1, first1)
    summed = finish(o_mine, o_theirs, o_first, o_second)
    grad_sum = jnp.concatenate((finish(m0, t0, first0, second0), finish(m1, t1, first1, second1)), axis=1)
    output = (hidden.astype(F32) + summed).astype(BF16)
    grad_hidden = (grad_out.astype(F32) + grad_sum).astype(BF16)
    return (output, grad_hidden)


def local_any(
    hidden,
    grad_out,
    database,
    enc_gain,
    query_weight,
    key_weight,
    value_weight,
    out_weight,
    block_ids,
    owners,
):
    tok_rows = hidden.shape[0]
    span_count = block_ids.shape[0]
    local_width = query_weight.shape[1]
    local_heads = local_width // HD
    owner_count = lax.axis_size("nbr")
    capacity = UNITS // owner_count
    score_scale = 1.0 / math.sqrt(HD)
    full_hidden, full_grad = (
        lax.all_gather(hidden, "mp", axis=1, tiled=True),
        lax.all_gather(grad_out, "mp", axis=1, tiled=True),
    )
    query_full, key_full, value_full, out_full = (
        lax.all_gather(query_weight, "dp", axis=0, tiled=True),
        lax.all_gather(key_weight, "dp", axis=0, tiled=True),
        lax.all_gather(value_weight, "dp", axis=0, tiled=True),
        lax.all_gather(out_weight, "dp", axis=1, tiled=True),
    )
    queries = jnp.dot(full_hidden, query_full, preferred_element_type=jnp.float32)
    queries = queries.astype(jnp.bfloat16).reshape(span_count, SPAN, local_heads, HD)
    owner_flat = owners.reshape(UNITS)
    id_flat = block_ids.reshape(UNITS)
    positions = jnp.arange(UNITS, dtype=jnp.int32)
    send_order = jnp.argsort(owner_flat * UNITS + positions)
    restore = jnp.argsort(send_order)
    requests = id_flat[send_order].reshape(owner_count, capacity)
    fetched = database[lax.all_to_all(requests, "nbr", split_axis=0, concat_axis=0, tiled=True)]
    encoded = encode_rows(fetched, enc_gain)
    key_part = jnp.einsum(
        "osbe,ef->osbf", encoded, key_full, preferred_element_type=jnp.float32
    ).astype(jnp.bfloat16)
    value_part = jnp.einsum(
        "osbe,ef->osbf", encoded, value_full, preferred_element_type=jnp.float32
    ).astype(jnp.bfloat16)
    stacked = jnp.concatenate((key_part, value_part), axis=-1)
    answers = lax.all_to_all(stacked, "nbr", split_axis=0, concat_axis=0, tiled=True)
    gathered = answers.reshape((UNITS,) + answers.shape[2:])[restore]
    kv_rows = gathered.reshape(span_count, UPC * BLOCK, 2 * local_width)
    key_rows = kv_rows[:, :, :local_width]
    value_rows = kv_rows[:, :, local_width:]
    key_rows = key_rows.reshape(span_count, UPC * BLOCK, local_heads, HD)
    value_rows = value_rows.reshape(span_count, UPC * BLOCK, local_heads, HD)
    scores = (
        jnp.einsum("cthd,cjhd->chtj", queries, key_rows, preferred_element_type=jnp.float32)
        * score_scale
    )
    attention = jax.nn.softmax(scores, axis=-1)
    attention_low = attention.astype(jnp.bfloat16)
    mixture = jnp.einsum(
        "chtj,cjhd->cthd", attention_low, value_rows, preferred_element_type=jnp.float32
    )
    mixture = mixture.astype(jnp.bfloat16).reshape(tok_rows, local_width)
    partial_out = jnp.dot(mixture, out_full, preferred_element_type=jnp.float32)
    summed = lax.psum_scatter(partial_out, "mp", scatter_dimension=1, tiled=True)
    output = (hidden.astype(jnp.float32) + summed).astype(jnp.bfloat16)
    grad_mixture = jnp.einsum("td,hd->th", full_grad, out_full, preferred_element_type=jnp.float32)
    grad_mixture = grad_mixture.astype(jnp.bfloat16).reshape(span_count, SPAN, local_heads, HD)
    grad_attention = jnp.einsum(
        "cthd,cjhd->chtj", grad_mixture, value_rows, preferred_element_type=jnp.float32
    )
    grad_scores = (
        attention
        * (grad_attention - jnp.sum(attention * grad_attention, axis=-1, keepdims=True))
        * score_scale
    )
    grad_scores = grad_scores.astype(jnp.bfloat16)
    grad_queries = jnp.einsum(
        "chtj,cjhd->cthd", grad_scores, key_rows, preferred_element_type=jnp.float32
    )
    grad_queries = grad_queries.astype(jnp.bfloat16).reshape(tok_rows, local_width)
    partial_grad = jnp.einsum(
        "th,dh->td", grad_queries, query_full, preferred_element_type=jnp.float32
    )
    grad_sum = lax.psum_scatter(partial_grad, "mp", scatter_dimension=1, tiled=True)
    grad_hidden = (grad_out.astype(jnp.float32) + grad_sum).astype(jnp.bfloat16)
    return (output, grad_hidden)


def solution(mesh):
    in_specs = (
        P(("groups", "dp", "nbr"), "mp"),
        P(("groups", "dp", "nbr"), "mp"),
        P(("groups", "dp", "nbr"), None, None),
        P(),
        P("dp", "mp"),
        P("dp", "mp"),
        P("dp", "mp"),
        P("mp", "dp"),
        P(("groups", "dp", "nbr"), None),
        P(("groups", "dp", "nbr"), None),
    )
    out_specs = (P(("groups", "dp", "nbr"), "mp"), P(("groups", "dp", "nbr"), "mp"))
    sizes = tuple(mesh.shape[a] for a in AXES)
    local = local_plane if sizes == (2, 4, 2, 2) else local_any
    return jax.shard_map(local, mesh=mesh, in_specs=in_specs, out_specs=out_specs, check_vma=False)
```

```python
import math

import jax
import jax.numpy as jnp
from jax import lax
from jax.experimental import pallas as pl
from jax.experimental.pallas import tpu as pltpu
from jax.sharding import PartitionSpec as P

HD = 128
SPAN = 64
BLOCK = 64
UPC = 4
UNITS = 8
AXES = ("groups", "dp", "nbr", "mp")
F32 = jnp.float32
BF16 = jnp.bfloat16


def encode_rows(states, enc_gain):
    widened = states.astype(F32)
    inverse = lax.rsqrt(jnp.mean(widened * widened, axis=-1, keepdims=True) + 1e-06)
    return (widened * inverse * enc_gain).astype(BF16)


def dot(a, b):
    return jnp.dot(a, b, preferred_element_type=F32)


def dot_t(a, b):
    return lax.dot_general(a, b, (((1,), (1,)), ((), ())), preferred_element_type=F32)


CROSSED = (0, 2, 1, 3)
TILE = 16
SCALE = 1.0 / math.sqrt(HD)
SHORT = pl.CostEstimate(flops=1024, bytes_accessed=1024, transcendentals=0)
LONG = pl.CostEstimate(flops=10**11, bytes_accessed=1024, transcendentals=0)


def shape_of(shape, dtype=BF16):
    return jax.ShapeDtypeStruct(shape, dtype)


def kernel_call(body, name, scalars, operands, out_shapes, in_specs):
    whole = lambda a: pl.BlockSpec(a.shape, lambda i, *_, n=len(a.shape): (0,) * n)
    return pl.pallas_call(
        body,
        grid_spec=pltpu.PrefetchScalarGridSpec(
            num_scalar_prefetch=len(scalars),
            grid=(1,),
            in_specs=[sp or whole(a) for sp, a in zip(in_specs, operands)],
            out_specs=[whole(a) for a in out_shapes],
        ),
        out_shape=tuple(out_shapes),
        compiler_params=pltpu.CompilerParams(vmem_limit_bytes=56 << 20),
        cost_estimate=LONG,
        name=name,
    )(*scalars, *operands)


class Copies:
    def __init__(self, sems):
        self.sems, self.used, self.open = sems, 0, {}

    def start(self, name, source, target):
        copy = pltpu.make_async_copy(source, target, self.sems.at[self.used])
        self.used += 1
        copy.start()
        self.open.setdefault(name, []).append(copy)

    def wait(self, *names):
        for name in names:
            for copy in self.open.pop(name):
                copy.wait()


def copy_call(body, name, scalars, operands, out_shapes, scratch, copies, cost=LONG, room=10, far=(), inputs=pl.ANY):
    smem = pl.BlockSpec(memory_space=pltpu.SMEM)
    need = sum(math.prod(a.shape) * jnp.dtype(a.dtype).itemsize for a in scratch)
    return pl.pallas_call(
        body,
        in_specs=[smem] * len(scalars) + [pl.BlockSpec(memory_space=inputs)] * len(operands),
        out_specs=[pl.BlockSpec(memory_space=pltpu.HBM if n in far else pl.ANY) for n in range(len(out_shapes))],
        out_shape=tuple(out_shapes),
        scratch_shapes=[pltpu.VMEM(a.shape, a.dtype) for a in scratch] + [pltpu.SemaphoreType.DMA((copies,))],
        compiler_params=pltpu.CompilerParams(vmem_limit_bytes=need + (room << 20)),
        cost_estimate=cost,
        name=name,
    )(*scalars, *operands)


def after(array, *earlier):
    return lax.optimization_barrier((array, *earlier))[0]


def step_kernel(before, now):
    now[0] = before[0] + 1


def step(*ready):
    smem = pl.BlockSpec(memory_space=pltpu.SMEM)
    return pl.pallas_call(
        step_kernel,
        in_specs=[smem],
        out_specs=smem,
        out_shape=shape_of((1,), jnp.int32),
        compiler_params=pltpu.CompilerParams(has_side_effects=True),
        cost_estimate=LONG,
        name="step",
    )(after(*ready))


def slices_kernel(place, q, k, v, o, early, late):
    depth, width = q.shape
    rank = k.shape[0]
    early[:rank] = k[...]
    early[rank : 2 * rank] = v[...]
    early[2 * rank :] = q[...]
    for c in range(depth // width):
        late[c * width : (c + 1) * width] = o[:, c * width : (c + 1) * width]


def projection_slices(chip, qw, kw, vw, ow):
    depth, width, rank = qw.shape[0], qw.shape[1] // 4, kw.shape[0]
    column = lambda i, place: (0, place[0])
    return kernel_call(
        slices_kernel,
        "projection_slices",
        (chip.reshape(1),),
        (qw, kw, vw, ow),
        (shape_of((2 * rank + depth, width)), shape_of((depth, width))),
        [
            pl.BlockSpec((depth, width), column),
            pl.BlockSpec((rank, width), column),
            pl.BlockSpec((rank, width), column),
            pl.BlockSpec((width, depth), lambda i, place: (place[0], 0)),
        ],
    )


def prepare_kernel(core, owners, ids, hid, db, gain, _, near, far):
    rows, half = hid.shape
    blocks, e = db.shape[0] // 2, db.shape[2]
    per = rows // BLOCK
    near[:, :half] = hid[...]
    for ref, which, start in ((near, core[0], half), (far, 1 - core[0], 0)):
        for part in range(blocks // per):
            states = db[pl.ds(which * blocks + part * per, per)].reshape(rows, e)
            ref[:, start + part * e : start + (part + 1) * e] = encode_rows(states, gain[...])
    lane = lax.broadcasted_iota(jnp.int32, (rows, near.shape[1] - half - blocks // per * e), 1)
    row = jnp.zeros(lane.shape, jnp.int32)
    for u in range(UNITS):
        at = divmod(u, UPC)
        row = jnp.where(lane == u, owners[at] * 2 * blocks + ids[at], row)
    near[:, near.shape[1] - lane.shape[1] :] = row.astype(F32).astype(BF16)


def prepare(core, owners, ids, hidden, db, gain, earlier):
    rows, half = hidden.shape
    wide = db.shape[0] // 2 * BLOCK // rows * db.shape[2]
    return kernel_call(
        prepare_kernel,
        "prepare",
        (core.reshape(1), owners, ids),
        (hidden, db, gain, earlier),
        (shape_of((rows, half + wide + 128)), shape_of((rows, wide))),
        [None] * 3 + [pl.BlockSpec(memory_space=pl.ANY)],
    )


def rows_of(ref, first, count):
    return ref.at[pl.ds(first, count)]


def take_blocks(idx, kv, span, cols):
    parts = []
    for u in range(UPC):
        row = pl.multiple_of(idx[span, u] * TILE, TILE)
        parts.append(kv[pl.ds(row, BLOCK), cols])
    return jnp.concatenate(parts, axis=0)


def span_rows(n):
    return slice(n * SPAN, (n + 1) * SPAN)


def head_cols(width, h):
    return slice(h * HD, (h + 1) * HD), slice(width + h * HD, width + (h + 1) * HD)


def stage_tokens(copies, name, arrays, target):
    rows, half = arrays[0].shape[0], target.shape[1]
    for slot, a in enumerate(arrays):
        source = a.at[:, pl.ds(0, half)] if a.shape[1] > half else a
        copies.start(name, source, rows_of(target, slot * rows, rows))


def stage_output(copies, name, part, target):
    width = part.shape[1]
    for c in range(part.shape[0] // width):
        copies.start(name, rows_of(part, c * width, width), target.at[:, pl.ds(c * width, width)])


def project(core, mix, weights, theirs, mine, columns):
    sub, rows = weights.shape[1] // 2, mix.shape[0] // 4
    crossed = jnp.concatenate([mix[s * rows : (s + 1) * rows] for s in CROSSED])
    for ref, tokens, which in ((theirs, crossed, 1 - core), (mine, mix[...], core)):
        cut = pl.ds(pl.multiple_of(which * sub, sub), sub)
        ref[:, columns] = dot(tokens, weights[:, cut]).astype(BF16)


def forward_kernel(src, idx, pos, *refs):
    banks, own, other, parts = refs[:8], refs[:4], refs[8:12], refs[12:16]
    kv_out, mix_out, att_out = refs[16:19]
    states, kvw, kv, near, far, weights, queries, mix, att, sems = refs[19:]
    e, columns = kvw.shape
    rank, rows, wide = e // 4, banks[0].shape[0], states.shape[1]
    half, width = near.shape[1], weights.shape[1]
    depth = weights.shape[0] // 4
    spans = att.shape[0]
    copies = Copies(sems)
    for r, part in enumerate(parts):
        place = pl.multiple_of(src[r] * rank, TILE)
        for c in range(2):
            target = kvw.at[pl.ds(place, rank), pl.ds(c * width, width)]
            copies.start("kvw", rows_of(part, c * rank, rank), target)
    for b, bank in enumerate(banks):
        start = 0 if b == 4 else bank.shape[1] - 128 - wide
        copies.start(b // 4, bank.at[:, pl.ds(start, wide)], rows_of(states, b * rows, rows))
    for r, part in enumerate(parts):
        place = pl.multiple_of(pos[r] * depth, depth)
        copies.start("query", rows_of(part, 2 * rank, depth), rows_of(weights, place, depth))
    stage_tokens(copies, "near", own, near)
    stage_tokens(copies, "far", other, far)
    copies.wait("kvw")
    for side in range(2):
        copies.wait(side)
        for c in range(wide // e):
            block = states[4 * side * rows : 4 * (side + 1) * rows, c * e : (c + 1) * e]
            at = (8 * c + 4 * side) * rows
            kv[at : at + 4 * rows] = dot(block, kvw[...]).astype(BF16)
    copies.start("out", kv, kv_out)
    copies.wait("query", "near")
    total = dot(near[...], weights[:half])
    copies.wait("far")
    queries[...] = (total + dot(far[...], weights[half:])).astype(BF16)
    todo = [(span_rows(n), n, h, *head_cols(width, h)) for n in range(spans) for h in range(width // HD)]
    scores = [dot_t(queries[rows, kc], take_blocks(idx, kv, n, kc)) * SCALE for rows, n, _, kc, _ in todo]
    scores = [jnp.exp(s - jnp.max(s, axis=-1, keepdims=True)) for s in scores]
    scores = [s * (1.0 / jnp.sum(s, axis=-1, keepdims=True)) for s in scores]
    for s, (_, n, h, _, _) in zip(scores, todo):
        att[n, h] = s
    copies.start("out", att, att_out)
    for s, (rows, n, _, kc, vc) in zip(scores, todo):
        mix[rows, kc] = dot(s.astype(BF16), take_blocks(idx, kv, n, vc)).astype(BF16)
    copies.start("out", mix, mix_out)
    copies.wait("out")


def forward(src, idx, pos, own, far_states, other, parts, half, e, depth):
    rows, width = own[0].shape[0], parts[0].shape[1]
    tokens = 4 * rows
    spans = tokens // SPAN
    wide = far_states.shape[1]
    kv = shape_of((8 * wide // e * rows, 2 * width))
    mix = shape_of((tokens, width))
    att = shape_of((spans, width // HD, SPAN, UPC * BLOCK), F32)
    side = shape_of((tokens, half))
    return copy_call(
        forward_kernel,
        "forward",
        (src, idx, pos),
        (*own, far_states, *other[1:], *other, *parts),
        (kv, mix, att),
        (
            shape_of((8 * rows, wide)),
            shape_of((e, 2 * width)),
            kv,
            side,
            side,
            shape_of((4 * depth, width)),
            mix,
            mix,
            att,
        ),
        31,
        SHORT,
        42,
    )


def output_kernel(core, *refs):
    mix_in, parts = refs[0], refs[1:4]
    theirs_out, mine_out, mix, weights, theirs, mine, sems = refs[4:]
    sub = weights.shape[2] // 2
    copies = Copies(sems)
    copies.start("mix", mix_in, mix)
    for r, part in enumerate(parts):
        stage_output(copies, r, part, weights.at[r])
    copies.wait("mix")
    for r in range(3):
        copies.wait(r)
        project(core[0], mix, weights.at[r], theirs, mine, slice(r * sub, (r + 1) * sub))
    copies.start("out", theirs, theirs_out)
    copies.start("out", mine, mine_out)
    copies.wait("out")


def output_slices(core, mix, parts):
    tokens, width = mix.shape
    depth = parts[0].shape[0]
    out = shape_of((tokens, 3 * depth // 2))
    return copy_call(
        output_kernel,
        "output_slices",
        (core.reshape(1),),
        (mix, *parts),
        (out, out),
        (mix, shape_of((3, width, depth)), out, out),
        3 + 3 * (depth // width),
        far=(0,),
    )


def cotangent_kernel(pos, *refs):
    own, other, parts, gm_out, rest_out = refs[:4], refs[4:8], refs[8:11], refs[11], refs[12]
    grads, weights, gm, sems = refs[13:]
    rows, depth = own[0].shape[0], grads.shape[2]
    copies = Copies(sems)
    for r, part in enumerate(parts):
        stage_output(copies, r, part, weights.at[r])
    for side, arrays in enumerate((own, other)):
        for slot, a in enumerate(arrays):
            for c in range(2):
                target = grads.at[2 * side + c, pl.ds(slot * rows, rows)]
                copies.start("grads", a.at[:, pl.ds(c * depth, depth)], target)
    copies.wait("grads")
    copies.start("out", grads.at[pos[3]], rest_out)
    copies.wait(0, 1, 2)
    gm[...] = sum(dot_t(grads[pos[r]], weights[r]) for r in range(3))
    copies.start("out", gm, gm_out)
    copies.wait("out")


def cotangent(pos, own, other, parts):
    tokens, (depth, width) = 4 * own[0].shape[0], parts[0].shape
    gm = shape_of((tokens, width), F32)
    return copy_call(
        cotangent_kernel,
        "cotangent",
        (pos,),
        (*own, *other, *parts),
        (gm, shape_of((tokens, depth))),
        (shape_of((4, tokens, depth)), shape_of((3, width, depth)), gm),
        3 * (depth // width) + 16 + 2,
    )


def late_kernel(core, idx, pos, *refs):
    gm_in, rest_in, part, mix_in, kv_in, att_in, parts, results = *refs[:6], refs[6:10], refs[10:16]
    gmf, rest, wo, mix, kv, att, wq, gm, gq, crossed, wide, narrow, sems = refs[16:]
    width, depth = wq.shape[1], wq.shape[0] // 4
    spans, sub = att.shape[0], depth // 2
    copies = Copies(sems)
    stage_output(copies, "in", part, wo)
    copies.start("in", rest_in, rest)
    copies.start("in", gm_in, gmf)
    copies.start("kv", kv_in, kv)
    copies.start("kv", att_in, att)
    copies.start("mix", mix_in, mix)
    for r, piece in enumerate(parts):
        place = pl.multiple_of(pos[r] * depth, depth)
        copies.start("query", rows_of(piece, piece.shape[0] - depth, depth), rows_of(wq, place, depth))
    copies.wait("in")
    gm[...] = (gmf[...] + dot_t(rest[...], wo[...])).astype(BF16)
    copies.wait("kv")
    todo = [(span_rows(n), n, h, *head_cols(width, h)) for n in range(spans) for h in range(width // HD)]
    grads = [dot_t(gm[rows, kc], take_blocks(idx, kv, n, vc)) for rows, n, _, kc, vc in todo]
    inner = [jnp.sum(att[n, h] * g, axis=-1, keepdims=True) for g, (_, n, h, _, _) in zip(grads, todo)]
    grads = [(att[n, h] * (g - a) * SCALE).astype(BF16) for g, a, (_, n, h, _, _) in zip(grads, inner, todo)]
    for g, (rows, n, _, kc, _) in zip(grads, todo):
        slot, within = divmod(n, spans // 4)
        value = dot(g, take_blocks(idx, kv, n, kc)).astype(BF16)
        gq[rows, kc] = value
        crossed[span_rows(CROSSED[slot] * (spans // 4) + within), kc] = value
    copies.wait("mix", "query")
    project(core[0], mix, wo, wide.at[0], wide.at[1], slice(0, sub))
    first = wide.shape[2] - sub
    for n, (source, chunk, side) in enumerate(((crossed, 0, 2), (crossed, 1, 2), (gq, 0, 0), (gq, 1, 0))):
        buffer = (narrow if chunk else wide).at[n // 2]
        start, place = side * depth + chunk * first, 0 if chunk else sub
        for at in range(0, buffer.shape[1] - place, 256):
            value = dot_t(source[...], wq[start + at : start + at + 256])
            buffer[:, place + at : place + at + 256] = value.astype(BF16)
        if n < 2:
            copies.start("out", buffer, results[n])
        else:
            rows = buffer.shape[0] // 2
            for half in range(2):
                copies.start("out", rows_of(buffer, half * rows, rows), results[2 * n - 2 + half])
    copies.wait("out")


def late_slices(core, idx, pos, gm, rest, part, mix, kv, att, parts):
    tokens, width = gm.shape
    depth = part.shape[0]
    wide = shape_of((tokens, depth // 2 + depth))
    narrow = shape_of((tokens, depth))
    heads = shape_of((tokens, width))
    return copy_call(
        late_kernel,
        "late_slices",
        (core.reshape(1), idx, pos),
        (gm, rest, part, mix, kv, att, *parts),
        (wide, narrow, *(shape_of((tokens // 2, a.shape[1])) for a in (wide, wide, narrow, narrow))),
        (
            gm,
            rest,
            shape_of((width, depth)),
            mix,
            kv,
            att,
            shape_of((4 * depth, width)),
            heads,
            heads,
            heads,
            shape_of((2, *wide.shape)),
            shape_of((2, *narrow.shape)),
        ),
        depth // width + 5 + 4 + 6,
        room=43,
        far=(0, 1),
    )


def add_kernel(firsts, *refs):
    n = len(firsts)
    arrays, out, held, sems = refs[:n], refs[n], refs[n + 1], refs[n + 2]
    rows = held.shape[1] // 2
    copies = Copies(sems)
    for part in range(2):
        for k, array in enumerate(arrays):
            copies.start(part, rows_of(array, firsts[k] + part * rows, rows), rows_of(held.at[k], part * rows, rows))
    for part in range(2):
        cut = slice(part * rows, (part + 1) * rows)
        copies.wait(part)
        held[0, cut] = sum(held[k, cut].astype(F32) for k in range(n)).astype(BF16)
        copies.start("out", rows_of(held.at[0], part * rows, rows), rows_of(out, part * rows, rows))
    copies.wait("out")


def add_rows(rows, *terms):
    arrays, firsts = zip(*terms)
    shape = (rows, arrays[0].shape[1])
    return copy_call(
        lambda *refs: add_kernel(firsts, *refs),
        "add_rows",
        (),
        arrays,
        (shape_of(shape),),
        (shape_of((len(arrays), *shape)),),
        2 * len(arrays) + 2,
        SHORT,
        room=46,
        far=(0,),
        inputs=pltpu.HBM,
    )[0]


def flat(y, z, x, m):
    return ((y * 4 + z) * 2 + x) * 2 + m


def permutation(move):
    pairs = []
    for y in range(2):
        for z in range(4):
            for x in range(2):
                for m in range(2):
                    pairs.append((flat(y, z, x, m), flat(*move(y, z, x, m))))
    return pairs


RING = (0, 1, 3, 2)
NEXT = {RING[i]: RING[(i + 1) % 4] for i in range(4)}
PREV = {RING[i]: RING[(i + 3) % 4] for i in range(4)}
FIRST = permutation(lambda y, z, x, m: (y, z, 1 - x, m) if m == 0 else (1 - y, z, x, m))
SECOND = permutation(lambda y, z, x, m: (1 - y, z, x, m) if m == 0 else (y, z, 1 - x, m))
DIAGONAL = permutation(lambda y, z, x, m: (1 - y, z, 1 - x, m))
CORE = permutation(lambda y, z, x, m: (y, z, x, 1 - m))
UP = permutation(lambda y, z, x, m: (y, NEXT[z], x, m))
DOWN = permutation(lambda y, z, x, m: (y, PREV[z], x, m))


def move(array, pairs):
    return lax.ppermute(array, AXES, pairs)


def phase(*arrays):
    return lax.optimization_barrier(arrays)


def local_plane(
    hidden,
    grad_out,
    database,
    enc_gain,
    query_weight,
    key_weight,
    value_weight,
    out_weight,
    block_ids,
    owners,
):
    y, z, x, m = (lax.axis_index(a).astype(jnp.int32) for a in AXES)
    depth, width = query_weight.shape[0], query_weight.shape[1] // 4
    rank = key_weight.shape[0]
    blocks, e = database.shape[0] // 2, database.shape[2]
    rows, half = hidden.shape
    nxt = lax.rem(2 * z + 1 - z // 2, 4)
    sources = (z, 3 - nxt, nxt, 3 - z)
    def codes_of(array):
        return array[0, array.shape[1] - 128 :][:UNITS].astype(jnp.int32)

    early, late = projection_slices(y * 2 + x, query_weight, key_weight, value_weight, out_weight)
    early_up, early_down = move(early, UP), move(early, DOWN)
    he, e_far = prepare(m, owners, block_ids, hidden, database, enc_gain, early)
    he_first, he_second = move(he, FIRST), move(he, SECOND)
    g_first = move(grad_out, FIRST)
    places = [s ^ (2 * m) for s in sources]
    turn, zz = after(m, early_up, early_down), after(z, early_up, early_down)
    nxt = lax.rem(2 * zz + 1 - zz // 2, 4)
    sources = (zz, 3 - nxt, nxt, 3 - zz)
    pos, sources = jnp.stack([s ^ (2 * turn) for s in sources]), jnp.stack(sources)
    codes = codes_of(after(he, pos))
    he_first, he_second, g_first, codes = phase(he_first, he_second, g_first, codes)
    h_zero = move(hidden, CORE)
    early_far = move(after(early_up, he_first, he_second), UP)
    he_last = move(he_first, SECOND)
    he_two, he_one = move(he_first, CORE), move(he_second, CORE)
    codes_last = move(after(he, he_first)[:TILE, he.shape[1] - 128 :], DIAGONAL)
    g_zero = move(grad_out, CORE)
    codes = jnp.stack([codes] + [codes_of(a) for a in (he_second, he_first, codes_last)])
    he_own = (he, he_second, he_first, he_last)

    per = rows // BLOCK
    own_of, id_of = codes // (2 * blocks), codes % (2 * blocks)
    slot = jnp.arange(4, dtype=jnp.int32)
    rel_x = own_of ^ x
    rel_y = jnp.where(m == 0, slot % 2, slot // 2)[:, None]
    bank = jnp.where(m == 0, rel_x * 2 + rel_y, rel_y * 2 + rel_x)
    holder, block = id_of // blocks, id_of % blocks
    idx = (block // per * 8 + (holder ^ m) * 4 + bank) * per + block % per
    idx = (idx * (BLOCK // TILE)).reshape(-1, UPC).astype(jnp.int32)

    he_two, he_one, idx = phase(he_two, he_one, idx)
    early_far = after(early_far, he_two)
    he_last = after(he_last, early_far)
    he_three = move(he_last, CORE)
    he_own = (*he_own[:3], he_last)
    he_other = (h_zero, he_two, he_one, he_three)
    g_second, g_last = move(grad_out, SECOND), move(g_first, SECOND)
    late_up, late_down = move(after(late, idx), UP), move(after(late, idx), DOWN)
    earlies = (early, early_up, early_down, early_far)
    kv, mixture, attention = forward(sources, idx, pos, he_own, e_far, he_other, earlies, half, e, depth)
    late_up, late_down, g_second, g_last, mixture = phase(late_up, late_down, g_second, g_last, mixture)

    late_far = move(late_up, UP)
    g_two, g_one, g_three = move(g_first, CORE), move(g_second, CORE), move(g_last, CORE)
    lates = (late, late_up, late_down)
    o_theirs, o_mine = output_slices(m, mixture, lates)
    g_two, g_one, g_three, o_mine = phase(g_two, g_one, g_three, o_mine)

    def slots(array):
        return array.reshape(-1, rows, array.shape[1])

    def begin(mine, theirs):
        return (mine.astype(F32) + theirs[2:].astype(F32)).astype(BF16)

    def carry_on(mine, theirs, first):
        return (mine[1].astype(F32) + theirs[1].astype(F32) + first[1].astype(F32)).astype(BF16)

    def finish(mine, theirs, first, second):
        return sum(a.astype(F32) for a in (mine[0], theirs[0], first[0], second))

    o_theirs, o_mine = slots(move(o_theirs, CORE)), slots(o_mine)
    g_other = (g_zero, g_two, g_one, g_three)
    gm, rest = cotangent(pos, (grad_out, g_second, g_first, g_last), g_other, lates)
    o_theirs = after(o_theirs, gm)
    o_send = begin(o_mine[2:], o_theirs)
    o_first = move(o_send, FIRST)
    late_far = after(late_far, o_send)
    t0, t1, m0, n0, m1, n1 = late_slices(m, idx, pos, gm, rest, late_far, mixture, kv, attention, earlies)
    t0, t1, o_first = phase(t0, t1, o_first)
    t0, t1 = move(t0, CORE), move(t1, CORE)
    send0 = add_rows(2 * rows, (n0, 0), (t0, 2 * rows))
    send1 = add_rows(2 * rows, (n1, 0), (after(t1, send0), 2 * rows))
    t0, t1, m0, m1, send0, send1 = (slots(a) for a in (t0, t1, m0, m1, send0, send1))
    first0, first1 = move(send0, FIRST), move(send1, FIRST)
    o_next = carry_on(o_mine, o_theirs, after(o_first, send0))
    o_second = move(o_next, SECOND)
    first0 = after(first0, o_next)
    next0 = carry_on(m0, t0, first0)
    second0 = move(next0, SECOND)
    first1 = after(first1, next0)
    next1 = carry_on(m1, t1, first1)
    second1 = move(next1, SECOND)
    sub = depth // 2
    o_sum = finish(o_mine, o_theirs, o_first, after(o_second, next1))
    sum0 = finish(m0, t0, first0, after(second0, next1))

    pieces = [o_sum[:, i * sub : (i + 1) * sub] for i in range(3)] + [sum0[:, :sub]]
    whole = jnp.zeros((4,) + pieces[0].shape, F32)
    for piece, place in zip(pieces, places):
        whole = lax.dynamic_update_slice_in_dim(whole, piece[None], place, 0)
    swapped = move(whole[2:].astype(BF16), CORE).astype(F32)
    low = jnp.where(m == 0, whole[:2], swapped)
    high = jnp.where(m == 0, swapped, whole[:2])
    summed = jnp.concatenate((low[0], high[0], low[1], high[1]), axis=1)
    output = (hidden.astype(F32) + summed).astype(BF16)

    edge = sum0.shape[1] - sub
    rest1 = m1[0].astype(F32) + t1[0].astype(F32) + first1[0].astype(F32)
    base = grad_out.astype(F32) + jnp.concatenate((sum0[:, sub:], rest1), axis=1)
    second1 = after(second1, base, whole)
    grad_hidden = (base + jnp.pad(second1.astype(F32), ((0, 0), (edge, 0)))).astype(BF16)
    return (output, grad_hidden)


def local_any(
    hidden,
    grad_out,
    database,
    enc_gain,
    query_weight,
    key_weight,
    value_weight,
    out_weight,
    block_ids,
    owners,
):
    tok_rows = hidden.shape[0]
    span_count = block_ids.shape[0]
    local_width = query_weight.shape[1]
    local_heads = local_width // HD
    owner_count = lax.axis_size("nbr")
    capacity = UNITS // owner_count
    score_scale = 1.0 / math.sqrt(HD)
    full_hidden, full_grad = (
        lax.all_gather(hidden, "mp", axis=1, tiled=True),
        lax.all_gather(grad_out, "mp", axis=1, tiled=True),
    )
    query_full, key_full, value_full, out_full = (
        lax.all_gather(query_weight, "dp", axis=0, tiled=True),
        lax.all_gather(key_weight, "dp", axis=0, tiled=True),
        lax.all_gather(value_weight, "dp", axis=0, tiled=True),
        lax.all_gather(out_weight, "dp", axis=1, tiled=True),
    )
    queries = jnp.dot(full_hidden, query_full, preferred_element_type=jnp.float32)
    queries = queries.astype(jnp.bfloat16).reshape(span_count, SPAN, local_heads, HD)
    owner_flat = owners.reshape(UNITS)
    id_flat = block_ids.reshape(UNITS)
    positions = jnp.arange(UNITS, dtype=jnp.int32)
    send_order = jnp.argsort(owner_flat * UNITS + positions)
    restore = jnp.argsort(send_order)
    requests = id_flat[send_order].reshape(owner_count, capacity)
    fetched = database[lax.all_to_all(requests, "nbr", split_axis=0, concat_axis=0, tiled=True)]
    encoded = encode_rows(fetched, enc_gain)
    key_part = jnp.einsum(
        "osbe,ef->osbf", encoded, key_full, preferred_element_type=jnp.float32
    ).astype(jnp.bfloat16)
    value_part = jnp.einsum(
        "osbe,ef->osbf", encoded, value_full, preferred_element_type=jnp.float32
    ).astype(jnp.bfloat16)
    stacked = jnp.concatenate((key_part, value_part), axis=-1)
    answers = lax.all_to_all(stacked, "nbr", split_axis=0, concat_axis=0, tiled=True)
    gathered = answers.reshape((UNITS,) + answers.shape[2:])[restore]
    kv_rows = gathered.reshape(span_count, UPC * BLOCK, 2 * local_width)
    key_rows = kv_rows[:, :, :local_width]
    value_rows = kv_rows[:, :, local_width:]
    key_rows = key_rows.reshape(span_count, UPC * BLOCK, local_heads, HD)
    value_rows = value_rows.reshape(span_count, UPC * BLOCK, local_heads, HD)
    scores = (
        jnp.einsum("cthd,cjhd->chtj", queries, key_rows, preferred_element_type=jnp.float32)
        * score_scale
    )
    attention = jax.nn.softmax(scores, axis=-1)
    attention_low = attention.astype(jnp.bfloat16)
    mixture = jnp.einsum(
        "chtj,cjhd->cthd", attention_low, value_rows, preferred_element_type=jnp.float32
    )
    mixture = mixture.astype(jnp.bfloat16).reshape(tok_rows, local_width)
    partial_out = jnp.dot(mixture, out_full, preferred_element_type=jnp.float32)
    summed = lax.psum_scatter(partial_out, "mp", scatter_dimension=1, tiled=True)
    output = (hidden.astype(jnp.float32) + summed).astype(jnp.bfloat16)
    grad_mixture = jnp.einsum("td,hd->th", full_grad, out_full, preferred_element_type=jnp.float32)
    grad_mixture = grad_mixture.astype(jnp.bfloat16).reshape(span_count, SPAN, local_heads, HD)
    grad_attention = jnp.einsum(
        "cthd,cjhd->chtj", grad_mixture, value_rows, preferred_element_type=jnp.float32
    )
    grad_scores = (
        attention
        * (grad_attention - jnp.sum(attention * grad_attention, axis=-1, keepdims=True))
        * score_scale
    )
    grad_scores = grad_scores.astype(jnp.bfloat16)
    grad_queries = jnp.einsum(
        "chtj,cjhd->cthd", grad_scores, key_rows, preferred_element_type=jnp.float32
    )
    grad_queries = grad_queries.astype(jnp.bfloat16).reshape(tok_rows, local_width)
    partial_grad = jnp.einsum(
        "th,dh->td", grad_queries, query_full, preferred_element_type=jnp.float32
    )
    grad_sum = lax.psum_scatter(partial_grad, "mp", scatter_dimension=1, tiled=True)
    grad_hidden = (grad_out.astype(jnp.float32) + grad_sum).astype(jnp.bfloat16)
    return (output, grad_hidden)


def solution(mesh):
    in_specs = (
        P(("groups", "dp", "nbr"), "mp"),
        P(("groups", "dp", "nbr"), "mp"),
        P(("groups", "dp", "nbr"), None, None),
        P(),
        P("dp", "mp"),
        P("dp", "mp"),
        P("dp", "mp"),
        P("mp", "dp"),
        P(("groups", "dp", "nbr"), None),
        P(("groups", "dp", "nbr"), None),
    )
    out_specs = (P(("groups", "dp", "nbr"), "mp"), P(("groups", "dp", "nbr"), "mp"))
    sizes = tuple(mesh.shape[a] for a in AXES)
    local = local_plane if sizes == (2, 4, 2, 2) else local_any
    return jax.shard_map(local, mesh=mesh, in_specs=in_specs, out_specs=out_specs, check_vma=False)
```

```python
import math

import jax
import jax.numpy as jnp
from jax import lax
from jax.experimental import pallas as pl
from jax.experimental.pallas import tpu as pltpu
from jax.sharding import PartitionSpec as P

HD = 128
SPAN = 64
BLOCK = 64
UPC = 4
UNITS = 8
AXES = ("groups", "dp", "nbr", "mp")
F32 = jnp.float32
BF16 = jnp.bfloat16


def encode_rows(states, enc_gain):
    widened = states.astype(F32)
    inverse = lax.rsqrt(jnp.mean(widened * widened, axis=-1, keepdims=True) + 1e-06)
    return (widened * inverse * enc_gain).astype(BF16)


def dot(a, b):
    return jnp.dot(a, b, preferred_element_type=F32)


def dot_t(a, b):
    return lax.dot_general(a, b, (((1,), (1,)), ((), ())), preferred_element_type=F32)


CROSSED = (0, 2, 1, 3)
TILE = 16
SCALE = 1.0 / math.sqrt(HD)
SHORT = pl.CostEstimate(flops=1024, bytes_accessed=1024, transcendentals=0)
LONG = pl.CostEstimate(flops=10**11, bytes_accessed=1024, transcendentals=0)


def shape_of(shape, dtype=BF16):
    return jax.ShapeDtypeStruct(shape, dtype)


def kernel_call(body, name, scalars, operands, out_shapes, in_specs):
    whole = lambda a: pl.BlockSpec(a.shape, lambda i, *_, n=len(a.shape): (0,) * n)
    return pl.pallas_call(
        body,
        grid_spec=pltpu.PrefetchScalarGridSpec(
            num_scalar_prefetch=len(scalars),
            grid=(1,),
            in_specs=[sp or whole(a) for sp, a in zip(in_specs, operands)],
            out_specs=[whole(a) for a in out_shapes],
        ),
        out_shape=tuple(out_shapes),
        compiler_params=pltpu.CompilerParams(vmem_limit_bytes=56 << 20),
        cost_estimate=LONG,
        name=name,
    )(*scalars, *operands)


class Copies:
    def __init__(self, sems):
        self.sems, self.used, self.open = sems, 0, {}

    def start(self, name, source, target):
        copy = pltpu.make_async_copy(source, target, self.sems.at[self.used])
        self.used += 1
        copy.start()
        self.open.setdefault(name, []).append(copy)

    def wait(self, *names):
        for name in names:
            for copy in self.open.pop(name):
                copy.wait()


def copy_call(body, name, scalars, operands, out_shapes, scratch, copies, cost=LONG, room=10, far=(), inputs=pl.ANY):
    smem = pl.BlockSpec(memory_space=pltpu.SMEM)
    need = sum(math.prod(a.shape) * jnp.dtype(a.dtype).itemsize for a in scratch)
    return pl.pallas_call(
        body,
        in_specs=[smem] * len(scalars) + [pl.BlockSpec(memory_space=inputs)] * len(operands),
        out_specs=[pl.BlockSpec(memory_space=pltpu.HBM if n in far else pl.ANY) for n in range(len(out_shapes))],
        out_shape=tuple(out_shapes),
        scratch_shapes=[pltpu.VMEM(a.shape, a.dtype) for a in scratch] + [pltpu.SemaphoreType.DMA((copies,))],
        compiler_params=pltpu.CompilerParams(vmem_limit_bytes=need + (room << 20)),
        cost_estimate=cost,
        name=name,
    )(*scalars, *operands)


def after(array, *earlier):
    return lax.optimization_barrier((array, *earlier))[0]


def step_kernel(before, now):
    now[0] = before[0] + 1


def step(*ready):
    smem = pl.BlockSpec(memory_space=pltpu.SMEM)
    return pl.pallas_call(
        step_kernel,
        in_specs=[smem],
        out_specs=smem,
        out_shape=shape_of((1,), jnp.int32),
        compiler_params=pltpu.CompilerParams(has_side_effects=True),
        cost_estimate=LONG,
        name="step",
    )(after(*ready))


def slices_kernel(place, q, k, v, o, early, late, both):
    depth, width = q.shape
    rank = k.shape[0]
    early[:rank] = k[...]
    early[rank : 2 * rank] = v[...]
    early[2 * rank :] = q[...]
    for c in range(depth // width):
        late[c * width : (c + 1) * width] = o[:, c * width : (c + 1) * width]
    both[: 2 * rank + depth] = early[...]
    both[2 * rank + depth :] = late[...]


def projection_slices(chip, qw, kw, vw, ow):
    depth, width, rank = qw.shape[0], qw.shape[1] // 4, kw.shape[0]
    column = lambda i, place: (0, place[0])
    return kernel_call(
        slices_kernel,
        "projection_slices",
        (chip.reshape(1),),
        (qw, kw, vw, ow),
        tuple(shape_of((n, width)) for n in (2 * rank + depth, depth, 2 * rank + 2 * depth)),
        [
            pl.BlockSpec((depth, width), column),
            pl.BlockSpec((rank, width), column),
            pl.BlockSpec((rank, width), column),
            pl.BlockSpec((width, depth), lambda i, place: (place[0], 0)),
        ],
    )


def prepare_kernel(core, owners, ids, hid, grad, db, gain, _, near, far):
    rows, half = hid.shape
    blocks, e = db.shape[0] // 2, db.shape[2]
    per = rows // BLOCK
    near[:, :half] = hid[...]
    for ref, which, start in ((near, core[0], half), (far, 1 - core[0], 0)):
        for part in range(blocks // per):
            states = db[pl.ds(which * blocks + part * per, per)].reshape(rows, e)
            ref[:, start + part * e : start + (part + 1) * e] = encode_rows(states, gain[...])
    near[:, near.shape[1] - half :] = grad[...]
    lane = lax.broadcasted_iota(jnp.int32, (rows, 128), 1)
    row = jnp.zeros(lane.shape, jnp.int32)
    for u in range(UNITS):
        at = divmod(u, UPC)
        row = jnp.where(lane == u, owners[at] * 2 * blocks + ids[at], row)
    near[:, near.shape[1] - half - 128 : near.shape[1] - half] = row.astype(F32).astype(BF16)


def prepare(core, owners, ids, hidden, grad, db, gain, earlier):
    rows, half = hidden.shape
    wide = db.shape[0] // 2 * BLOCK // rows * db.shape[2]
    return kernel_call(
        prepare_kernel,
        "prepare",
        (core.reshape(1), owners, ids),
        (hidden, grad, db, gain, earlier),
        (shape_of((rows, half + wide + 128 + half)), shape_of((rows, wide))),
        [None] * 4 + [pl.BlockSpec(memory_space=pl.ANY)],
    )


def rows_of(ref, first, count):
    return ref.at[pl.ds(first, count)]


def take_blocks(idx, kv, span, cols):
    parts = []
    for u in range(UPC):
        row = pl.multiple_of(idx[span, u] * TILE, TILE)
        parts.append(kv[pl.ds(row, BLOCK), cols])
    return jnp.concatenate(parts, axis=0)


def span_rows(n):
    return slice(n * SPAN, (n + 1) * SPAN)


def head_cols(width, h):
    return slice(h * HD, (h + 1) * HD), slice(width + h * HD, width + (h + 1) * HD)


def stage_tokens(copies, name, arrays, target):
    rows, half = arrays[0].shape[0], target.shape[1]
    for slot, a in enumerate(arrays):
        source = a.at[:, pl.ds(0, half)] if a.shape[1] > half else a
        copies.start(name, source, rows_of(target, slot * rows, rows))


def stage_output(copies, name, part, target):
    width = part.shape[1]
    count = target.shape[1] // width
    first = part.shape[0] - count * width
    for c in range(count):
        copies.start(name, rows_of(part, first + c * width, width), target.at[:, pl.ds(c * width, width)])


def project(core, mix, weights, theirs, mine, columns):
    sub, rows = weights.shape[1] // 2, mix.shape[0] // 4
    crossed = jnp.concatenate([mix[s * rows : (s + 1) * rows] for s in CROSSED])
    for ref, tokens, which in ((theirs, crossed, 1 - core), (mine, mix[...], core)):
        cut = pl.ds(pl.multiple_of(which * sub, sub), sub)
        ref[:, columns] = dot(tokens, weights[:, cut]).astype(BF16)


def forward_kernel(src, idx, pos, *refs):
    banks, own, other, parts = refs[:8], refs[:4], refs[8:12], refs[12:16]
    kv_out, mix_out, att_out = refs[16:19]
    states, kvw, kv, near, far, weights, queries, mix, att, sems = refs[19:]
    e, columns = kvw.shape
    rank, rows, wide = e // 4, banks[0].shape[0], states.shape[1]
    half, width = near.shape[1], weights.shape[1]
    depth = weights.shape[0] // 4
    spans = att.shape[0]
    copies = Copies(sems)
    for r, part in enumerate(parts):
        place = pl.multiple_of(src[r] * rank, TILE)
        for c in range(2):
            target = kvw.at[pl.ds(place, rank), pl.ds(c * width, width)]
            copies.start("kvw", rows_of(part, c * rank, rank), target)
    for b, bank in enumerate(banks):
        start = 0 if b == 4 else half
        copies.start(b // 4, bank.at[:, pl.ds(start, wide)], rows_of(states, b * rows, rows))
    for r, part in enumerate(parts):
        place = pl.multiple_of(pos[r] * depth, depth)
        copies.start("query", rows_of(part, 2 * rank, depth), rows_of(weights, place, depth))
    stage_tokens(copies, "near", own, near)
    stage_tokens(copies, "far", other, far)
    copies.wait("kvw")
    for side in range(2):
        copies.wait(side)
        for c in range(wide // e):
            block = states[4 * side * rows : 4 * (side + 1) * rows, c * e : (c + 1) * e]
            at = (8 * c + 4 * side) * rows
            kv[at : at + 4 * rows] = dot(block, kvw[...]).astype(BF16)
    copies.start("out", kv, kv_out)
    copies.wait("query", "near")
    total = dot(near[...], weights[:half])
    copies.wait("far")
    queries[...] = (total + dot(far[...], weights[half:])).astype(BF16)
    todo = [(span_rows(n), n, h, *head_cols(width, h)) for n in range(spans) for h in range(width // HD)]
    scores = [dot_t(queries[rows, kc], take_blocks(idx, kv, n, kc)) * SCALE for rows, n, _, kc, _ in todo]
    scores = [jnp.exp(s - jnp.max(s, axis=-1, keepdims=True)) for s in scores]
    scores = [s * (1.0 / jnp.sum(s, axis=-1, keepdims=True)) for s in scores]
    for s, (_, n, h, _, _) in zip(scores, todo):
        att[n, h] = s
    copies.start("out", att, att_out)
    for s, (rows, n, _, kc, vc) in zip(scores, todo):
        mix[rows, kc] = dot(s.astype(BF16), take_blocks(idx, kv, n, vc)).astype(BF16)
    copies.start("out", mix, mix_out)
    copies.wait("out")


def forward(src, idx, pos, own, far_states, other, parts, half, e, depth):
    rows, width = own[0].shape[0], parts[0].shape[1]
    tokens = 4 * rows
    spans = tokens // SPAN
    wide = far_states.shape[1]
    kv = shape_of((8 * wide // e * rows, 2 * width))
    mix = shape_of((tokens, width))
    att = shape_of((spans, width // HD, SPAN, UPC * BLOCK), F32)
    side = shape_of((tokens, half))
    return copy_call(
        forward_kernel,
        "forward",
        (src, idx, pos),
        (*own, far_states, *other[1:], *other, *parts),
        (kv, mix, att),
        (
            shape_of((8 * rows, wide)),
            shape_of((e, 2 * width)),
            kv,
            side,
            side,
            shape_of((4 * depth, width)),
            mix,
            mix,
            att,
        ),
        31,
        SHORT,
        42,
    )


def output_kernel(core, *refs):
    mix_in, parts = refs[0], refs[1:4]
    theirs_out, mine_out, mix, weights, theirs, mine, sems = refs[4:]
    sub = weights.shape[2] // 2
    copies = Copies(sems)
    copies.start("mix", mix_in, mix)
    for r, part in enumerate(parts):
        stage_output(copies, r, part, weights.at[r])
    copies.wait("mix")
    for r in range(3):
        copies.wait(r)
        project(core[0], mix, weights.at[r], theirs, mine, slice(r * sub, (r + 1) * sub))
    copies.start("out", theirs, theirs_out)
    copies.start("out", mine, mine_out)
    copies.wait("out")


def output_slices(core, mix, parts):
    tokens, width = mix.shape
    depth = parts[0].shape[0]
    out = shape_of((tokens, 3 * depth // 2))
    return copy_call(
        output_kernel,
        "output_slices",
        (core.reshape(1),),
        (mix, *parts),
        (out, out),
        (mix, shape_of((3, width, depth)), out, out),
        3 + 3 * (depth // width),
        far=(0,),
    )


def cotangent_kernel(pos, *refs):
    own, other, parts, gm_out, rest_out = refs[:4], refs[4:8], refs[8:11], refs[11], refs[12]
    grads, weights, gm, sems = refs[13:]
    rows, depth = own[0].shape[0], grads.shape[2]
    copies = Copies(sems)
    for r, part in enumerate(parts):
        stage_output(copies, r, part, weights.at[r])
    for side, arrays in enumerate((own, other)):
        for slot, a in enumerate(arrays):
            for c in range(2):
                target = grads.at[2 * side + c, pl.ds(slot * rows, rows)]
                start = a.shape[1] - 2 * depth + c * depth
                copies.start("grads", a.at[:, pl.ds(start, depth)], target)
    copies.wait("grads")
    copies.start("out", grads.at[pos[3]], rest_out)
    copies.wait(0, 1, 2)
    gm[...] = sum(dot_t(grads[pos[r]], weights[r]) for r in range(3))
    copies.start("out", gm, gm_out)
    copies.wait("out")


def cotangent(pos, own, other, parts):
    tokens, (depth, width) = 4 * own[0].shape[0], parts[0].shape
    gm = shape_of((tokens, width), F32)
    return copy_call(
        cotangent_kernel,
        "cotangent",
        (pos,),
        (*own, *other, *parts),
        (gm, shape_of((tokens, depth))),
        (shape_of((4, tokens, depth)), shape_of((3, width, depth)), gm),
        3 * (depth // width) + 16 + 2,
    )


def late_kernel(core, idx, pos, *refs):
    gm_in, rest_in, part, mix_in, kv_in, att_in, parts, results = *refs[:6], refs[6:10], refs[10:16]
    gmf, rest, wo, mix, kv, att, wq, gm, gq, crossed, wide, narrow, sems = refs[16:]
    width, depth = wq.shape[1], wq.shape[0] // 4
    spans, sub = att.shape[0], depth // 2
    copies = Copies(sems)
    stage_output(copies, "in", part, wo)
    copies.start("in", rest_in, rest)
    copies.start("in", gm_in, gmf)
    copies.start("kv", kv_in, kv)
    copies.start("kv", att_in, att)
    copies.start("mix", mix_in, mix)
    for r, piece in enumerate(parts):
        place = pl.multiple_of(pos[r] * depth, depth)
        copies.start("query", rows_of(piece, parts[0].shape[0] - depth, depth), rows_of(wq, place, depth))
    copies.wait("in")
    gm[...] = (gmf[...] + dot_t(rest[...], wo[...])).astype(BF16)
    copies.wait("kv")
    todo = [(span_rows(n), n, h, *head_cols(width, h)) for n in range(spans) for h in range(width // HD)]
    grads = [dot_t(gm[rows, kc], take_blocks(idx, kv, n, vc)) for rows, n, _, kc, vc in todo]
    inner = [jnp.sum(att[n, h] * g, axis=-1, keepdims=True) for g, (_, n, h, _, _) in zip(grads, todo)]
    grads = [(att[n, h] * (g - a) * SCALE).astype(BF16) for g, a, (_, n, h, _, _) in zip(grads, inner, todo)]
    for g, (rows, n, _, kc, _) in zip(grads, todo):
        slot, within = divmod(n, spans // 4)
        value = dot(g, take_blocks(idx, kv, n, kc)).astype(BF16)
        gq[rows, kc] = value
        crossed[span_rows(CROSSED[slot] * (spans // 4) + within), kc] = value
    copies.wait("mix", "query")
    project(core[0], mix, wo, wide.at[0], wide.at[1], slice(0, sub))
    first = wide.shape[2] - sub
    for n, (source, chunk, side) in enumerate(((crossed, 0, 2), (crossed, 1, 2), (gq, 0, 0), (gq, 1, 0))):
        buffer = (narrow if chunk else wide).at[n // 2]
        start, place = side * depth + chunk * first, 0 if chunk else sub
        for at in range(0, buffer.shape[1] - place, 256):
            value = dot_t(source[...], wq[start + at : start + at + 256])
            buffer[:, place + at : place + at + 256] = value.astype(BF16)
        if n < 2:
            copies.start("out", buffer, results[n])
        else:
            rows = buffer.shape[0] // 2
            for half in range(2):
                copies.start("out", rows_of(buffer, half * rows, rows), results[2 * n - 2 + half])
    copies.wait("out")


def late_slices(core, idx, pos, gm, rest, part, mix, kv, att, parts):
    tokens, width = gm.shape
    depth = part.shape[0]
    wide = shape_of((tokens, depth // 2 + depth))
    narrow = shape_of((tokens, depth))
    heads = shape_of((tokens, width))
    return copy_call(
        late_kernel,
        "late_slices",
        (core.reshape(1), idx, pos),
        (gm, rest, part, mix, kv, att, *parts),
        (wide, narrow, *(shape_of((tokens // 2, a.shape[1])) for a in (wide, wide, narrow, narrow))),
        (
            gm,
            rest,
            shape_of((width, depth)),
            mix,
            kv,
            att,
            shape_of((4 * depth, width)),
            heads,
            heads,
            heads,
            shape_of((2, *wide.shape)),
            shape_of((2, *narrow.shape)),
        ),
        depth // width + 5 + 4 + 6,
        room=43,
        far=(0, 1),
    )


def add_kernel(firsts, *refs):
    n = len(firsts)
    arrays, out, held, sems = refs[:n], refs[n], refs[n + 1], refs[n + 2]
    rows = held.shape[1] // 2
    copies = Copies(sems)
    for part in range(2):
        for k, array in enumerate(arrays):
            copies.start(part, rows_of(array, firsts[k] + part * rows, rows), rows_of(held.at[k], part * rows, rows))
    for part in range(2):
        cut = slice(part * rows, (part + 1) * rows)
        copies.wait(part)
        held[0, cut] = sum(held[k, cut].astype(F32) for k in range(n)).astype(BF16)
        copies.start("out", rows_of(held.at[0], part * rows, rows), rows_of(out, part * rows, rows))
    copies.wait("out")


def add_rows(rows, *terms):
    arrays, firsts = zip(*terms)
    shape = (rows, arrays[0].shape[1])
    return copy_call(
        lambda *refs: add_kernel(firsts, *refs),
        "add_rows",
        (),
        arrays,
        (shape_of(shape),),
        (shape_of((len(arrays), *shape)),),
        2 * len(arrays) + 2,
        SHORT,
        room=46,
        far=(0,),
        inputs=pltpu.HBM,
    )[0]


def flat(y, z, x, m):
    return ((y * 4 + z) * 2 + x) * 2 + m


def permutation(move):
    pairs = []
    for y in range(2):
        for z in range(4):
            for x in range(2):
                for m in range(2):
                    pairs.append((flat(y, z, x, m), flat(*move(y, z, x, m))))
    return pairs


RING = (0, 1, 3, 2)
NEXT = {RING[i]: RING[(i + 1) % 4] for i in range(4)}
PREV = {RING[i]: RING[(i + 3) % 4] for i in range(4)}
FIRST = permutation(lambda y, z, x, m: (y, z, 1 - x, m) if m == 0 else (1 - y, z, x, m))
SECOND = permutation(lambda y, z, x, m: (1 - y, z, x, m) if m == 0 else (y, z, 1 - x, m))
DIAGONAL = permutation(lambda y, z, x, m: (1 - y, z, 1 - x, m))
CORE = permutation(lambda y, z, x, m: (y, z, x, 1 - m))
UP = permutation(lambda y, z, x, m: (y, NEXT[z], x, m))
DOWN = permutation(lambda y, z, x, m: (y, PREV[z], x, m))


def move(array, pairs):
    return lax.ppermute(array, AXES, pairs)


def phase(*arrays):
    return lax.optimization_barrier(arrays)


def local_plane(
    hidden,
    grad_out,
    database,
    enc_gain,
    query_weight,
    key_weight,
    value_weight,
    out_weight,
    block_ids,
    owners,
):
    y, z, x, m = (lax.axis_index(a).astype(jnp.int32) for a in AXES)
    depth, width = query_weight.shape[0], query_weight.shape[1] // 4
    rank = key_weight.shape[0]
    blocks, e = database.shape[0] // 2, database.shape[2]
    rows, half = hidden.shape
    nxt = lax.rem(2 * z + 1 - z // 2, 4)
    sources = (z, 3 - nxt, nxt, 3 - z)
    def codes_of(array):
        start = array.shape[1] - half - 128 if array.shape[1] > 128 else 0
        return array[0, start : start + UNITS].astype(jnp.int32)

    early, late, both = projection_slices(y * 2 + x, query_weight, key_weight, value_weight, out_weight)
    early_up, early_down = move(early, UP), move(both, DOWN)
    he, e_far = prepare(m, owners, block_ids, hidden, grad_out, database, enc_gain, early)
    he_first, he_second = move(he, FIRST), move(he, SECOND)
    places = [s ^ (2 * m) for s in sources]
    turn, zz = after(m, early_up, early_down), after(z, early_up, early_down)
    nxt = lax.rem(2 * zz + 1 - zz // 2, 4)
    sources = (zz, 3 - nxt, nxt, 3 - zz)
    pos, sources = jnp.stack([s ^ (2 * turn) for s in sources]), jnp.stack(sources)
    codes = codes_of(after(he, pos))
    he_first, he_second, codes = phase(he_first, he_second, codes)
    h_zero = move(hidden, CORE)
    early_far = move(after(early_up, he_first, he_second), UP)
    he_last = move(he_first, SECOND)
    he_two, he_one = move(he_first, CORE), move(he_second, CORE)
    h_zero, g_zero = move(hidden, CORE), move(grad_out, CORE)
    codes = jnp.stack([codes] + [codes_of(a) for a in (he_second, he_first)])
    he_two, he_one, h_zero, g_zero, codes = phase(he_two, he_one, h_zero, g_zero, codes)
    early_far = after(early_far, he_two)
    he_last = after(he_last, early_far)
    he_three = move(he_last, CORE)
    late_up = move(after(late, early_far), UP)
    he_own = (he, he_second, he_first, he_last)
    he_other = (h_zero, he_two, he_one, he_three)

    per = rows // BLOCK
    codes = jnp.concatenate((codes, codes_of(he_last)[None]))
    own_of, id_of = codes // (2 * blocks), codes % (2 * blocks)
    slot = jnp.arange(4, dtype=jnp.int32)
    rel_x = own_of ^ x
    rel_y = jnp.where(m == 0, slot % 2, slot // 2)[:, None]
    bank = jnp.where(m == 0, rel_x * 2 + rel_y, rel_y * 2 + rel_x)
    holder, block = id_of // blocks, id_of % blocks
    idx = (block // per * 8 + (holder ^ m) * 4 + bank) * per + block % per
    idx = (idx * (BLOCK // TILE)).reshape(-1, UPC).astype(jnp.int32)

    earlies = (early, early_up, early_down, early_far)
    kv, mixture, attention = forward(sources, idx, pos, he_own, e_far, he_other, earlies, half, e, depth)
    late_up, mixture = phase(late_up, mixture)

    late_far = move(late_up, UP)
    lates = (late, late_up, early_down)
    o_theirs, o_mine = output_slices(m, mixture, lates)

    def slots(array):
        return array.reshape(-1, rows, array.shape[1])

    def begin(mine, theirs):
        return (mine.astype(F32) + theirs[2:].astype(F32)).astype(BF16)

    def carry_on(mine, theirs, first):
        return (mine[1].astype(F32) + theirs[1].astype(F32) + first[1].astype(F32)).astype(BF16)

    def finish(mine, theirs, first, second):
        return sum(a.astype(F32) for a in (mine[0], theirs[0], first[0], second))

    o_theirs, o_mine = slots(move(o_theirs, CORE)), slots(o_mine)
    g_other = (after(g_zero, o_mine), *he_other[1:])
    gm, rest = cotangent(pos, he_own, g_other, lates)
    o_theirs = after(o_theirs, gm)
    o_send = begin(o_mine[2:], o_theirs)
    o_first = move(o_send, FIRST)
    late_far = after(late_far, o_send)
    t0, t1, m0, n0, m1, n1 = late_slices(m, idx, pos, gm, rest, late_far, mixture, kv, attention, earlies)
    t0, t1, o_first = phase(t0, t1, o_first)
    t0, t1 = move(t0, CORE), move(t1, CORE)
    send0 = add_rows(2 * rows, (n0, 0), (t0, 2 * rows))
    send1 = add_rows(2 * rows, (n1, 0), (after(t1, send0), 2 * rows))
    t0, t1, m0, m1, send0, send1 = (slots(a) for a in (t0, t1, m0, m1, send0, send1))
    first0, first1 = move(send0, FIRST), move(send1, FIRST)
    o_next = carry_on(o_mine, o_theirs, after(o_first, send0))
    o_second = move(o_next, SECOND)
    first0 = after(first0, o_next)
    next0 = carry_on(m0, t0, first0)
    second0 = move(next0, SECOND)
    first1 = after(first1, next0)
    next1 = carry_on(m1, t1, first1)
    second1 = move(next1, SECOND)
    sub = depth // 2
    o_sum = finish(o_mine, o_theirs, o_first, after(o_second, next1))
    sum0 = finish(m0, t0, first0, after(second0, next1))

    pieces = [o_sum[:, i * sub : (i + 1) * sub] for i in range(3)] + [sum0[:, :sub]]
    whole = jnp.zeros((4,) + pieces[0].shape, F32)
    for piece, place in zip(pieces, places):
        whole = lax.dynamic_update_slice_in_dim(whole, piece[None], place, 0)
    swapped = move(whole[2:].astype(BF16), CORE).astype(F32)
    low = jnp.where(m == 0, whole[:2], swapped)
    high = jnp.where(m == 0, swapped, whole[:2])
    summed = jnp.concatenate((low[0], high[0], low[1], high[1]), axis=1)
    output = (hidden.astype(F32) + summed).astype(BF16)

    edge = sum0.shape[1] - sub
    rest1 = m1[0].astype(F32) + t1[0].astype(F32) + first1[0].astype(F32)
    base = grad_out.astype(F32) + jnp.concatenate((sum0[:, sub:], rest1), axis=1)
    second1 = after(second1, base, whole)
    grad_hidden = (base + jnp.pad(second1.astype(F32), ((0, 0), (edge, 0)))).astype(BF16)
    return (output, grad_hidden)


def local_any(
    hidden,
    grad_out,
    database,
    enc_gain,
    query_weight,
    key_weight,
    value_weight,
    out_weight,
    block_ids,
    owners,
):
    tok_rows = hidden.shape[0]
    span_count = block_ids.shape[0]
    local_width = query_weight.shape[1]
    local_heads = local_width // HD
    owner_count = lax.axis_size("nbr")
    capacity = UNITS // owner_count
    score_scale = 1.0 / math.sqrt(HD)
    full_hidden, full_grad = (
        lax.all_gather(hidden, "mp", axis=1, tiled=True),
        lax.all_gather(grad_out, "mp", axis=1, tiled=True),
    )
    query_full, key_full, value_full, out_full = (
        lax.all_gather(query_weight, "dp", axis=0, tiled=True),
        lax.all_gather(key_weight, "dp", axis=0, tiled=True),
        lax.all_gather(value_weight, "dp", axis=0, tiled=True),
        lax.all_gather(out_weight, "dp", axis=1, tiled=True),
    )
    queries = jnp.dot(full_hidden, query_full, preferred_element_type=jnp.float32)
    queries = queries.astype(jnp.bfloat16).reshape(span_count, SPAN, local_heads, HD)
    owner_flat = owners.reshape(UNITS)
    id_flat = block_ids.reshape(UNITS)
    positions = jnp.arange(UNITS, dtype=jnp.int32)
    send_order = jnp.argsort(owner_flat * UNITS + positions)
    restore = jnp.argsort(send_order)
    requests = id_flat[send_order].reshape(owner_count, capacity)
    fetched = database[lax.all_to_all(requests, "nbr", split_axis=0, concat_axis=0, tiled=True)]
    encoded = encode_rows(fetched, enc_gain)
    key_part = jnp.einsum(
        "osbe,ef->osbf", encoded, key_full, preferred_element_type=jnp.float32
    ).astype(jnp.bfloat16)
    value_part = jnp.einsum(
        "osbe,ef->osbf", encoded, value_full, preferred_element_type=jnp.float32
    ).astype(jnp.bfloat16)
    stacked = jnp.concatenate((key_part, value_part), axis=-1)
    answers = lax.all_to_all(stacked, "nbr", split_axis=0, concat_axis=0, tiled=True)
    gathered = answers.reshape((UNITS,) + answers.shape[2:])[restore]
    kv_rows = gathered.reshape(span_count, UPC * BLOCK, 2 * local_width)
    key_rows = kv_rows[:, :, :local_width]
    value_rows = kv_rows[:, :, local_width:]
    key_rows = key_rows.reshape(span_count, UPC * BLOCK, local_heads, HD)
    value_rows = value_rows.reshape(span_count, UPC * BLOCK, local_heads, HD)
    scores = (
        jnp.einsum("cthd,cjhd->chtj", queries, key_rows, preferred_element_type=jnp.float32)
        * score_scale
    )
    attention = jax.nn.softmax(scores, axis=-1)
    attention_low = attention.astype(jnp.bfloat16)
    mixture = jnp.einsum(
        "chtj,cjhd->cthd", attention_low, value_rows, preferred_element_type=jnp.float32
    )
    mixture = mixture.astype(jnp.bfloat16).reshape(tok_rows, local_width)
    partial_out = jnp.dot(mixture, out_full, preferred_element_type=jnp.float32)
    summed = lax.psum_scatter(partial_out, "mp", scatter_dimension=1, tiled=True)
    output = (hidden.astype(jnp.float32) + summed).astype(jnp.bfloat16)
    grad_mixture = jnp.einsum("td,hd->th", full_grad, out_full, preferred_element_type=jnp.float32)
    grad_mixture = grad_mixture.astype(jnp.bfloat16).reshape(span_count, SPAN, local_heads, HD)
    grad_attention = jnp.einsum(
        "cthd,cjhd->chtj", grad_mixture, value_rows, preferred_element_type=jnp.float32
    )
    grad_scores = (
        attention
        * (grad_attention - jnp.sum(attention * grad_attention, axis=-1, keepdims=True))
        * score_scale
    )
    grad_scores = grad_scores.astype(jnp.bfloat16)
    grad_queries = jnp.einsum(
        "chtj,cjhd->cthd", grad_scores, key_rows, preferred_element_type=jnp.float32
    )
    grad_queries = grad_queries.astype(jnp.bfloat16).reshape(tok_rows, local_width)
    partial_grad = jnp.einsum(
        "th,dh->td", grad_queries, query_full, preferred_element_type=jnp.float32
    )
    grad_sum = lax.psum_scatter(partial_grad, "mp", scatter_dimension=1, tiled=True)
    grad_hidden = (grad_out.astype(jnp.float32) + grad_sum).astype(jnp.bfloat16)
    return (output, grad_hidden)


def solution(mesh):
    in_specs = (
        P(("groups", "dp", "nbr"), "mp"),
        P(("groups", "dp", "nbr"), "mp"),
        P(("groups", "dp", "nbr"), None, None),
        P(),
        P("dp", "mp"),
        P("dp", "mp"),
        P("dp", "mp"),
        P("mp", "dp"),
        P(("groups", "dp", "nbr"), None),
        P(("groups", "dp", "nbr"), None),
    )
    out_specs = (P(("groups", "dp", "nbr"), "mp"), P(("groups", "dp", "nbr"), "mp"))
    sizes = tuple(mesh.shape[a] for a in AXES)
    local = local_plane if sizes == (2, 4, 2, 2) else local_any
    return jax.shard_map(local, mesh=mesh, in_specs=in_specs, out_specs=out_specs, check_vma=False)
```

```python
import math

import jax
import jax.numpy as jnp
from jax import lax
from jax.experimental import pallas as pl
from jax.experimental.pallas import tpu as pltpu
from jax.sharding import PartitionSpec as P

HD = 128
SPAN = 64
BLOCK = 64
UPC = 4
UNITS = 8
AXES = ("groups", "dp", "nbr", "mp")
F32 = jnp.float32
BF16 = jnp.bfloat16


def encode_rows(states, enc_gain):
    widened = states.astype(F32)
    inverse = lax.rsqrt(jnp.mean(widened * widened, axis=-1, keepdims=True) + 1e-06)
    return (widened * inverse * enc_gain).astype(BF16)


def dot(a, b):
    return jnp.dot(a, b, preferred_element_type=F32)


def dot_t(a, b):
    return lax.dot_general(a, b, (((1,), (1,)), ((), ())), preferred_element_type=F32)


CROSSED = (0, 2, 1, 3)
TILE = 16
SCALE = 1.0 / math.sqrt(HD)
SHORT = pl.CostEstimate(flops=1024, bytes_accessed=1024, transcendentals=0)
LONG = pl.CostEstimate(flops=10**11, bytes_accessed=1024, transcendentals=0)


def shape_of(shape, dtype=BF16):
    return jax.ShapeDtypeStruct(shape, dtype)


def kernel_call(body, name, scalars, operands, out_shapes, in_specs):
    whole = lambda a: pl.BlockSpec(a.shape, lambda i, *_, n=len(a.shape): (0,) * n)
    return pl.pallas_call(
        body,
        grid_spec=pltpu.PrefetchScalarGridSpec(
            num_scalar_prefetch=len(scalars),
            grid=(1,),
            in_specs=[sp or whole(a) for sp, a in zip(in_specs, operands)],
            out_specs=[whole(a) for a in out_shapes],
        ),
        out_shape=tuple(out_shapes),
        compiler_params=pltpu.CompilerParams(vmem_limit_bytes=56 << 20),
        cost_estimate=LONG,
        name=name,
    )(*scalars, *operands)


class Copies:
    def __init__(self, sems):
        self.sems, self.used, self.open = sems, 0, {}

    def start(self, name, source, target):
        copy = pltpu.make_async_copy(source, target, self.sems.at[self.used])
        self.used += 1
        copy.start()
        self.open.setdefault(name, []).append(copy)

    def wait(self, *names):
        for name in names:
            for copy in self.open.pop(name):
                copy.wait()


def copy_call(body, name, scalars, operands, out_shapes, scratch, copies, cost=LONG, room=10, far=(), inputs=pl.ANY):
    smem = pl.BlockSpec(memory_space=pltpu.SMEM)
    need = sum(math.prod(a.shape) * jnp.dtype(a.dtype).itemsize for a in scratch)
    return pl.pallas_call(
        body,
        in_specs=[smem] * len(scalars) + [pl.BlockSpec(memory_space=inputs)] * len(operands),
        out_specs=[pl.BlockSpec(memory_space=pltpu.HBM if n in far else pl.ANY) for n in range(len(out_shapes))],
        out_shape=tuple(out_shapes),
        scratch_shapes=[pltpu.VMEM(a.shape, a.dtype) for a in scratch] + [pltpu.SemaphoreType.DMA((copies,))],
        compiler_params=pltpu.CompilerParams(vmem_limit_bytes=need + (room << 20)),
        cost_estimate=cost,
        name=name,
    )(*scalars, *operands)


def after(array, *earlier):
    return lax.optimization_barrier((array, *earlier))[0]


def step_kernel(before, now):
    now[0] = before[0] + 1


def step(*ready):
    smem = pl.BlockSpec(memory_space=pltpu.SMEM)
    return pl.pallas_call(
        step_kernel,
        in_specs=[smem],
        out_specs=smem,
        out_shape=shape_of((1,), jnp.int32),
        compiler_params=pltpu.CompilerParams(has_side_effects=True),
        cost_estimate=LONG,
        name="step",
    )(after(*ready))


def slices_kernel(place, q, k, v, o, early, late, both):
    depth, width = q.shape
    rank = k.shape[0]
    early[:rank] = k[...]
    early[rank : 2 * rank] = v[...]
    early[2 * rank :] = q[...]
    for c in range(depth // width):
        late[c * width : (c + 1) * width] = o[:, c * width : (c + 1) * width]
    both[: 2 * rank + depth] = early[...]
    both[2 * rank + depth :] = late[...]


def projection_slices(chip, qw, kw, vw, ow):
    depth, width, rank = qw.shape[0], qw.shape[1] // 4, kw.shape[0]
    column = lambda i, place: (0, place[0])
    return kernel_call(
        slices_kernel,
        "projection_slices",
        (chip.reshape(1),),
        (qw, kw, vw, ow),
        tuple(shape_of((n, width)) for n in (2 * rank + depth, depth, 2 * rank + 2 * depth)),
        [
            pl.BlockSpec((depth, width), column),
            pl.BlockSpec((rank, width), column),
            pl.BlockSpec((rank, width), column),
            pl.BlockSpec((width, depth), lambda i, place: (place[0], 0)),
        ],
    )


def prepare_kernel(core, owners, ids, hid, grad, db, gain, _, near, far):
    rows, half = hid.shape
    blocks, e = db.shape[0] // 2, db.shape[2]
    per = rows // BLOCK
    near[:, :half] = hid[...]
    for ref, which, start in ((near, core[0], half), (far, 1 - core[0], 0)):
        for part in range(blocks // per):
            states = db[pl.ds(which * blocks + part * per, per)].reshape(rows, e)
            ref[:, start + part * e : start + (part + 1) * e] = encode_rows(states, gain[...])
    near[:, near.shape[1] - half :] = grad[...]
    lane = lax.broadcasted_iota(jnp.int32, (rows, 128), 1)
    row = jnp.zeros(lane.shape, jnp.int32)
    for u in range(UNITS):
        at = divmod(u, UPC)
        row = jnp.where(lane == u, owners[at] * 2 * blocks + ids[at], row)
    near[:, near.shape[1] - half - 128 : near.shape[1] - half] = row.astype(F32).astype(BF16)


def prepare(core, owners, ids, hidden, grad, db, gain, earlier):
    rows, half = hidden.shape
    wide = db.shape[0] // 2 * BLOCK // rows * db.shape[2]
    return kernel_call(
        prepare_kernel,
        "prepare",
        (core.reshape(1), owners, ids),
        (hidden, grad, db, gain, earlier),
        (shape_of((rows, half + wide + 128 + half)), shape_of((rows, wide))),
        [None] * 4 + [pl.BlockSpec(memory_space=pl.ANY)],
    )


def rows_of(ref, first, count):
    return ref.at[pl.ds(first, count)]


def take_blocks(idx, kv, span, cols):
    parts = []
    for u in range(UPC):
        row = pl.multiple_of(idx[span, u] * TILE, TILE)
        parts.append(kv[pl.ds(row, BLOCK), cols])
    return jnp.concatenate(parts, axis=0)


def span_rows(n):
    return slice(n * SPAN, (n + 1) * SPAN)


def head_cols(width, h):
    return slice(h * HD, (h + 1) * HD), slice(width + h * HD, width + (h + 1) * HD)


def stage_tokens(copies, name, arrays, target):
    rows, half = arrays[0].shape[0], target.shape[1]
    for slot, a in enumerate(arrays):
        source = a.at[:, pl.ds(0, half)] if a.shape[1] > half else a
        copies.start(name, source, rows_of(target, slot * rows, rows))


def stage_output(copies, name, part, target):
    width = part.shape[1]
    count = target.shape[1] // width
    first = part.shape[0] - count * width
    for c in range(count):
        copies.start(name, rows_of(part, first + c * width, width), target.at[:, pl.ds(c * width, width)])


def project(core, mix, weights, theirs, mine, columns):
    sub, rows = weights.shape[1] // 2, mix.shape[0] // 4
    crossed = jnp.concatenate([mix[s * rows : (s + 1) * rows] for s in CROSSED])
    for ref, tokens, which in ((theirs, crossed, 1 - core), (mine, mix[...], core)):
        cut = pl.ds(pl.multiple_of(which * sub, sub), sub)
        ref[:, columns] = dot(tokens, weights[:, cut]).astype(BF16)


def forward_kernel(src, idx, pos, *refs):
    banks, own, other, parts = refs[:8], refs[:4], refs[8:12], refs[12:16]
    kv_out, mix_out, att_out = refs[16:19]
    states, kvw, kv, near, far, weights, queries, mix, att, sems = refs[19:]
    e, columns = kvw.shape
    rank, rows, wide = e // 4, banks[0].shape[0], states.shape[1]
    half, width = near.shape[1], weights.shape[1]
    depth = weights.shape[0] // 4
    spans = att.shape[0]
    copies = Copies(sems)
    for r, part in enumerate(parts):
        place = pl.multiple_of(src[r] * rank, TILE)
        for c in range(2):
            target = kvw.at[pl.ds(place, rank), pl.ds(c * width, width)]
            copies.start("kvw", rows_of(part, c * rank, rank), target)
    for b, bank in enumerate(banks):
        start = 0 if b == 4 else half
        copies.start(b // 4, bank.at[:, pl.ds(start, wide)], rows_of(states, b * rows, rows))
    for r, part in enumerate(parts):
        place = pl.multiple_of(pos[r] * depth, depth)
        copies.start("query", rows_of(part, 2 * rank, depth), rows_of(weights, place, depth))
    stage_tokens(copies, "near", own, near)
    stage_tokens(copies, "far", other, far)
    copies.wait("kvw")
    for side in range(2):
        copies.wait(side)
        for c in range(wide // e):
            block = states[4 * side * rows : 4 * (side + 1) * rows, c * e : (c + 1) * e]
            at = (8 * c + 4 * side) * rows
            kv[at : at + 4 * rows] = dot(block, kvw[...]).astype(BF16)
    copies.start("out", kv, kv_out)
    copies.wait("query", "near")
    total = dot(near[...], weights[:half])
    copies.wait("far")
    queries[...] = (total + dot(far[...], weights[half:])).astype(BF16)
    todo = [(span_rows(n), n, h, *head_cols(width, h)) for n in range(spans) for h in range(width // HD)]
    scores = [dot_t(queries[rows, kc], take_blocks(idx, kv, n, kc)) * SCALE for rows, n, _, kc, _ in todo]
    scores = [jnp.exp(s - jnp.max(s, axis=-1, keepdims=True)) for s in scores]
    scores = [s * (1.0 / jnp.sum(s, axis=-1, keepdims=True)) for s in scores]
    for s, (_, n, h, _, _) in zip(scores, todo):
        att[n, h] = s
    copies.start("out", att, att_out)
    for s, (rows, n, _, kc, vc) in zip(scores, todo):
        mix[rows, kc] = dot(s.astype(BF16), take_blocks(idx, kv, n, vc)).astype(BF16)
    copies.start("out", mix, mix_out)
    copies.wait("out")


def forward(src, idx, pos, own, far_states, other, parts, half, e, depth):
    rows, width = own[0].shape[0], parts[0].shape[1]
    tokens = 4 * rows
    spans = tokens // SPAN
    wide = far_states.shape[1]
    kv = shape_of((8 * wide // e * rows, 2 * width))
    mix = shape_of((tokens, width))
    att = shape_of((spans, width // HD, SPAN, UPC * BLOCK), F32)
    side = shape_of((tokens, half))
    return copy_call(
        forward_kernel,
        "forward",
        (src, idx, pos),
        (*own, far_states, *other[1:], *other, *parts),
        (kv, mix, att),
        (
            shape_of((8 * rows, wide)),
            shape_of((e, 2 * width)),
            kv,
            side,
            side,
            shape_of((4 * depth, width)),
            mix,
            mix,
            att,
        ),
        31,
        SHORT,
        42,
    )


def output_kernel(core, *refs):
    mix_in, parts = refs[0], refs[1:4]
    theirs_out, mine_out, mix, weights, theirs, mine, sems = refs[4:]
    sub = weights.shape[2] // 2
    copies = Copies(sems)
    copies.start("mix", mix_in, mix)
    for r, part in enumerate(parts):
        stage_output(copies, r, part, weights.at[r])
    copies.wait("mix")
    for r in range(3):
        copies.wait(r)
        project(core[0], mix, weights.at[r], theirs, mine, slice(r * sub, (r + 1) * sub))
    copies.start("out", theirs, theirs_out)
    copies.start("out", mine, mine_out)
    copies.wait("out")


def output_slices(core, mix, parts):
    tokens, width = mix.shape
    depth = parts[0].shape[0]
    out = shape_of((tokens, 3 * depth // 2))
    return copy_call(
        output_kernel,
        "output_slices",
        (core.reshape(1),),
        (mix, *parts),
        (out, out),
        (mix, shape_of((3, width, depth)), out, out),
        3 + 3 * (depth // width),
        far=(0,),
    )


def cotangent_kernel(pos, *refs):
    own, other, parts, gm_out, rest_out = refs[:4], refs[4:8], refs[8:11], refs[11], refs[12]
    grads, weights, gm, sems = refs[13:]
    rows, depth = own[0].shape[0], grads.shape[2]
    copies = Copies(sems)
    for r, part in enumerate(parts):
        stage_output(copies, r, part, weights.at[r])
    for side, arrays in enumerate((own, other)):
        for slot, a in enumerate(arrays):
            for c in range(2):
                target = grads.at[2 * side + c, pl.ds(slot * rows, rows)]
                start = a.shape[1] - 2 * depth + c * depth
                copies.start("grads", a.at[:, pl.ds(start, depth)], target)
    copies.wait("grads")
    copies.start("out", grads.at[pos[3]], rest_out)
    copies.wait(0, 1, 2)
    gm[...] = sum(dot_t(grads[pos[r]], weights[r]) for r in range(3))
    copies.start("out", gm, gm_out)
    copies.wait("out")


def cotangent(pos, own, other, parts):
    tokens, (depth, width) = 4 * own[0].shape[0], parts[0].shape
    gm = shape_of((tokens, width), F32)
    return copy_call(
        cotangent_kernel,
        "cotangent",
        (pos,),
        (*own, *other, *parts),
        (gm, shape_of((tokens, depth))),
        (shape_of((4, tokens, depth)), shape_of((3, width, depth)), gm),
        3 * (depth // width) + 16 + 2,
    )


def late_kernel(core, idx, pos, *refs):
    gm_in, rest_in, part, mix_in, kv_in, att_in, parts, results = *refs[:6], refs[6:10], refs[10:16]
    gmf, rest, wo, mix, kv, att, wq, gm, gq, crossed, wide, narrow, sems = refs[16:]
    width, depth = wq.shape[1], wq.shape[0] // 4
    spans, sub = att.shape[0], depth // 2
    copies = Copies(sems)
    stage_output(copies, "in", part, wo)
    copies.start("in", rest_in, rest)
    copies.start("in", gm_in, gmf)
    copies.start("kv", kv_in, kv)
    copies.start("kv", att_in, att)
    copies.start("mix", mix_in, mix)
    for r, piece in enumerate(parts):
        place = pl.multiple_of(pos[r] * depth, depth)
        copies.start("query", rows_of(piece, parts[0].shape[0] - depth, depth), rows_of(wq, place, depth))
    copies.wait("in")
    gm[...] = (gmf[...] + dot_t(rest[...], wo[...])).astype(BF16)
    copies.wait("kv")
    todo = [(span_rows(n), n, h, *head_cols(width, h)) for n in range(spans) for h in range(width // HD)]
    grads = [dot_t(gm[rows, kc], take_blocks(idx, kv, n, vc)) for rows, n, _, kc, vc in todo]
    inner = [jnp.sum(att[n, h] * g, axis=-1, keepdims=True) for g, (_, n, h, _, _) in zip(grads, todo)]
    grads = [(att[n, h] * (g - a) * SCALE).astype(BF16) for g, a, (_, n, h, _, _) in zip(grads, inner, todo)]
    for g, (rows, n, _, kc, _) in zip(grads, todo):
        slot, within = divmod(n, spans // 4)
        value = dot(g, take_blocks(idx, kv, n, kc)).astype(BF16)
        gq[rows, kc] = value
        crossed[span_rows(CROSSED[slot] * (spans // 4) + within), kc] = value
    copies.wait("mix", "query")
    project(core[0], mix, wo, wide.at[0], wide.at[1], slice(0, sub))
    first = wide.shape[2] - sub
    for n, (source, chunk, side) in enumerate(((crossed, 0, 2), (crossed, 1, 2), (gq, 0, 0), (gq, 1, 0))):
        buffer = (narrow if chunk else wide).at[n // 2]
        start, place = side * depth + chunk * first, 0 if chunk else sub
        for at in range(0, buffer.shape[1] - place, 256):
            value = dot_t(source[...], wq[start + at : start + at + 256])
            buffer[:, place + at : place + at + 256] = value.astype(BF16)
        if n < 2:
            copies.start("out", buffer, results[n])
        else:
            rows = buffer.shape[0] // 2
            for half in range(2):
                copies.start("out", rows_of(buffer, half * rows, rows), results[2 * n - 2 + half])
    copies.wait("out")


def late_slices(core, idx, pos, gm, rest, part, mix, kv, att, parts):
    tokens, width = gm.shape
    depth = part.shape[0]
    wide = shape_of((tokens, depth // 2 + depth))
    narrow = shape_of((tokens, depth))
    heads = shape_of((tokens, width))
    return copy_call(
        late_kernel,
        "late_slices",
        (core.reshape(1), idx, pos),
        (gm, rest, part, mix, kv, att, *parts),
        (wide, narrow, *(shape_of((tokens // 2, a.shape[1])) for a in (wide, wide, narrow, narrow))),
        (
            gm,
            rest,
            shape_of((width, depth)),
            mix,
            kv,
            att,
            shape_of((4 * depth, width)),
            heads,
            heads,
            heads,
            shape_of((2, *wide.shape)),
            shape_of((2, *narrow.shape)),
        ),
        depth // width + 5 + 4 + 6,
        room=43,
        far=(0, 1),
    )


def add_kernel(firsts, *refs):
    n = len(firsts)
    arrays, out, held, sems = refs[:n], refs[n], refs[n + 1], refs[n + 2]
    rows = held.shape[1] // 2
    copies = Copies(sems)
    for part in range(2):
        for k, array in enumerate(arrays):
            copies.start(part, rows_of(array, firsts[k] + part * rows, rows), rows_of(held.at[k], part * rows, rows))
    for part in range(2):
        cut = slice(part * rows, (part + 1) * rows)
        copies.wait(part)
        held[0, cut] = sum(held[k, cut].astype(F32) for k in range(n)).astype(BF16)
        copies.start("out", rows_of(held.at[0], part * rows, rows), rows_of(out, part * rows, rows))
    copies.wait("out")


def add_rows(rows, *terms):
    arrays, firsts = zip(*terms)
    shape = (rows, arrays[0].shape[1])
    return copy_call(
        lambda *refs: add_kernel(firsts, *refs),
        "add_rows",
        (),
        arrays,
        (shape_of(shape),),
        (shape_of((len(arrays), *shape)),),
        2 * len(arrays) + 2,
        room=46,
        far=(0,),
        inputs=pltpu.HBM,
    )[0]


def flat(y, z, x, m):
    return ((y * 4 + z) * 2 + x) * 2 + m


def permutation(move):
    pairs = []
    for y in range(2):
        for z in range(4):
            for x in range(2):
                for m in range(2):
                    pairs.append((flat(y, z, x, m), flat(*move(y, z, x, m))))
    return pairs


RING = (0, 1, 3, 2)
NEXT = {RING[i]: RING[(i + 1) % 4] for i in range(4)}
PREV = {RING[i]: RING[(i + 3) % 4] for i in range(4)}
FIRST = permutation(lambda y, z, x, m: (y, z, 1 - x, m) if m == 0 else (1 - y, z, x, m))
SECOND = permutation(lambda y, z, x, m: (1 - y, z, x, m) if m == 0 else (y, z, 1 - x, m))
DIAGONAL = permutation(lambda y, z, x, m: (1 - y, z, 1 - x, m))
CORE = permutation(lambda y, z, x, m: (y, z, x, 1 - m))
UP = permutation(lambda y, z, x, m: (y, NEXT[z], x, m))
DOWN = permutation(lambda y, z, x, m: (y, PREV[z], x, m))


def move(array, pairs):
    return lax.ppermute(array, AXES, pairs)


def phase(*arrays):
    return lax.optimization_barrier(arrays)


def local_plane(
    hidden,
    grad_out,
    database,
    enc_gain,
    query_weight,
    key_weight,
    value_weight,
    out_weight,
    block_ids,
    owners,
):
    y, z, x, m = (lax.axis_index(a).astype(jnp.int32) for a in AXES)
    depth, width = query_weight.shape[0], query_weight.shape[1] // 4
    rank = key_weight.shape[0]
    blocks, e = database.shape[0] // 2, database.shape[2]
    rows, half = hidden.shape
    nxt = lax.rem(2 * z + 1 - z // 2, 4)
    sources = (z, 3 - nxt, nxt, 3 - z)
    def codes_of(array):
        start = array.shape[1] - half - 128 if array.shape[1] > 128 else 0
        return array[0, start : start + UNITS].astype(jnp.int32)

    early, late, both = projection_slices(y * 2 + x, query_weight, key_weight, value_weight, out_weight)
    early_up, early_down = move(early, UP), move(both, DOWN)
    he, e_far = prepare(m, owners, block_ids, hidden, grad_out, database, enc_gain, early)
    he_first, he_second = move(he, FIRST), move(he, SECOND)
    places = [s ^ (2 * m) for s in sources]
    turn, zz = after(m, early_up, early_down), after(z, early_up, early_down)
    nxt = lax.rem(2 * zz + 1 - zz // 2, 4)
    sources = (zz, 3 - nxt, nxt, 3 - zz)
    pos, sources = jnp.stack([s ^ (2 * turn) for s in sources]), jnp.stack(sources)
    codes = codes_of(after(he, pos))
    he_first, he_second, codes = phase(he_first, he_second, codes)
    h_zero = move(hidden, CORE)
    early_far = move(after(early_up, he_first, he_second), UP)
    he_last = move(he_first, SECOND)
    he_two, he_one = move(he_first, CORE), move(he_second, CORE)
    h_zero, g_zero = move(hidden, CORE), move(grad_out, CORE)
    codes = jnp.stack([codes] + [codes_of(a) for a in (he_second, he_first)])
    he_two, he_one, h_zero, g_zero, codes = phase(he_two, he_one, h_zero, g_zero, codes)
    early_far = after(early_far, he_two)
    he_last = after(he_last, early_far)
    he_three = move(he_last, CORE)
    late_up = move(after(late, early_far), UP)
    he_own = (he, he_second, he_first, he_last)
    he_other = (h_zero, he_two, he_one, he_three)

    per = rows // BLOCK
    codes = jnp.concatenate((codes, codes_of(he_last)[None]))
    own_of, id_of = codes // (2 * blocks), codes % (2 * blocks)
    slot = jnp.arange(4, dtype=jnp.int32)
    rel_x = own_of ^ x
    rel_y = jnp.where(m == 0, slot % 2, slot // 2)[:, None]
    bank = jnp.where(m == 0, rel_x * 2 + rel_y, rel_y * 2 + rel_x)
    holder, block = id_of // blocks, id_of % blocks
    idx = (block // per * 8 + (holder ^ m) * 4 + bank) * per + block % per
    idx = (idx * (BLOCK // TILE)).reshape(-1, UPC).astype(jnp.int32)

    earlies = (early, early_up, early_down, early_far)
    kv, mixture, attention = forward(sources, idx, pos, he_own, e_far, he_other, earlies, half, e, depth)
    late_up, mixture = phase(late_up, mixture)

    late_far = move(late_up, UP)
    lates = (late, late_up, early_down)
    o_theirs, o_mine = output_slices(m, mixture, lates)

    def slots(array):
        return array.reshape(-1, rows, array.shape[1])

    def begin(mine, theirs):
        return (mine.astype(F32) + theirs[2:].astype(F32)).astype(BF16)

    def carry_on(mine, theirs, first):
        return (mine[1].astype(F32) + theirs[1].astype(F32) + first[1].astype(F32)).astype(BF16)

    def finish(mine, theirs, first, second):
        return sum(a.astype(F32) for a in (mine[0], theirs[0], first[0], second))

    o_theirs, o_mine = slots(move(o_theirs, CORE)), slots(o_mine)
    g_other = (after(g_zero, o_mine), *he_other[1:])
    gm, rest = cotangent(pos, he_own, g_other, lates)
    o_theirs = after(o_theirs, gm)
    o_send = begin(o_mine[2:], o_theirs)
    o_first = move(o_send, FIRST)
    late_far = after(late_far, o_send)
    t0, t1, m0, n0, m1, n1 = late_slices(m, idx, pos, gm, rest, late_far, mixture, kv, attention, earlies)
    t0, t1, o_first = phase(t0, t1, o_first)
    t0, t1 = move(t0, CORE), move(t1, CORE)
    o_next = carry_on(o_mine, o_theirs, o_first)
    o_second = move(o_next, SECOND)
    t0 = after(t0, o_next)
    send0 = add_rows(2 * rows, (n0, 0), (t0, 2 * rows))
    send1 = add_rows(2 * rows, (n1, 0), (after(t1, send0), 2 * rows))
    t0, t1, m0, m1, send0, send1 = (slots(a) for a in (t0, t1, m0, m1, send0, send1))
    first0, first1 = move(send0, FIRST), move(send1, FIRST)
    first0 = after(first0, o_next)
    next0 = carry_on(m0, t0, first0)
    second0 = move(next0, SECOND)
    o_sum = finish(o_mine, o_theirs, o_first, after(o_second, next0))
    first1 = after(first1, next0, o_sum)
    next1 = carry_on(m1, t1, first1)
    second1 = move(next1, SECOND)
    sub = depth // 2
    sum0 = finish(m0, t0, first0, after(second0, next1))

    pieces = [o_sum[:, i * sub : (i + 1) * sub] for i in range(3)] + [sum0[:, :sub]]
    whole = jnp.zeros((4,) + pieces[0].shape, F32)
    for piece, place in zip(pieces, places):
        whole = lax.dynamic_update_slice_in_dim(whole, piece[None], place, 0)
    swapped = move(whole[2:].astype(BF16), CORE).astype(F32)
    low = jnp.where(m == 0, whole[:2], swapped)
    high = jnp.where(m == 0, swapped, whole[:2])
    summed = jnp.concatenate((low[0], high[0], low[1], high[1]), axis=1)
    output = (hidden.astype(F32) + summed).astype(BF16)

    edge = sum0.shape[1] - sub
    rest1 = m1[0].astype(F32) + t1[0].astype(F32) + first1[0].astype(F32)
    base = grad_out.astype(F32) + jnp.concatenate((sum0[:, sub:], rest1), axis=1)
    second1 = after(second1, base, output)
    grad_hidden = (base + jnp.pad(second1.astype(F32), ((0, 0), (edge, 0)))).astype(BF16)
    return (output, grad_hidden)


def local_any(
    hidden,
    grad_out,
    database,
    enc_gain,
    query_weight,
    key_weight,
    value_weight,
    out_weight,
    block_ids,
    owners,
):
    tok_rows = hidden.shape[0]
    span_count = block_ids.shape[0]
    local_width = query_weight.shape[1]
    local_heads = local_width // HD
    owner_count = lax.axis_size("nbr")
    capacity = UNITS // owner_count
    score_scale = 1.0 / math.sqrt(HD)
    full_hidden, full_grad = (
        lax.all_gather(hidden, "mp", axis=1, tiled=True),
        lax.all_gather(grad_out, "mp", axis=1, tiled=True),
    )
    query_full, key_full, value_full, out_full = (
        lax.all_gather(query_weight, "dp", axis=0, tiled=True),
        lax.all_gather(key_weight, "dp", axis=0, tiled=True),
        lax.all_gather(value_weight, "dp", axis=0, tiled=True),
        lax.all_gather(out_weight, "dp", axis=1, tiled=True),
    )
    queries = jnp.dot(full_hidden, query_full, preferred_element_type=jnp.float32)
    queries = queries.astype(jnp.bfloat16).reshape(span_count, SPAN, local_heads, HD)
    owner_flat = owners.reshape(UNITS)
    id_flat = block_ids.reshape(UNITS)
    positions = jnp.arange(UNITS, dtype=jnp.int32)
    send_order = jnp.argsort(owner_flat * UNITS + positions)
    restore = jnp.argsort(send_order)
    requests = id_flat[send_order].reshape(owner_count, capacity)
    fetched = database[lax.all_to_all(requests, "nbr", split_axis=0, concat_axis=0, tiled=True)]
    encoded = encode_rows(fetched, enc_gain)
    key_part = jnp.einsum(
        "osbe,ef->osbf", encoded, key_full, preferred_element_type=jnp.float32
    ).astype(jnp.bfloat16)
    value_part = jnp.einsum(
        "osbe,ef->osbf", encoded, value_full, preferred_element_type=jnp.float32
    ).astype(jnp.bfloat16)
    stacked = jnp.concatenate((key_part, value_part), axis=-1)
    answers = lax.all_to_all(stacked, "nbr", split_axis=0, concat_axis=0, tiled=True)
    gathered = answers.reshape((UNITS,) + answers.shape[2:])[restore]
    kv_rows = gathered.reshape(span_count, UPC * BLOCK, 2 * local_width)
    key_rows = kv_rows[:, :, :local_width]
    value_rows = kv_rows[:, :, local_width:]
    key_rows = key_rows.reshape(span_count, UPC * BLOCK, local_heads, HD)
    value_rows = value_rows.reshape(span_count, UPC * BLOCK, local_heads, HD)
    scores = (
        jnp.einsum("cthd,cjhd->chtj", queries, key_rows, preferred_element_type=jnp.float32)
        * score_scale
    )
    attention = jax.nn.softmax(scores, axis=-1)
    attention_low = attention.astype(jnp.bfloat16)
    mixture = jnp.einsum(
        "chtj,cjhd->cthd", attention_low, value_rows, preferred_element_type=jnp.float32
    )
    mixture = mixture.astype(jnp.bfloat16).reshape(tok_rows, local_width)
    partial_out = jnp.dot(mixture, out_full, preferred_element_type=jnp.float32)
    summed = lax.psum_scatter(partial_out, "mp", scatter_dimension=1, tiled=True)
    output = (hidden.astype(jnp.float32) + summed).astype(jnp.bfloat16)
    grad_mixture = jnp.einsum("td,hd->th", full_grad, out_full, preferred_element_type=jnp.float32)
    grad_mixture = grad_mixture.astype(jnp.bfloat16).reshape(span_count, SPAN, local_heads, HD)
    grad_attention = jnp.einsum(
        "cthd,cjhd->chtj", grad_mixture, value_rows, preferred_element_type=jnp.float32
    )
    grad_scores = (
        attention
        * (grad_attention - jnp.sum(attention * grad_attention, axis=-1, keepdims=True))
        * score_scale
    )
    grad_scores = grad_scores.astype(jnp.bfloat16)
    grad_queries = jnp.einsum(
        "chtj,cjhd->cthd", grad_scores, key_rows, preferred_element_type=jnp.float32
    )
    grad_queries = grad_queries.astype(jnp.bfloat16).reshape(tok_rows, local_width)
    partial_grad = jnp.einsum(
        "th,dh->td", grad_queries, query_full, preferred_element_type=jnp.float32
    )
    grad_sum = lax.psum_scatter(partial_grad, "mp", scatter_dimension=1, tiled=True)
    grad_hidden = (grad_out.astype(jnp.float32) + grad_sum).astype(jnp.bfloat16)
    return (output, grad_hidden)


def solution(mesh):
    in_specs = (
        P(("groups", "dp", "nbr"), "mp"),
        P(("groups", "dp", "nbr"), "mp"),
        P(("groups", "dp", "nbr"), None, None),
        P(),
        P("dp", "mp"),
        P("dp", "mp"),
        P("dp", "mp"),
        P("mp", "dp"),
        P(("groups", "dp", "nbr"), None),
        P(("groups", "dp", "nbr"), None),
    )
    out_specs = (P(("groups", "dp", "nbr"), "mp"), P(("groups", "dp", "nbr"), "mp"))
    sizes = tuple(mesh.shape[a] for a in AXES)
    local = local_plane if sizes == (2, 4, 2, 2) else local_any
    return jax.shard_map(local, mesh=mesh, in_specs=in_specs, out_specs=out_specs, check_vma=False)
```

```python
import math

import jax
import jax.numpy as jnp
from jax import lax
from jax.experimental import pallas as pl
from jax.experimental.pallas import tpu as pltpu
from jax.sharding import PartitionSpec as P

HD = 128
SPAN = 64
BLOCK = 64
UPC = 4
UNITS = 8
AXES = ("groups", "dp", "nbr", "mp")
F32 = jnp.float32
BF16 = jnp.bfloat16


def encode_rows(states, enc_gain):
    widened = states.astype(F32)
    inverse = lax.rsqrt(jnp.mean(widened * widened, axis=-1, keepdims=True) + 1e-06)
    return (widened * inverse * enc_gain).astype(BF16)


def dot(a, b):
    return jnp.dot(a, b, preferred_element_type=F32)


def dot_t(a, b):
    return lax.dot_general(a, b, (((1,), (1,)), ((), ())), preferred_element_type=F32)


CROSSED = (0, 2, 1, 3)
TILE = 16
SCALE = 1.0 / math.sqrt(HD)
SHORT = pl.CostEstimate(flops=1024, bytes_accessed=1024, transcendentals=0)
LONG = pl.CostEstimate(flops=10**11, bytes_accessed=1024, transcendentals=0)


def shape_of(shape, dtype=BF16):
    return jax.ShapeDtypeStruct(shape, dtype)


def kernel_call(body, name, scalars, operands, out_shapes, in_specs):
    whole = lambda a: pl.BlockSpec(a.shape, lambda i, *_, n=len(a.shape): (0,) * n)
    return pl.pallas_call(
        body,
        grid_spec=pltpu.PrefetchScalarGridSpec(
            num_scalar_prefetch=len(scalars),
            grid=(1,),
            in_specs=[sp or whole(a) for sp, a in zip(in_specs, operands)],
            out_specs=[whole(a) for a in out_shapes],
        ),
        out_shape=tuple(out_shapes),
        compiler_params=pltpu.CompilerParams(vmem_limit_bytes=56 << 20),
        cost_estimate=LONG,
        name=name,
    )(*scalars, *operands)


class Copies:
    def __init__(self, sems):
        self.sems, self.used, self.open = sems, 0, {}

    def start(self, name, source, target):
        copy = pltpu.make_async_copy(source, target, self.sems.at[self.used])
        self.used += 1
        copy.start()
        self.open.setdefault(name, []).append(copy)

    def wait(self, *names):
        for name in names:
            for copy in self.open.pop(name):
                copy.wait()


def copy_call(body, name, scalars, operands, out_shapes, scratch, copies, cost=LONG, room=10, far=(), inputs=pl.ANY):
    smem = pl.BlockSpec(memory_space=pltpu.SMEM)
    need = sum(math.prod(a.shape) * jnp.dtype(a.dtype).itemsize for a in scratch)
    return pl.pallas_call(
        body,
        in_specs=[smem] * len(scalars) + [pl.BlockSpec(memory_space=inputs)] * len(operands),
        out_specs=[pl.BlockSpec(memory_space=pltpu.HBM if n in far else pl.ANY) for n in range(len(out_shapes))],
        out_shape=tuple(out_shapes),
        scratch_shapes=[pltpu.VMEM(a.shape, a.dtype) for a in scratch] + [pltpu.SemaphoreType.DMA((copies,))],
        compiler_params=pltpu.CompilerParams(vmem_limit_bytes=need + (room << 20)),
        cost_estimate=cost,
        name=name,
    )(*scalars, *operands)


def after(array, *earlier):
    return lax.optimization_barrier((array, *earlier))[0]


def step_kernel(before, now):
    now[0] = before[0] + 1


def step(*ready):
    smem = pl.BlockSpec(memory_space=pltpu.SMEM)
    return pl.pallas_call(
        step_kernel,
        in_specs=[smem],
        out_specs=smem,
        out_shape=shape_of((1,), jnp.int32),
        compiler_params=pltpu.CompilerParams(has_side_effects=True),
        cost_estimate=LONG,
        name="step",
    )(after(*ready))


def slices_kernel(place, q, k, v, o, out):
    depth, width = q.shape
    rank = k.shape[0]
    out[:rank] = k[...]
    out[rank : 2 * rank] = v[...]
    out[2 * rank : 2 * rank + depth] = q[...]
    for c in range(depth // width):
        at = 2 * rank + depth + c * width
        out[at : at + width] = o[:, c * width : (c + 1) * width]


def projection_slices(chip, qw, kw, vw, ow):
    depth, width, rank = qw.shape[0], qw.shape[1] // 4, kw.shape[0]
    column = lambda i, place: (0, place[0])
    return kernel_call(
        slices_kernel,
        "projection_slices",
        (chip.reshape(1),),
        (qw, kw, vw, ow),
        (shape_of((2 * rank + 2 * depth, width)),),
        [
            pl.BlockSpec((depth, width), column),
            pl.BlockSpec((rank, width), column),
            pl.BlockSpec((rank, width), column),
            pl.BlockSpec((width, depth), lambda i, place: (place[0], 0)),
        ],
    )[0]


def prepare_kernel(core, owners, ids, hid, grad, db, gain, _, near, far):
    rows, half = hid.shape
    blocks, e = db.shape[0] // 2, db.shape[2]
    per = rows // BLOCK
    near[:, :half] = hid[...]
    for ref, which, start in ((near, core[0], half), (far, 1 - core[0], 0)):
        for part in range(blocks // per):
            states = db[pl.ds(which * blocks + part * per, per)].reshape(rows, e)
            ref[:, start + part * e : start + (part + 1) * e] = encode_rows(states, gain[...])
    near[:, near.shape[1] - half :] = grad[...]
    lane = lax.broadcasted_iota(jnp.int32, (rows, 128), 1)
    row = jnp.zeros(lane.shape, jnp.int32)
    for u in range(UNITS):
        at = divmod(u, UPC)
        row = jnp.where(lane == u, owners[at] * 2 * blocks + ids[at], row)
    near[:, near.shape[1] - half - 128 : near.shape[1] - half] = row.astype(F32).astype(BF16)


def prepare(core, owners, ids, hidden, grad, db, gain, earlier):
    rows, half = hidden.shape
    wide = db.shape[0] // 2 * BLOCK // rows * db.shape[2]
    return kernel_call(
        prepare_kernel,
        "prepare",
        (core.reshape(1), owners, ids),
        (hidden, grad, db, gain, earlier),
        (shape_of((rows, half + wide + 128 + half)), shape_of((rows, wide))),
        [None] * 4 + [pl.BlockSpec(memory_space=pl.ANY)],
    )


def rows_of(ref, first, count):
    return ref.at[pl.ds(first, count)]


def take_blocks(idx, kv, span, cols):
    parts = []
    for u in range(UPC):
        row = pl.multiple_of(idx[span, u] * TILE, TILE)
        parts.append(kv[pl.ds(row, BLOCK), cols])
    return jnp.concatenate(parts, axis=0)


def span_rows(n):
    return slice(n * SPAN, (n + 1) * SPAN)


def head_cols(width, h):
    return slice(h * HD, (h + 1) * HD), slice(width + h * HD, width + (h + 1) * HD)


def stage_tokens(copies, name, arrays, target):
    rows, half = arrays[0].shape[0], target.shape[1]
    for slot, a in enumerate(arrays):
        source = a.at[:, pl.ds(0, half)] if a.shape[1] > half else a
        copies.start(name, source, rows_of(target, slot * rows, rows))


def stage_output(copies, name, part, target):
    width = part.shape[1]
    count = target.shape[1] // width
    first = part.shape[0] - count * width
    for c in range(count):
        copies.start(name, rows_of(part, first + c * width, width), target.at[:, pl.ds(c * width, width)])


def project(core, mix, weights, theirs, mine, columns):
    sub, rows = weights.shape[1] // 2, mix.shape[0] // 4
    crossed = jnp.concatenate([mix[s * rows : (s + 1) * rows] for s in CROSSED])
    for ref, tokens, which in ((theirs, crossed, 1 - core), (mine, mix[...], core)):
        cut = pl.ds(pl.multiple_of(which * sub, sub), sub)
        ref[:, columns] = dot(tokens, weights[:, cut]).astype(BF16)


def forward_kernel(src, idx, pos, *refs):
    banks, own, other, parts = refs[:8], refs[:4], refs[8:12], refs[12:16]
    kv_out, mix_out, att_out = refs[16:19]
    states, kvw, kv, near, far, weights, queries, mix, att, sems = refs[19:]
    e, columns = kvw.shape
    rank, rows, wide = e // 4, banks[0].shape[0], states.shape[1]
    half, width = near.shape[1], weights.shape[1]
    depth = weights.shape[0] // 4
    spans = att.shape[0]
    copies = Copies(sems)
    for r, part in enumerate(parts):
        place = pl.multiple_of(src[r] * rank, TILE)
        for c in range(2):
            target = kvw.at[pl.ds(place, rank), pl.ds(c * width, width)]
            copies.start("kvw", rows_of(part, c * rank, rank), target)
    for b, bank in enumerate(banks):
        start = 0 if b == 4 else half
        copies.start(b // 4, bank.at[:, pl.ds(start, wide)], rows_of(states, b * rows, rows))
    for r, part in enumerate(parts):
        place = pl.multiple_of(pos[r] * depth, depth)
        copies.start("query", rows_of(part, 2 * rank, depth), rows_of(weights, place, depth))
    stage_tokens(copies, "near", own, near)
    stage_tokens(copies, "far", other, far)
    copies.wait("kvw")
    for side in range(2):
        copies.wait(side)
        for c in range(wide // e):
            block = states[4 * side * rows : 4 * (side + 1) * rows, c * e : (c + 1) * e]
            at = (8 * c + 4 * side) * rows
            kv[at : at + 4 * rows] = dot(block, kvw[...]).astype(BF16)
    copies.start("out", kv, kv_out)
    copies.wait("query", "near")
    total = dot(near[...], weights[:half])
    copies.wait("far")
    queries[...] = (total + dot(far[...], weights[half:])).astype(BF16)
    todo = [(span_rows(n), n, h, *head_cols(width, h)) for n in range(spans) for h in range(width // HD)]
    scores = [dot_t(queries[rows, kc], take_blocks(idx, kv, n, kc)) * SCALE for rows, n, _, kc, _ in todo]
    scores = [jnp.exp(s - jnp.max(s, axis=-1, keepdims=True)) for s in scores]
    scores = [s * (1.0 / jnp.sum(s, axis=-1, keepdims=True)) for s in scores]
    for s, (_, n, h, _, _) in zip(scores, todo):
        att[n, h] = s
    copies.start("out", att, att_out)
    for s, (rows, n, _, kc, vc) in zip(scores, todo):
        mix[rows, kc] = dot(s.astype(BF16), take_blocks(idx, kv, n, vc)).astype(BF16)
    copies.start("out", mix, mix_out)
    copies.wait("out")


def forward(src, idx, pos, own, far_states, other, parts, half, e, depth):
    rows, width = own[0].shape[0], parts[0].shape[1]
    tokens = 4 * rows
    spans = tokens // SPAN
    wide = far_states.shape[1]
    kv = shape_of((8 * wide // e * rows, 2 * width))
    mix = shape_of((tokens, width))
    att = shape_of((spans, width // HD, SPAN, UPC * BLOCK), F32)
    side = shape_of((tokens, half))
    return copy_call(
        forward_kernel,
        "forward",
        (src, idx, pos),
        (*own, far_states, *other[1:], *other, *parts),
        (kv, mix, att),
        (
            shape_of((8 * rows, wide)),
            shape_of((e, 2 * width)),
            kv,
            side,
            side,
            shape_of((4 * depth, width)),
            mix,
            mix,
            att,
        ),
        31,
        SHORT,
        42,
    )


def output_kernel(core, *refs):
    mix_in, parts = refs[0], refs[1:4]
    theirs_out, mine_out, mix, weights, theirs, mine, sems = refs[4:]
    sub = weights.shape[2] // 2
    copies = Copies(sems)
    copies.start("mix", mix_in, mix)
    for r, part in enumerate(parts):
        stage_output(copies, r, part, weights.at[r])
    copies.wait("mix")
    for r in range(3):
        copies.wait(r)
        project(core[0], mix, weights.at[r], theirs, mine, slice(r * sub, (r + 1) * sub))
    copies.start("out", theirs, theirs_out)
    copies.start("out", mine, mine_out)
    copies.wait("out")


def output_slices(core, mix, parts):
    tokens, width = mix.shape
    depth = parts[0].shape[0]
    out = shape_of((tokens, 3 * depth // 2))
    return copy_call(
        output_kernel,
        "output_slices",
        (core.reshape(1),),
        (mix, *parts),
        (out, out),
        (mix, shape_of((3, width, depth)), out, out),
        3 + 3 * (depth // width),
        far=(0,),
    )


def cotangent_kernel(pos, *refs):
    own, other, parts, gm_out, rest_out = refs[:4], refs[4:8], refs[8:11], refs[11], refs[12]
    grads, weights, gm, sems = refs[13:]
    rows, depth = own[0].shape[0], grads.shape[2]
    copies = Copies(sems)
    for r, part in enumerate(parts):
        stage_output(copies, r, part, weights.at[r])
    for side, arrays in enumerate((own, other)):
        for slot, a in enumerate(arrays):
            for c in range(2):
                target = grads.at[2 * side + c, pl.ds(slot * rows, rows)]
                start = a.shape[1] - 2 * depth + c * depth
                copies.start("grads", a.at[:, pl.ds(start, depth)], target)
    copies.wait("grads")
    copies.start("out", grads.at[pos[3]], rest_out)
    copies.wait(0, 1, 2)
    gm[...] = sum(dot_t(grads[pos[r]], weights[r]) for r in range(3))
    copies.start("out", gm, gm_out)
    copies.wait("out")


def cotangent(pos, own, other, parts):
    tokens, (depth, width) = 4 * own[0].shape[0], parts[0].shape
    gm = shape_of((tokens, width), F32)
    return copy_call(
        cotangent_kernel,
        "cotangent",
        (pos,),
        (*own, *other, *parts),
        (gm, shape_of((tokens, depth))),
        (shape_of((4, tokens, depth)), shape_of((3, width, depth)), gm),
        3 * (depth // width) + 16 + 2,
    )


def late_kernel(core, idx, pos, *refs):
    gm_in, rest_in, part, mix_in, kv_in, att_in, parts, results = *refs[:6], refs[6:10], refs[10:16]
    gmf, rest, wo, mix, kv, att, wq, gm, gq, crossed, wide, narrow, sems = refs[16:]
    width, depth = wq.shape[1], wq.shape[0] // 4
    spans, sub = att.shape[0], depth // 2
    copies = Copies(sems)
    stage_output(copies, "in", part, wo)
    copies.start("in", rest_in, rest)
    copies.start("in", gm_in, gmf)
    copies.start("kv", kv_in, kv)
    copies.start("kv", att_in, att)
    copies.start("mix", mix_in, mix)
    for r, piece in enumerate(parts):
        place = pl.multiple_of(pos[r] * depth, depth)
        copies.start("query", rows_of(piece, parts[0].shape[0] - depth, depth), rows_of(wq, place, depth))
    copies.wait("in")
    gm[...] = (gmf[...] + dot_t(rest[...], wo[...])).astype(BF16)
    copies.wait("kv")
    todo = [(span_rows(n), n, h, *head_cols(width, h)) for n in range(spans) for h in range(width // HD)]
    grads = [dot_t(gm[rows, kc], take_blocks(idx, kv, n, vc)) for rows, n, _, kc, vc in todo]
    inner = [jnp.sum(att[n, h] * g, axis=-1, keepdims=True) for g, (_, n, h, _, _) in zip(grads, todo)]
    grads = [(att[n, h] * (g - a) * SCALE).astype(BF16) for g, a, (_, n, h, _, _) in zip(grads, inner, todo)]
    for g, (rows, n, _, kc, _) in zip(grads, todo):
        slot, within = divmod(n, spans // 4)
        value = dot(g, take_blocks(idx, kv, n, kc)).astype(BF16)
        gq[rows, kc] = value
        crossed[span_rows(CROSSED[slot] * (spans // 4) + within), kc] = value
    copies.wait("mix", "query")
    project(core[0], mix, wo, wide.at[0], wide.at[1], slice(0, sub))
    first = wide.shape[2] - sub
    for n, (source, chunk, side) in enumerate(((crossed, 0, 2), (crossed, 1, 2), (gq, 0, 0), (gq, 1, 0))):
        buffer = (narrow if chunk else wide).at[n // 2]
        start, place = side * depth + chunk * first, 0 if chunk else sub
        for at in range(0, buffer.shape[1] - place, 256):
            value = dot_t(source[...], wq[start + at : start + at + 256])
            buffer[:, place + at : place + at + 256] = value.astype(BF16)
        if n < 2:
            copies.start("out", buffer, results[n])
        else:
            rows = buffer.shape[0] // 2
            for half in range(2):
                copies.start("out", rows_of(buffer, half * rows, rows), results[2 * n - 2 + half])
    copies.wait("out")


def late_slices(core, idx, pos, gm, rest, part, mix, kv, att, parts):
    tokens, width = gm.shape
    depth = part.shape[0]
    wide = shape_of((tokens, depth // 2 + depth))
    narrow = shape_of((tokens, depth))
    heads = shape_of((tokens, width))
    return copy_call(
        late_kernel,
        "late_slices",
        (core.reshape(1), idx, pos),
        (gm, rest, part, mix, kv, att, *parts),
        (wide, narrow, *(shape_of((tokens // 2, a.shape[1])) for a in (wide, wide, narrow, narrow))),
        (
            gm,
            rest,
            shape_of((width, depth)),
            mix,
            kv,
            att,
            shape_of((4 * depth, width)),
            heads,
            heads,
            heads,
            shape_of((2, *wide.shape)),
            shape_of((2, *narrow.shape)),
        ),
        depth // width + 5 + 4 + 6,
        room=43,
        far=(0, 1),
    )


def add_kernel(firsts, *refs):
    n = len(firsts)
    arrays, out, held, sems = refs[:n], refs[n], refs[n + 1], refs[n + 2]
    rows = held.shape[1] // 2
    copies = Copies(sems)
    for part in range(2):
        for k, array in enumerate(arrays):
            copies.start(part, rows_of(array, firsts[k] + part * rows, rows), rows_of(held.at[k], part * rows, rows))
    for part in range(2):
        cut = slice(part * rows, (part + 1) * rows)
        copies.wait(part)
        held[0, cut] = sum(held[k, cut].astype(F32) for k in range(n)).astype(BF16)
        copies.start("out", rows_of(held.at[0], part * rows, rows), rows_of(out, part * rows, rows))
    copies.wait("out")


def add_rows(rows, *terms):
    arrays, firsts = zip(*terms)
    shape = (rows, arrays[0].shape[1])
    return copy_call(
        lambda *refs: add_kernel(firsts, *refs),
        "add_rows",
        (),
        arrays,
        (shape_of(shape),),
        (shape_of((len(arrays), *shape)),),
        2 * len(arrays) + 2,
        room=46,
        far=(0,),
        inputs=pltpu.HBM,
    )[0]


def flat(y, z, x, m):
    return ((y * 4 + z) * 2 + x) * 2 + m


def permutation(move):
    pairs = []
    for y in range(2):
        for z in range(4):
            for x in range(2):
                for m in range(2):
                    pairs.append((flat(y, z, x, m), flat(*move(y, z, x, m))))
    return pairs


RING = (0, 1, 3, 2)
NEXT = {RING[i]: RING[(i + 1) % 4] for i in range(4)}
PREV = {RING[i]: RING[(i + 3) % 4] for i in range(4)}
FIRST = permutation(lambda y, z, x, m: (y, z, 1 - x, m) if m == 0 else (1 - y, z, x, m))
SECOND = permutation(lambda y, z, x, m: (1 - y, z, x, m) if m == 0 else (y, z, 1 - x, m))
CORE = permutation(lambda y, z, x, m: (y, z, x, 1 - m))
UP = permutation(lambda y, z, x, m: (y, NEXT[z], x, m))
DOWN = permutation(lambda y, z, x, m: (y, PREV[z], x, m))


def move(array, pairs):
    return lax.ppermute(array, AXES, pairs)


def phase(*arrays):
    return lax.optimization_barrier(arrays)


def local_plane(
    hidden,
    grad_out,
    database,
    enc_gain,
    query_weight,
    key_weight,
    value_weight,
    out_weight,
    block_ids,
    owners,
):
    y, z, x, m = (lax.axis_index(a).astype(jnp.int32) for a in AXES)
    depth, width = query_weight.shape[0], query_weight.shape[1] // 4
    rank = key_weight.shape[0]
    blocks, e = database.shape[0] // 2, database.shape[2]
    rows, half = hidden.shape
    nxt = lax.rem(2 * z + 1 - z // 2, 4)
    sources = (z, 3 - nxt, nxt, 3 - z)

    def codes_of(array):
        start = array.shape[1] - half - 128 if array.shape[1] > 128 else 0
        return array[0, start : start + UNITS].astype(jnp.int32)

    both = projection_slices(y * 2 + x, query_weight, key_weight, value_weight, out_weight)
    early, late = both[: 2 * rank + depth], both[2 * rank + depth :]
    early_up, early_down = move(early, UP), move(both, DOWN)
    he, e_far = prepare(m, owners, block_ids, hidden, grad_out, database, enc_gain, both)
    he_first, he_second = move(he, FIRST), move(he, SECOND)
    places = [s ^ (2 * m) for s in sources]
    turn, zz = after(m, early_up, early_down), after(z, early_up, early_down)
    nxt = lax.rem(2 * zz + 1 - zz // 2, 4)
    sources = (zz, 3 - nxt, nxt, 3 - zz)
    pos, sources = jnp.stack([s ^ (2 * turn) for s in sources]), jnp.stack(sources)
    codes = codes_of(after(he, pos))
    he_first, he_second, codes = phase(he_first, he_second, codes)
    early_far = move(after(early_up, he_first, he_second), UP)
    he_last = move(he_first, SECOND)
    he_two, he_one = move(he_first, CORE), move(he_second, CORE)
    h_zero, g_zero = move(hidden, CORE), move(grad_out, CORE)
    codes = jnp.stack([codes] + [codes_of(a) for a in (he_second, he_first)])
    he_two, he_one, h_zero, g_zero, codes, sources, late = phase(
        he_two, he_one, h_zero, g_zero, codes, sources, late
    )
    early_far = after(early_far, he_two)
    he_last = after(he_last, early_far)
    he_three = move(he_last, CORE)
    late_up = move(after(late, early_far), UP)
    he_own = (he, he_second, he_first, he_last)
    he_other = (h_zero, he_two, he_one, he_three)

    per = rows // BLOCK
    codes = jnp.concatenate((codes, codes_of(he_last)[None]))
    own_of, id_of = codes // (2 * blocks), codes % (2 * blocks)
    slot = jnp.arange(4, dtype=jnp.int32)
    rel_x = own_of ^ x
    rel_y = jnp.where(m == 0, slot % 2, slot // 2)[:, None]
    bank = jnp.where(m == 0, rel_x * 2 + rel_y, rel_y * 2 + rel_x)
    holder, block = id_of // blocks, id_of % blocks
    idx = (block // per * 8 + (holder ^ m) * 4 + bank) * per + block % per
    idx = (idx * (BLOCK // TILE)).reshape(-1, UPC).astype(jnp.int32)

    earlies = (early, early_up, early_down, early_far)
    kv, mixture, attention = forward(sources, idx, pos, he_own, e_far, he_other, earlies, half, e, depth)
    late_up, mixture = phase(late_up, mixture)

    late_far = move(late_up, UP)
    lates = (late, late_up, early_down)
    o_theirs, o_mine = output_slices(m, mixture, lates)

    def slots(array):
        return array.reshape(-1, rows, array.shape[1])

    def begin(mine, theirs):
        return (mine.astype(F32) + theirs[2:].astype(F32)).astype(BF16)

    def carry_on(mine, theirs, first):
        return (mine[1].astype(F32) + theirs[1].astype(F32) + first[1].astype(F32)).astype(BF16)

    def finish(mine, theirs, first, second):
        return sum(a.astype(F32) for a in (mine[0], theirs[0], first[0], second))

    o_theirs, o_mine = slots(move(o_theirs, CORE)), slots(o_mine)
    g_other = (after(g_zero, o_mine), *he_other[1:])
    gm, rest = cotangent(pos, he_own, g_other, lates)
    o_theirs = after(o_theirs, gm)
    o_send = begin(o_mine[2:], o_theirs)
    o_first = move(o_send, FIRST)
    late_far = after(late_far, o_send)
    t0, t1, m0, n0, m1, n1 = late_slices(m, idx, pos, gm, rest, late_far, mixture, kv, attention, earlies)
    t0, t1, o_first = phase(t0, t1, o_first)
    t0, t1 = move(t0, CORE), move(t1, CORE)
    o_next = carry_on(o_mine, o_theirs, o_first)
    o_second = move(o_next, SECOND)
    t0 = after(t0, o_next)
    send0 = add_rows(2 * rows, (n0, 0), (t0, 2 * rows))
    send1 = add_rows(2 * rows, (n1, 0), (after(t1, send0), 2 * rows))
    t0, t1, m0, m1, send0, send1 = (slots(a) for a in (t0, t1, m0, m1, send0, send1))
    first0, first1 = move(send0, FIRST), move(send1, FIRST)
    first0 = after(first0, o_next)
    next0 = carry_on(m0, t0, first0)
    second0 = move(next0, SECOND)
    o_sum = finish(o_mine, o_theirs, o_first, after(o_second, next0))
    first1 = after(first1, next0, o_sum)
    next1 = carry_on(m1, t1, first1)
    second1 = move(next1, SECOND)
    sub = depth // 2
    sum0 = finish(m0, t0, first0, after(second0, next1))

    pieces = [o_sum[:, i * sub : (i + 1) * sub] for i in range(3)] + [sum0[:, :sub]]
    whole = jnp.zeros((4,) + pieces[0].shape, F32)
    for piece, place in zip(pieces, places):
        whole = lax.dynamic_update_slice_in_dim(whole, piece[None], place, 0)
    swapped = move(whole[2:].astype(BF16), CORE).astype(F32)
    low = jnp.where(m == 0, whole[:2], swapped)
    high = jnp.where(m == 0, swapped, whole[:2])
    summed = jnp.concatenate((low[0], high[0], low[1], high[1]), axis=1)
    output = (hidden.astype(F32) + summed).astype(BF16)

    edge = sum0.shape[1] - sub
    rest1 = m1[0].astype(F32) + t1[0].astype(F32) + first1[0].astype(F32)
    base = grad_out.astype(F32) + jnp.concatenate((sum0[:, sub:], rest1), axis=1)
    second1 = after(second1, base, output)
    grad_hidden = (base + jnp.pad(second1.astype(F32), ((0, 0), (edge, 0)))).astype(BF16)
    return (output, grad_hidden)


def local_any(
    hidden,
    grad_out,
    database,
    enc_gain,
    query_weight,
    key_weight,
    value_weight,
    out_weight,
    block_ids,
    owners,
):
    tok_rows = hidden.shape[0]
    span_count = block_ids.shape[0]
    local_width = query_weight.shape[1]
    local_heads = local_width // HD
    owner_count = lax.axis_size("nbr")
    capacity = UNITS // owner_count
    score_scale = 1.0 / math.sqrt(HD)
    full_hidden, full_grad = (
        lax.all_gather(hidden, "mp", axis=1, tiled=True),
        lax.all_gather(grad_out, "mp", axis=1, tiled=True),
    )
    query_full, key_full, value_full, out_full = (
        lax.all_gather(query_weight, "dp", axis=0, tiled=True),
        lax.all_gather(key_weight, "dp", axis=0, tiled=True),
        lax.all_gather(value_weight, "dp", axis=0, tiled=True),
        lax.all_gather(out_weight, "dp", axis=1, tiled=True),
    )
    queries = jnp.dot(full_hidden, query_full, preferred_element_type=jnp.float32)
    queries = queries.astype(jnp.bfloat16).reshape(span_count, SPAN, local_heads, HD)
    owner_flat = owners.reshape(UNITS)
    id_flat = block_ids.reshape(UNITS)
    positions = jnp.arange(UNITS, dtype=jnp.int32)
    send_order = jnp.argsort(owner_flat * UNITS + positions)
    restore = jnp.argsort(send_order)
    requests = id_flat[send_order].reshape(owner_count, capacity)
    fetched = database[lax.all_to_all(requests, "nbr", split_axis=0, concat_axis=0, tiled=True)]
    encoded = encode_rows(fetched, enc_gain)
    key_part = jnp.einsum(
        "osbe,ef->osbf", encoded, key_full, preferred_element_type=jnp.float32
    ).astype(jnp.bfloat16)
    value_part = jnp.einsum(
        "osbe,ef->osbf", encoded, value_full, preferred_element_type=jnp.float32
    ).astype(jnp.bfloat16)
    stacked = jnp.concatenate((key_part, value_part), axis=-1)
    answers = lax.all_to_all(stacked, "nbr", split_axis=0, concat_axis=0, tiled=True)
    gathered = answers.reshape((UNITS,) + answers.shape[2:])[restore]
    kv_rows = gathered.reshape(span_count, UPC * BLOCK, 2 * local_width)
    key_rows = kv_rows[:, :, :local_width]
    value_rows = kv_rows[:, :, local_width:]
    key_rows = key_rows.reshape(span_count, UPC * BLOCK, local_heads, HD)
    value_rows = value_rows.reshape(span_count, UPC * BLOCK, local_heads, HD)
    scores = (
        jnp.einsum("cthd,cjhd->chtj", queries, key_rows, preferred_element_type=jnp.float32)
        * score_scale
    )
    attention = jax.nn.softmax(scores, axis=-1)
    attention_low = attention.astype(jnp.bfloat16)
    mixture = jnp.einsum(
        "chtj,cjhd->cthd", attention_low, value_rows, preferred_element_type=jnp.float32
    )
    mixture = mixture.astype(jnp.bfloat16).reshape(tok_rows, local_width)
    partial_out = jnp.dot(mixture, out_full, preferred_element_type=jnp.float32)
    summed = lax.psum_scatter(partial_out, "mp", scatter_dimension=1, tiled=True)
    output = (hidden.astype(jnp.float32) + summed).astype(jnp.bfloat16)
    grad_mixture = jnp.einsum("td,hd->th", full_grad, out_full, preferred_element_type=jnp.float32)
    grad_mixture = grad_mixture.astype(jnp.bfloat16).reshape(span_count, SPAN, local_heads, HD)
    grad_attention = jnp.einsum(
        "cthd,cjhd->chtj", grad_mixture, value_rows, preferred_element_type=jnp.float32
    )
    grad_scores = (
        attention
        * (grad_attention - jnp.sum(attention * grad_attention, axis=-1, keepdims=True))
        * score_scale
    )
    grad_scores = grad_scores.astype(jnp.bfloat16)
    grad_queries = jnp.einsum(
        "chtj,cjhd->cthd", grad_scores, key_rows, preferred_element_type=jnp.float32
    )
    grad_queries = grad_queries.astype(jnp.bfloat16).reshape(tok_rows, local_width)
    partial_grad = jnp.einsum(
        "th,dh->td", grad_queries, query_full, preferred_element_type=jnp.float32
    )
    grad_sum = lax.psum_scatter(partial_grad, "mp", scatter_dimension=1, tiled=True)
    grad_hidden = (grad_out.astype(jnp.float32) + grad_sum).astype(jnp.bfloat16)
    return (output, grad_hidden)


def solution(mesh):
    in_specs = (
        P(("groups", "dp", "nbr"), "mp"),
        P(("groups", "dp", "nbr"), "mp"),
        P(("groups", "dp", "nbr"), None, None),
        P(),
        P("dp", "mp"),
        P("dp", "mp"),
        P("dp", "mp"),
        P("mp", "dp"),
        P(("groups", "dp", "nbr"), None),
        P(("groups", "dp", "nbr"), None),
    )
    out_specs = (P(("groups", "dp", "nbr"), "mp"), P(("groups", "dp", "nbr"), "mp"))
    sizes = tuple(mesh.shape[a] for a in AXES)
    local = local_plane if sizes == (2, 4, 2, 2) else local_any
    return jax.shard_map(local, mesh=mesh, in_specs=in_specs, out_specs=out_specs, check_vma=False)
```

```python
import math

import jax
import jax.numpy as jnp
from jax import lax
from jax.experimental import pallas as pl
from jax.experimental.pallas import tpu as pltpu
from jax.sharding import PartitionSpec as P

HD = 128
SPAN = 64
BLOCK = 64
UPC = 4
UNITS = 8
AXES = ("groups", "dp", "nbr", "mp")
F32 = jnp.float32
BF16 = jnp.bfloat16


def encode_rows(states, enc_gain):
    widened = states.astype(F32)
    inverse = lax.rsqrt(jnp.mean(widened * widened, axis=-1, keepdims=True) + 1e-06)
    return (widened * inverse * enc_gain).astype(BF16)


def dot(a, b):
    return jnp.dot(a, b, preferred_element_type=F32)


def dot_t(a, b):
    return lax.dot_general(a, b, (((1,), (1,)), ((), ())), preferred_element_type=F32)


CROSSED = (0, 2, 1, 3)
TILE = 16
SCALE = 1.0 / math.sqrt(HD)
SHORT = pl.CostEstimate(flops=1024, bytes_accessed=1024, transcendentals=0)
LONG = pl.CostEstimate(flops=10**11, bytes_accessed=1024, transcendentals=0)


def shape_of(shape, dtype=BF16):
    return jax.ShapeDtypeStruct(shape, dtype)


def kernel_call(body, name, scalars, operands, out_shapes, in_specs):
    whole = lambda a: pl.BlockSpec(a.shape, lambda i, *_, n=len(a.shape): (0,) * n)
    return pl.pallas_call(
        body,
        grid_spec=pltpu.PrefetchScalarGridSpec(
            num_scalar_prefetch=len(scalars),
            grid=(1,),
            in_specs=[sp or whole(a) for sp, a in zip(in_specs, operands)],
            out_specs=[whole(a) for a in out_shapes],
        ),
        out_shape=tuple(out_shapes),
        compiler_params=pltpu.CompilerParams(vmem_limit_bytes=56 << 20),
        cost_estimate=LONG,
        name=name,
    )(*scalars, *operands)


class Copies:
    def __init__(self, sems):
        self.sems, self.used, self.open = sems, 0, {}

    def start(self, name, source, target):
        copy = pltpu.make_async_copy(source, target, self.sems.at[self.used])
        self.used += 1
        copy.start()
        self.open.setdefault(name, []).append(copy)

    def wait(self, *names):
        for name in names:
            for copy in self.open.pop(name):
                copy.wait()


def copy_call(body, name, scalars, operands, out_shapes, scratch, copies, cost=LONG, room=10, far=(), inputs=pl.ANY):
    smem = pl.BlockSpec(memory_space=pltpu.SMEM)
    need = sum(math.prod(a.shape) * jnp.dtype(a.dtype).itemsize for a in scratch)
    return pl.pallas_call(
        body,
        in_specs=[smem] * len(scalars) + [pl.BlockSpec(memory_space=inputs)] * len(operands),
        out_specs=[pl.BlockSpec(memory_space=pltpu.HBM if n in far else pl.ANY) for n in range(len(out_shapes))],
        out_shape=tuple(out_shapes),
        scratch_shapes=[pltpu.VMEM(a.shape, a.dtype) for a in scratch] + [pltpu.SemaphoreType.DMA((copies,))],
        compiler_params=pltpu.CompilerParams(vmem_limit_bytes=need + (room << 20)),
        cost_estimate=cost,
        name=name,
    )(*scalars, *operands)


def after(array, *earlier):
    return lax.optimization_barrier((array, *earlier))[0]


def step_kernel(before, now):
    now[0] = before[0] + 1


def step(*ready):
    smem = pl.BlockSpec(memory_space=pltpu.SMEM)
    return pl.pallas_call(
        step_kernel,
        in_specs=[smem],
        out_specs=smem,
        out_shape=shape_of((1,), jnp.int32),
        compiler_params=pltpu.CompilerParams(has_side_effects=True),
        cost_estimate=LONG,
        name="step",
    )(after(*ready))


def slices_kernel(place, q, k, v, o, out):
    depth, width = q.shape
    rank = k.shape[0]
    out[:rank] = k[...]
    out[rank : 2 * rank] = v[...]
    out[2 * rank : 2 * rank + depth] = q[...]
    for c in range(depth // width):
        at = 2 * rank + depth + c * width
        out[at : at + width] = o[:, c * width : (c + 1) * width]


def projection_slices(chip, qw, kw, vw, ow):
    depth, width, rank = qw.shape[0], qw.shape[1] // 4, kw.shape[0]
    column = lambda i, place: (0, place[0])
    return kernel_call(
        slices_kernel,
        "projection_slices",
        (chip.reshape(1),),
        (qw, kw, vw, ow),
        (shape_of((2 * rank + 2 * depth, width)),),
        [
            pl.BlockSpec((depth, width), column),
            pl.BlockSpec((rank, width), column),
            pl.BlockSpec((rank, width), column),
            pl.BlockSpec((width, depth), lambda i, place: (place[0], 0)),
        ],
    )[0]


def prepare_kernel(core, owners, ids, hid, grad, db, gain, _, near, far):
    rows, half = hid.shape
    blocks, e = db.shape[0] // 2, db.shape[2]
    per = rows // BLOCK
    near[:, :half] = hid[...]
    for ref, which, start in ((near, core[0], half), (far, 1 - core[0], 0)):
        for part in range(blocks // per):
            states = db[pl.ds(which * blocks + part * per, per)].reshape(rows, e)
            ref[:, start + part * e : start + (part + 1) * e] = encode_rows(states, gain[...])
    near[:, near.shape[1] - half :] = grad[...]
    lane = lax.broadcasted_iota(jnp.int32, (rows, 128), 1)
    row = jnp.zeros(lane.shape, jnp.int32)
    for u in range(UNITS):
        at = divmod(u, UPC)
        row = jnp.where(lane == u, owners[at] * 2 * blocks + ids[at], row)
    near[:, near.shape[1] - half - 128 : near.shape[1] - half] = row.astype(F32).astype(BF16)


def prepare(core, owners, ids, hidden, grad, db, gain, earlier):
    rows, half = hidden.shape
    wide = db.shape[0] // 2 * BLOCK // rows * db.shape[2]
    return kernel_call(
        prepare_kernel,
        "prepare",
        (core.reshape(1), owners, ids),
        (hidden, grad, db, gain, earlier),
        (shape_of((rows, half + wide + 128 + half)), shape_of((rows, wide))),
        [None] * 4 + [pl.BlockSpec(memory_space=pl.ANY)],
    )


def rows_of(ref, first, count):
    return ref.at[pl.ds(first, count)]


def take_blocks(idx, kv, span, cols):
    parts = []
    for u in range(UPC):
        row = pl.multiple_of(idx[span, u] * TILE, TILE)
        parts.append(kv[pl.ds(row, BLOCK), cols])
    return jnp.concatenate(parts, axis=0)


def span_rows(n):
    return slice(n * SPAN, (n + 1) * SPAN)


def head_cols(width, h):
    return slice(h * HD, (h + 1) * HD), slice(width + h * HD, width + (h + 1) * HD)


def stage_tokens(copies, name, arrays, target):
    rows, half = arrays[0].shape[0], target.shape[1]
    for slot, a in enumerate(arrays):
        source = a.at[:, pl.ds(0, half)] if a.shape[1] > half else a
        copies.start(name, source, rows_of(target, slot * rows, rows))


def stage_output(copies, name, part, target):
    width = part.shape[1]
    count = target.shape[1] // width
    first = part.shape[0] - count * width
    for c in range(count):
        copies.start(name, rows_of(part, first + c * width, width), target.at[:, pl.ds(c * width, width)])


def project(core, mix, weights, theirs, mine, columns):
    sub, rows = weights.shape[1] // 2, mix.shape[0] // 4
    crossed = jnp.concatenate([mix[s * rows : (s + 1) * rows] for s in CROSSED])
    for ref, tokens, which in ((theirs, crossed, 1 - core), (mine, mix[...], core)):
        cut = pl.ds(pl.multiple_of(which * sub, sub), sub)
        ref[:, columns] = dot(tokens, weights[:, cut]).astype(BF16)


def forward_kernel(src, idx, pos, *refs):
    banks, own, other, parts = refs[:8], refs[:4], refs[8:12], refs[12:16]
    kv_out, mix_out, att_out = refs[16:19]
    states, kvw, kv, near, far, weights, queries, mix, att, sems = refs[19:]
    e, columns = kvw.shape
    rank, rows, wide = e // 4, banks[0].shape[0], states.shape[1]
    half, width = near.shape[1], weights.shape[1]
    depth = weights.shape[0] // 4
    spans = att.shape[0]
    copies = Copies(sems)
    for r, part in enumerate(parts):
        place = pl.multiple_of(src[r] * rank, TILE)
        for c in range(2):
            target = kvw.at[pl.ds(place, rank), pl.ds(c * width, width)]
            copies.start("kvw", rows_of(part, c * rank, rank), target)
    for b, bank in enumerate(banks):
        start = 0 if b == 4 else half
        copies.start(b // 4, bank.at[:, pl.ds(start, wide)], rows_of(states, b * rows, rows))
    for r, part in enumerate(parts):
        place = pl.multiple_of(pos[r] * depth, depth)
        copies.start("query", rows_of(part, 2 * rank, depth), rows_of(weights, place, depth))
    stage_tokens(copies, "near", own, near)
    stage_tokens(copies, "far", other, far)
    copies.wait("kvw")
    for side in range(2):
        copies.wait(side)
        for c in range(wide // e):
            block = states[4 * side * rows : 4 * (side + 1) * rows, c * e : (c + 1) * e]
            at = (8 * c + 4 * side) * rows
            kv[at : at + 4 * rows] = dot(block, kvw[...]).astype(BF16)
    copies.start("out", kv, kv_out)
    copies.wait("query", "near")
    total = dot(near[...], weights[:half])
    copies.wait("far")
    queries[...] = (total + dot(far[...], weights[half:])).astype(BF16)
    todo = [(span_rows(n), n, h, *head_cols(width, h)) for n in range(spans) for h in range(width // HD)]
    scores = [dot_t(queries[rows, kc], take_blocks(idx, kv, n, kc)) * SCALE for rows, n, _, kc, _ in todo]
    scores = [jnp.exp(s - jnp.max(s, axis=-1, keepdims=True)) for s in scores]
    scores = [s * (1.0 / jnp.sum(s, axis=-1, keepdims=True)) for s in scores]
    for s, (_, n, h, _, _) in zip(scores, todo):
        att[n, h] = s
    copies.start("out", att, att_out)
    for s, (rows, n, _, kc, vc) in zip(scores, todo):
        mix[rows, kc] = dot(s.astype(BF16), take_blocks(idx, kv, n, vc)).astype(BF16)
    copies.start("out", mix, mix_out)
    copies.wait("out")


def forward(src, idx, pos, own, far_states, other, parts, half, e, depth):
    rows, width = own[0].shape[0], parts[0].shape[1]
    tokens = 4 * rows
    spans = tokens // SPAN
    wide = far_states.shape[1]
    kv = shape_of((8 * wide // e * rows, 2 * width))
    mix = shape_of((tokens, width))
    att = shape_of((spans, width // HD, SPAN, UPC * BLOCK), F32)
    side = shape_of((tokens, half))
    return copy_call(
        forward_kernel,
        "forward",
        (src, idx, pos),
        (*own, far_states, *other[1:], *other, *parts),
        (kv, mix, att),
        (
            shape_of((8 * rows, wide)),
            shape_of((e, 2 * width)),
            kv,
            side,
            side,
            shape_of((4 * depth, width)),
            mix,
            mix,
            att,
        ),
        31,
        SHORT,
        42,
    )


def output_kernel(core, *refs):
    mix_in, parts = refs[0], refs[1:4]
    theirs_out, mine_out, mix, weights, theirs, mine, sems = refs[4:]
    sub = weights.shape[2] // 2
    copies = Copies(sems)
    copies.start("mix", mix_in, mix)
    for r, part in enumerate(parts):
        stage_output(copies, r, part, weights.at[r])
    copies.wait("mix")
    for r in range(3):
        copies.wait(r)
        project(core[0], mix, weights.at[r], theirs, mine, slice(r * sub, (r + 1) * sub))
    copies.start("out", theirs, theirs_out)
    copies.start("out", mine, mine_out)
    copies.wait("out")


def output_slices(core, mix, parts):
    tokens, width = mix.shape
    depth = parts[0].shape[0]
    out = shape_of((tokens, 3 * depth // 2))
    return copy_call(
        output_kernel,
        "output_slices",
        (core.reshape(1),),
        (mix, *parts),
        (out, out),
        (mix, shape_of((3, width, depth)), out, out),
        3 + 3 * (depth // width),
        far=(0,),
    )


def cotangent_kernel(pos, *refs):
    own, other, parts, gm_out, rest_out = refs[:4], refs[4:8], refs[8:11], refs[11], refs[12]
    grads, weights, gm, sems = refs[13:]
    rows, depth = own[0].shape[0], grads.shape[2]
    copies = Copies(sems)
    for r, part in enumerate(parts):
        stage_output(copies, r, part, weights.at[r])
    for side, arrays in enumerate((own, other)):
        for slot, a in enumerate(arrays):
            for c in range(2):
                target = grads.at[2 * side + c, pl.ds(slot * rows, rows)]
                start = a.shape[1] - 2 * depth + c * depth
                copies.start("grads", a.at[:, pl.ds(start, depth)], target)
    copies.wait("grads")
    copies.start("out", grads.at[pos[3]], rest_out)
    copies.wait(0, 1, 2)
    gm[...] = sum(dot_t(grads[pos[r]], weights[r]) for r in range(3))
    copies.start("out", gm, gm_out)
    copies.wait("out")


def cotangent(pos, own, other, parts):
    tokens, (depth, width) = 4 * own[0].shape[0], parts[0].shape
    gm = shape_of((tokens, width), F32)
    return copy_call(
        cotangent_kernel,
        "cotangent",
        (pos,),
        (*own, *other, *parts),
        (gm, shape_of((tokens, depth))),
        (shape_of((4, tokens, depth)), shape_of((3, width, depth)), gm),
        3 * (depth // width) + 16 + 2,
    )


def late_kernel(core, idx, pos, *refs):
    gm_in, rest_in, part, mix_in, kv_in, att_in, parts, results = *refs[:6], refs[6:10], refs[10:16]
    gmf, rest, wo, mix, kv, att, wq, gm, gq, crossed, wide, narrow, sems = refs[16:]
    width, depth = wq.shape[1], wq.shape[0] // 4
    spans, sub = att.shape[0], depth // 2
    copies = Copies(sems)
    stage_output(copies, "in", part, wo)
    copies.start("in", rest_in, rest)
    copies.start("in", gm_in, gmf)
    copies.start("kv", kv_in, kv)
    copies.start("kv", att_in, att)
    copies.start("mix", mix_in, mix)
    for r, piece in enumerate(parts):
        place = pl.multiple_of(pos[r] * depth, depth)
        copies.start("query", rows_of(piece, parts[0].shape[0] - depth, depth), rows_of(wq, place, depth))
    copies.wait("in")
    gm[...] = (gmf[...] + dot_t(rest[...], wo[...])).astype(BF16)
    copies.wait("kv")
    todo = [(span_rows(n), n, h, *head_cols(width, h)) for n in range(spans) for h in range(width // HD)]
    grads = [dot_t(gm[rows, kc], take_blocks(idx, kv, n, vc)) for rows, n, _, kc, vc in todo]
    inner = [jnp.sum(att[n, h] * g, axis=-1, keepdims=True) for g, (_, n, h, _, _) in zip(grads, todo)]
    grads = [(att[n, h] * (g - a) * SCALE).astype(BF16) for g, a, (_, n, h, _, _) in zip(grads, inner, todo)]
    for g, (rows, n, _, kc, _) in zip(grads, todo):
        slot, within = divmod(n, spans // 4)
        value = dot(g, take_blocks(idx, kv, n, kc)).astype(BF16)
        gq[rows, kc] = value
        crossed[span_rows(CROSSED[slot] * (spans // 4) + within), kc] = value
    copies.wait("mix", "query")
    project(core[0], mix, wo, wide.at[0], wide.at[1], slice(0, sub))
    first = wide.shape[2] - sub
    for n, (source, chunk, side) in enumerate(((crossed, 0, 2), (crossed, 1, 2), (gq, 0, 0), (gq, 1, 0))):
        buffer = (narrow if chunk else wide).at[n // 2]
        start, place = side * depth + chunk * first, 0 if chunk else sub
        for at in range(0, buffer.shape[1] - place, 256):
            value = dot_t(source[...], wq[start + at : start + at + 256])
            buffer[:, place + at : place + at + 256] = value.astype(BF16)
        if n < 2:
            copies.start("out", buffer, results[n])
        else:
            rows = buffer.shape[0] // 2
            for half in range(2):
                copies.start("out", rows_of(buffer, half * rows, rows), results[2 * n - 2 + half])
    copies.wait("out")


def late_slices(core, idx, pos, gm, rest, part, mix, kv, att, parts):
    tokens, width = gm.shape
    depth = part.shape[0]
    wide = shape_of((tokens, depth // 2 + depth * 5 // 4))
    narrow = shape_of((tokens, depth * 3 // 4))
    heads = shape_of((tokens, width))
    return copy_call(
        late_kernel,
        "late_slices",
        (core.reshape(1), idx, pos),
        (gm, rest, part, mix, kv, att, *parts),
        (wide, narrow, *(shape_of((tokens // 2, a.shape[1])) for a in (wide, wide, narrow, narrow))),
        (
            gm,
            rest,
            shape_of((width, depth)),
            mix,
            kv,
            att,
            shape_of((4 * depth, width)),
            heads,
            heads,
            heads,
            shape_of((2, *wide.shape)),
            shape_of((2, *narrow.shape)),
        ),
        depth // width + 5 + 4 + 6,
        room=43,
        far=(0, 1),
    )


def add_kernel(firsts, *refs):
    n = len(firsts)
    arrays, out, held, sems = refs[:n], refs[n], refs[n + 1], refs[n + 2]
    rows = held.shape[1] // 2
    copies = Copies(sems)
    for part in range(2):
        for k, array in enumerate(arrays):
            copies.start(part, rows_of(array, firsts[k] + part * rows, rows), rows_of(held.at[k], part * rows, rows))
    for part in range(2):
        cut = slice(part * rows, (part + 1) * rows)
        copies.wait(part)
        held[0, cut] = sum(held[k, cut].astype(F32) for k in range(n)).astype(BF16)
        copies.start("out", rows_of(held.at[0], part * rows, rows), rows_of(out, part * rows, rows))
    copies.wait("out")


def add_rows(rows, *terms):
    arrays, firsts = zip(*terms)
    shape = (rows, arrays[0].shape[1])
    return copy_call(
        lambda *refs: add_kernel(firsts, *refs),
        "add_rows",
        (),
        arrays,
        (shape_of(shape),),
        (shape_of((len(arrays), *shape)),),
        2 * len(arrays) + 2,
        room=46,
        far=(0,),
        inputs=pltpu.HBM,
    )[0]


def flat(y, z, x, m):
    return ((y * 4 + z) * 2 + x) * 2 + m


def permutation(move):
    pairs = []
    for y in range(2):
        for z in range(4):
            for x in range(2):
                for m in range(2):
                    pairs.append((flat(y, z, x, m), flat(*move(y, z, x, m))))
    return pairs


RING = (0, 1, 3, 2)
NEXT = {RING[i]: RING[(i + 1) % 4] for i in range(4)}
PREV = {RING[i]: RING[(i + 3) % 4] for i in range(4)}
FIRST = permutation(lambda y, z, x, m: (y, z, 1 - x, m) if m == 0 else (1 - y, z, x, m))
SECOND = permutation(lambda y, z, x, m: (1 - y, z, x, m) if m == 0 else (y, z, 1 - x, m))
CORE = permutation(lambda y, z, x, m: (y, z, x, 1 - m))
UP = permutation(lambda y, z, x, m: (y, NEXT[z], x, m))
DOWN = permutation(lambda y, z, x, m: (y, PREV[z], x, m))


def move(array, pairs):
    return lax.ppermute(array, AXES, pairs)


def phase(*arrays):
    return lax.optimization_barrier(arrays)


def local_plane(
    hidden,
    grad_out,
    database,
    enc_gain,
    query_weight,
    key_weight,
    value_weight,
    out_weight,
    block_ids,
    owners,
):
    y, z, x, m = (lax.axis_index(a).astype(jnp.int32) for a in AXES)
    depth, width = query_weight.shape[0], query_weight.shape[1] // 4
    rank = key_weight.shape[0]
    blocks, e = database.shape[0] // 2, database.shape[2]
    rows, half = hidden.shape
    nxt = lax.rem(2 * z + 1 - z // 2, 4)
    sources = (z, 3 - nxt, nxt, 3 - z)

    def codes_of(array):
        start = array.shape[1] - half - 128 if array.shape[1] > 128 else 0
        return array[0, start : start + UNITS].astype(jnp.int32)

    both = projection_slices(y * 2 + x, query_weight, key_weight, value_weight, out_weight)
    early, late = both[: 2 * rank + depth], both[2 * rank + depth :]
    early_up, early_down = move(early, UP), move(both, DOWN)
    he, e_far = prepare(m, owners, block_ids, hidden, grad_out, database, enc_gain, both)
    he_first, he_second = move(he, FIRST), move(he, SECOND)
    places = [s ^ (2 * m) for s in sources]
    turn, zz = after(m, early_up, early_down), after(z, early_up, early_down)
    nxt = lax.rem(2 * zz + 1 - zz // 2, 4)
    sources = (zz, 3 - nxt, nxt, 3 - zz)
    pos, sources = jnp.stack([s ^ (2 * turn) for s in sources]), jnp.stack(sources)
    codes = codes_of(after(he, pos))
    he_first, he_second, codes = phase(he_first, he_second, codes)
    early_far = move(after(early_up, he_first, he_second), UP)
    he_last = move(he_first, SECOND)
    he_two, he_one = move(he_first, CORE), move(he_second, CORE)
    h_zero, g_zero = move(hidden, CORE), move(grad_out, CORE)
    codes = jnp.stack([codes] + [codes_of(a) for a in (he_second, he_first)])
    he_two, he_one, h_zero, g_zero, codes, sources, late = phase(
        he_two, he_one, h_zero, g_zero, codes, sources, late
    )
    early_far = after(early_far, he_two)
    he_last = after(he_last, early_far)
    he_three = move(he_last, CORE)
    late_up = move(after(late, early_far), UP)
    he_own = (he, he_second, he_first, he_last)
    he_other = (h_zero, he_two, he_one, he_three)

    per = rows // BLOCK
    codes = jnp.concatenate((codes, codes_of(he_last)[None]))
    own_of, id_of = codes // (2 * blocks), codes % (2 * blocks)
    slot = jnp.arange(4, dtype=jnp.int32)
    rel_x = own_of ^ x
    rel_y = jnp.where(m == 0, slot % 2, slot // 2)[:, None]
    bank = jnp.where(m == 0, rel_x * 2 + rel_y, rel_y * 2 + rel_x)
    holder, block = id_of // blocks, id_of % blocks
    idx = (block // per * 8 + (holder ^ m) * 4 + bank) * per + block % per
    idx = (idx * (BLOCK // TILE)).reshape(-1, UPC).astype(jnp.int32)

    earlies = (early, early_up, early_down, early_far)
    kv, mixture, attention = forward(sources, idx, pos, he_own, e_far, he_other, earlies, half, e, depth)
    late_up, mixture = phase(late_up, mixture)

    late_far = move(late_up, UP)
    lates = (late, late_up, early_down)
    o_theirs, o_mine = output_slices(m, mixture, lates)

    def slots(array):
        return array.reshape(-1, rows, array.shape[1])

    def begin(mine, theirs):
        return (mine.astype(F32) + theirs[2:].astype(F32)).astype(BF16)

    def carry_on(mine, theirs, first):
        return (mine[1].astype(F32) + theirs[1].astype(F32) + first[1].astype(F32)).astype(BF16)

    def finish(mine, theirs, first, second):
        return sum(a.astype(F32) for a in (mine[0], theirs[0], first[0], second))

    o_theirs, o_mine = slots(move(o_theirs, CORE)), slots(o_mine)
    g_other = (after(g_zero, o_mine), *he_other[1:])
    gm, rest = cotangent(pos, he_own, g_other, lates)
    o_theirs = after(o_theirs, gm)
    o_send = begin(o_mine[2:], o_theirs)
    o_first = move(o_send, FIRST)
    late_far = after(late_far, o_send)
    t0, t1, m0, n0, m1, n1 = late_slices(m, idx, pos, gm, rest, late_far, mixture, kv, attention, earlies)
    t0, t1, o_first = phase(t0, t1, o_first)
    t0, t1 = move(t0, CORE), move(t1, CORE)
    o_next = carry_on(o_mine, o_theirs, o_first)
    o_second = move(o_next, SECOND)
    t0 = after(t0, o_next)
    send0 = add_rows(2 * rows, (n0, 0), (t0, 2 * rows))
    send1 = add_rows(2 * rows, (n1, 0), (after(t1, send0), 2 * rows))
    t0, t1, m0, m1, send0, send1 = (slots(a) for a in (t0, t1, m0, m1, send0, send1))
    first0, first1 = move(send0, FIRST), move(send1, FIRST)
    first0 = after(first0, o_next)
    next0 = carry_on(m0, t0, first0)
    second0 = move(next0, SECOND)
    o_sum = finish(o_mine, o_theirs, o_first, after(o_second, next0))
    first1 = after(first1, next0, o_sum)
    next1 = carry_on(m1, t1, first1)
    second1 = move(next1, SECOND)
    sub = depth // 2
    sum0 = finish(m0, t0, first0, after(second0, next1))

    pieces = [o_sum[:, i * sub : (i + 1) * sub] for i in range(3)] + [sum0[:, :sub]]
    whole = jnp.zeros((4,) + pieces[0].shape, F32)
    for piece, place in zip(pieces, places):
        whole = lax.dynamic_update_slice_in_dim(whole, piece[None], place, 0)
    swapped = move(whole[2:].astype(BF16), CORE).astype(F32)
    low = jnp.where(m == 0, whole[:2], swapped)
    high = jnp.where(m == 0, swapped, whole[:2])
    summed = jnp.concatenate((low[0], high[0], low[1], high[1]), axis=1)
    output = (hidden.astype(F32) + summed).astype(BF16)

    edge = sum0.shape[1] - sub
    rest1 = m1[0].astype(F32) + t1[0].astype(F32) + first1[0].astype(F32)
    base = grad_out.astype(F32) + jnp.concatenate((sum0[:, sub:], rest1), axis=1)
    second1 = after(second1, base, output)
    grad_hidden = (base + jnp.pad(second1.astype(F32), ((0, 0), (edge, 0)))).astype(BF16)
    return (output, grad_hidden)


def local_any(
    hidden,
    grad_out,
    database,
    enc_gain,
    query_weight,
    key_weight,
    value_weight,
    out_weight,
    block_ids,
    owners,
):
    tok_rows = hidden.shape[0]
    span_count = block_ids.shape[0]
    local_width = query_weight.shape[1]
    local_heads = local_width // HD
    owner_count = lax.axis_size("nbr")
    capacity = UNITS // owner_count
    score_scale = 1.0 / math.sqrt(HD)
    full_hidden, full_grad = (
        lax.all_gather(hidden, "mp", axis=1, tiled=True),
        lax.all_gather(grad_out, "mp", axis=1, tiled=True),
    )
    query_full, key_full, value_full, out_full = (
        lax.all_gather(query_weight, "dp", axis=0, tiled=True),
        lax.all_gather(key_weight, "dp", axis=0, tiled=True),
        lax.all_gather(value_weight, "dp", axis=0, tiled=True),
        lax.all_gather(out_weight, "dp", axis=1, tiled=True),
    )
    queries = jnp.dot(full_hidden, query_full, preferred_element_type=jnp.float32)
    queries = queries.astype(jnp.bfloat16).reshape(span_count, SPAN, local_heads, HD)
    owner_flat = owners.reshape(UNITS)
    id_flat = block_ids.reshape(UNITS)
    positions = jnp.arange(UNITS, dtype=jnp.int32)
    send_order = jnp.argsort(owner_flat * UNITS + positions)
    restore = jnp.argsort(send_order)
    requests = id_flat[send_order].reshape(owner_count, capacity)
    fetched = database[lax.all_to_all(requests, "nbr", split_axis=0, concat_axis=0, tiled=True)]
    encoded = encode_rows(fetched, enc_gain)
    key_part = jnp.einsum(
        "osbe,ef->osbf", encoded, key_full, preferred_element_type=jnp.float32
    ).astype(jnp.bfloat16)
    value_part = jnp.einsum(
        "osbe,ef->osbf", encoded, value_full, preferred_element_type=jnp.float32
    ).astype(jnp.bfloat16)
    stacked = jnp.concatenate((key_part, value_part), axis=-1)
    answers = lax.all_to_all(stacked, "nbr", split_axis=0, concat_axis=0, tiled=True)
    gathered = answers.reshape((UNITS,) + answers.shape[2:])[restore]
    kv_rows = gathered.reshape(span_count, UPC * BLOCK, 2 * local_width)
    key_rows = kv_rows[:, :, :local_width]
    value_rows = kv_rows[:, :, local_width:]
    key_rows = key_rows.reshape(span_count, UPC * BLOCK, local_heads, HD)
    value_rows = value_rows.reshape(span_count, UPC * BLOCK, local_heads, HD)
    scores = (
        jnp.einsum("cthd,cjhd->chtj", queries, key_rows, preferred_element_type=jnp.float32)
        * score_scale
    )
    attention = jax.nn.softmax(scores, axis=-1)
    attention_low = attention.astype(jnp.bfloat16)
    mixture = jnp.einsum(
        "chtj,cjhd->cthd", attention_low, value_rows, preferred_element_type=jnp.float32
    )
    mixture = mixture.astype(jnp.bfloat16).reshape(tok_rows, local_width)
    partial_out = jnp.dot(mixture, out_full, preferred_element_type=jnp.float32)
    summed = lax.psum_scatter(partial_out, "mp", scatter_dimension=1, tiled=True)
    output = (hidden.astype(jnp.float32) + summed).astype(jnp.bfloat16)
    grad_mixture = jnp.einsum("td,hd->th", full_grad, out_full, preferred_element_type=jnp.float32)
    grad_mixture = grad_mixture.astype(jnp.bfloat16).reshape(span_count, SPAN, local_heads, HD)
    grad_attention = jnp.einsum(
        "cthd,cjhd->chtj", grad_mixture, value_rows, preferred_element_type=jnp.float32
    )
    grad_scores = (
        attention
        * (grad_attention - jnp.sum(attention * grad_attention, axis=-1, keepdims=True))
        * score_scale
    )
    grad_scores = grad_scores.astype(jnp.bfloat16)
    grad_queries = jnp.einsum(
        "chtj,cjhd->cthd", grad_scores, key_rows, preferred_element_type=jnp.float32
    )
    grad_queries = grad_queries.astype(jnp.bfloat16).reshape(tok_rows, local_width)
    partial_grad = jnp.einsum(
        "th,dh->td", grad_queries, query_full, preferred_element_type=jnp.float32
    )
    grad_sum = lax.psum_scatter(partial_grad, "mp", scatter_dimension=1, tiled=True)
    grad_hidden = (grad_out.astype(jnp.float32) + grad_sum).astype(jnp.bfloat16)
    return (output, grad_hidden)


def solution(mesh):
    in_specs = (
        P(("groups", "dp", "nbr"), "mp"),
        P(("groups", "dp", "nbr"), "mp"),
        P(("groups", "dp", "nbr"), None, None),
        P(),
        P("dp", "mp"),
        P("dp", "mp"),
        P("dp", "mp"),
        P("mp", "dp"),
        P(("groups", "dp", "nbr"), None),
        P(("groups", "dp", "nbr"), None),
    )
    out_specs = (P(("groups", "dp", "nbr"), "mp"), P(("groups", "dp", "nbr"), "mp"))
    sizes = tuple(mesh.shape[a] for a in AXES)
    local = local_plane if sizes == (2, 4, 2, 2) else local_any
    return jax.shard_map(local, mesh=mesh, in_specs=in_specs, out_specs=out_specs, check_vma=False)
```

```python
import math

import jax
import jax.numpy as jnp
from jax import lax
from jax.experimental import pallas as pl
from jax.experimental.pallas import tpu as pltpu
from jax.sharding import PartitionSpec as P

HD = 128
SPAN = 64
BLOCK = 64
UPC = 4
UNITS = 8
AXES = ("groups", "dp", "nbr", "mp")
F32 = jnp.float32
BF16 = jnp.bfloat16


def encode_rows(states, enc_gain):
    widened = states.astype(F32)
    inverse = lax.rsqrt(jnp.mean(widened * widened, axis=-1, keepdims=True) + 1e-06)
    return (widened * inverse * enc_gain).astype(BF16)


def dot(a, b):
    return jnp.dot(a, b, preferred_element_type=F32)


def dot_t(a, b):
    return lax.dot_general(a, b, (((1,), (1,)), ((), ())), preferred_element_type=F32)


CROSSED = (0, 2, 1, 3)
TILE = 16
SCALE = 1.0 / math.sqrt(HD)
SHORT = pl.CostEstimate(flops=1024, bytes_accessed=1024, transcendentals=0)
LONG = pl.CostEstimate(flops=10**11, bytes_accessed=1024, transcendentals=0)


def shape_of(shape, dtype=BF16):
    return jax.ShapeDtypeStruct(shape, dtype)


def kernel_call(body, name, scalars, operands, out_shapes, in_specs):
    whole = lambda a: pl.BlockSpec(a.shape, lambda i, *_, n=len(a.shape): (0,) * n)
    return pl.pallas_call(
        body,
        grid_spec=pltpu.PrefetchScalarGridSpec(
            num_scalar_prefetch=len(scalars),
            grid=(1,),
            in_specs=[sp or whole(a) for sp, a in zip(in_specs, operands)],
            out_specs=[whole(a) for a in out_shapes],
        ),
        out_shape=tuple(out_shapes),
        compiler_params=pltpu.CompilerParams(vmem_limit_bytes=56 << 20),
        cost_estimate=LONG,
        name=name,
    )(*scalars, *operands)


class Copies:
    def __init__(self, sems):
        self.sems, self.used, self.open = sems, 0, {}

    def start(self, name, source, target):
        copy = pltpu.make_async_copy(source, target, self.sems.at[self.used])
        self.used += 1
        copy.start()
        self.open.setdefault(name, []).append(copy)

    def wait(self, *names):
        for name in names:
            for copy in self.open.pop(name):
                copy.wait()


def copy_call(body, name, scalars, operands, out_shapes, scratch, copies, cost=LONG, room=10, far=(), inputs=pl.ANY):
    smem = pl.BlockSpec(memory_space=pltpu.SMEM)
    need = sum(math.prod(a.shape) * jnp.dtype(a.dtype).itemsize for a in scratch)
    return pl.pallas_call(
        body,
        in_specs=[smem] * len(scalars) + [pl.BlockSpec(memory_space=inputs)] * len(operands),
        out_specs=[pl.BlockSpec(memory_space=pltpu.HBM if n in far else pl.ANY) for n in range(len(out_shapes))],
        out_shape=tuple(out_shapes),
        scratch_shapes=[pltpu.VMEM(a.shape, a.dtype) for a in scratch] + [pltpu.SemaphoreType.DMA((copies,))],
        compiler_params=pltpu.CompilerParams(vmem_limit_bytes=need + (room << 20)),
        cost_estimate=cost,
        name=name,
    )(*scalars, *operands)


def after(array, *earlier):
    return lax.optimization_barrier((array, *earlier))[0]


def step_kernel(before, now):
    now[0] = before[0] + 1


def step(*ready):
    smem = pl.BlockSpec(memory_space=pltpu.SMEM)
    return pl.pallas_call(
        step_kernel,
        in_specs=[smem],
        out_specs=smem,
        out_shape=shape_of((1,), jnp.int32),
        compiler_params=pltpu.CompilerParams(has_side_effects=True),
        cost_estimate=LONG,
        name="step",
    )(after(*ready))


def slices_kernel(place, q, k, v, o, out):
    depth, width = q.shape
    rank = k.shape[0]
    out[:rank] = k[...]
    out[rank : 2 * rank] = v[...]
    out[2 * rank : 2 * rank + depth] = q[...]
    for c in range(depth // width):
        at = 2 * rank + depth + c * width
        out[at : at + width] = o[:, c * width : (c + 1) * width]


def projection_slices(chip, qw, kw, vw, ow):
    depth, width, rank = qw.shape[0], qw.shape[1] // 4, kw.shape[0]
    column = lambda i, place: (0, place[0])
    return kernel_call(
        slices_kernel,
        "projection_slices",
        (chip.reshape(1),),
        (qw, kw, vw, ow),
        (shape_of((2 * rank + 2 * depth, width)),),
        [
            pl.BlockSpec((depth, width), column),
            pl.BlockSpec((rank, width), column),
            pl.BlockSpec((rank, width), column),
            pl.BlockSpec((width, depth), lambda i, place: (place[0], 0)),
        ],
    )[0]


def prepare_kernel(core, owners, ids, hid, grad, db, gain, _, near, far):
    rows, half = hid.shape
    blocks, e = db.shape[0] // 2, db.shape[2]
    per = rows // BLOCK
    near[:, :half] = hid[...]
    for ref, which, start in ((near, core[0], half), (far, 1 - core[0], 0)):
        for part in range(blocks // per):
            states = db[pl.ds(which * blocks + part * per, per)].reshape(rows, e)
            ref[:, start + part * e : start + (part + 1) * e] = encode_rows(states, gain[...])
    near[:, near.shape[1] - half :] = grad[...]
    lane = lax.broadcasted_iota(jnp.int32, (rows, 128), 1)
    row = jnp.zeros(lane.shape, jnp.int32)
    for u in range(UNITS):
        at = divmod(u, UPC)
        row = jnp.where(lane == u, owners[at] * 2 * blocks + ids[at], row)
    near[:, near.shape[1] - half - 128 : near.shape[1] - half] = row.astype(F32).astype(BF16)


def prepare(core, owners, ids, hidden, grad, db, gain, earlier):
    rows, half = hidden.shape
    wide = db.shape[0] // 2 * BLOCK // rows * db.shape[2]
    return kernel_call(
        prepare_kernel,
        "prepare",
        (core.reshape(1), owners, ids),
        (hidden, grad, db, gain, earlier),
        (shape_of((rows, half + wide + 128 + half)), shape_of((rows, wide))),
        [None] * 4 + [pl.BlockSpec(memory_space=pl.ANY)],
    )


def rows_of(ref, first, count):
    return ref.at[pl.ds(first, count)]


def take_blocks(idx, kv, span, cols):
    parts = []
    for u in range(UPC):
        row = pl.multiple_of(idx[span, u] * TILE, TILE)
        parts.append(kv[pl.ds(row, BLOCK), cols])
    return jnp.concatenate(parts, axis=0)


def span_rows(n):
    return slice(n * SPAN, (n + 1) * SPAN)


def head_cols(width, h):
    return slice(h * HD, (h + 1) * HD), slice(width + h * HD, width + (h + 1) * HD)


def stage_tokens(copies, name, arrays, target):
    rows, half = arrays[0].shape[0], target.shape[1]
    for slot, a in enumerate(arrays):
        source = a.at[:, pl.ds(0, half)] if a.shape[1] > half else a
        copies.start(name, source, rows_of(target, slot * rows, rows))


def stage_output(copies, name, part, target):
    width = part.shape[1]
    count = target.shape[1] // width
    first = part.shape[0] - count * width
    for c in range(count):
        copies.start(name, rows_of(part, first + c * width, width), target.at[:, pl.ds(c * width, width)])


def project(core, mix, weights, theirs, mine, columns):
    sub, rows = weights.shape[1] // 2, mix.shape[0] // 4
    crossed = jnp.concatenate([mix[s * rows : (s + 1) * rows] for s in CROSSED])
    for ref, tokens, which in ((theirs, crossed, 1 - core), (mine, mix[...], core)):
        cut = pl.ds(pl.multiple_of(which * sub, sub), sub)
        ref[:, columns] = dot(tokens, weights[:, cut]).astype(BF16)


def forward_kernel(src, idx, pos, *refs):
    banks, own, other, parts = refs[:8], refs[:4], refs[8:12], refs[12:16]
    kv_out, mix_out, att_out = refs[16:19]
    states, kvw, kv, near, far, weights, queries, mix, att, sems = refs[19:]
    e, columns = kvw.shape
    rank, rows, wide = e // 4, banks[0].shape[0], states.shape[1]
    half, width = near.shape[1], weights.shape[1]
    depth = weights.shape[0] // 4
    spans = att.shape[0]
    copies = Copies(sems)
    for r, part in enumerate(parts):
        place = pl.multiple_of(src[r] * rank, TILE)
        for c in range(2):
            target = kvw.at[pl.ds(place, rank), pl.ds(c * width, width)]
            copies.start("kvw", rows_of(part, c * rank, rank), target)
    for b, bank in enumerate(banks):
        start = 0 if b == 4 else half
        copies.start(b // 4, bank.at[:, pl.ds(start, wide)], rows_of(states, b * rows, rows))
    for r, part in enumerate(parts):
        place = pl.multiple_of(pos[r] * depth, depth)
        copies.start("query", rows_of(part, 2 * rank, depth), rows_of(weights, place, depth))
    stage_tokens(copies, "near", own, near)
    stage_tokens(copies, "far", other, far)
    copies.wait("kvw")
    for side in range(2):
        copies.wait(side)
        for c in range(wide // e):
            block = states[4 * side * rows : 4 * (side + 1) * rows, c * e : (c + 1) * e]
            at = (8 * c + 4 * side) * rows
            kv[at : at + 4 * rows] = dot(block, kvw[...]).astype(BF16)
    copies.start("out", kv, kv_out)
    copies.wait("query", "near")
    total = dot(near[...], weights[:half])
    copies.wait("far")
    queries[...] = (total + dot(far[...], weights[half:])).astype(BF16)
    todo = [(span_rows(n), n, h, *head_cols(width, h)) for n in range(spans) for h in range(width // HD)]
    scores = [dot_t(queries[rows, kc], take_blocks(idx, kv, n, kc)) * SCALE for rows, n, _, kc, _ in todo]
    scores = [jnp.exp(s - jnp.max(s, axis=-1, keepdims=True)) for s in scores]
    scores = [s * (1.0 / jnp.sum(s, axis=-1, keepdims=True)) for s in scores]
    for s, (_, n, h, _, _) in zip(scores, todo):
        att[n, h] = s
    copies.start("out", att, att_out)
    for s, (rows, n, _, kc, vc) in zip(scores, todo):
        mix[rows, kc] = dot(s.astype(BF16), take_blocks(idx, kv, n, vc)).astype(BF16)
    copies.start("out", mix, mix_out)
    copies.wait("out")


def forward(src, idx, pos, own, far_states, other, parts, half, e, depth):
    rows, width = own[0].shape[0], parts[0].shape[1]
    tokens = 4 * rows
    spans = tokens // SPAN
    wide = far_states.shape[1]
    kv = shape_of((8 * wide // e * rows, 2 * width))
    mix = shape_of((tokens, width))
    att = shape_of((spans, width // HD, SPAN, UPC * BLOCK), F32)
    side = shape_of((tokens, half))
    return copy_call(
        forward_kernel,
        "forward",
        (src, idx, pos),
        (*own, far_states, *other[1:], *other, *parts),
        (kv, mix, att),
        (
            shape_of((8 * rows, wide)),
            shape_of((e, 2 * width)),
            kv,
            side,
            side,
            shape_of((4 * depth, width)),
            mix,
            mix,
            att,
        ),
        31,
        SHORT,
        42,
    )


def output_kernel(core, *refs):
    mix_in, parts = refs[0], refs[1:4]
    theirs_out, mine_out, mix, weights, theirs, mine, sems = refs[4:]
    sub = weights.shape[2] // 2
    copies = Copies(sems)
    copies.start("mix", mix_in, mix)
    for r, part in enumerate(parts):
        stage_output(copies, r, part, weights.at[r])
    copies.wait("mix")
    for r in range(3):
        copies.wait(r)
        project(core[0], mix, weights.at[r], theirs, mine, slice(r * sub, (r + 1) * sub))
    copies.start("out", theirs, theirs_out)
    copies.start("out", mine, mine_out)
    copies.wait("out")


def output_slices(core, mix, parts):
    tokens, width = mix.shape
    depth = parts[0].shape[0]
    out = shape_of((tokens, 3 * depth // 2))
    return copy_call(
        output_kernel,
        "output_slices",
        (core.reshape(1),),
        (mix, *parts),
        (out, out),
        (mix, shape_of((3, width, depth)), out, out),
        3 + 3 * (depth // width),
        far=(0,),
    )


def cotangent_kernel(pos, *refs):
    own, other, parts, gm_out, rest_out = refs[:4], refs[4:8], refs[8:11], refs[11], refs[12]
    grads, weights, gm, sems = refs[13:]
    rows, depth = own[0].shape[0], grads.shape[2]
    copies = Copies(sems)
    for r, part in enumerate(parts):
        stage_output(copies, r, part, weights.at[r])
    for side, arrays in enumerate((own, other)):
        for slot, a in enumerate(arrays):
            for c in range(2):
                target = grads.at[2 * side + c, pl.ds(slot * rows, rows)]
                start = a.shape[1] - 2 * depth + c * depth
                copies.start("grads", a.at[:, pl.ds(start, depth)], target)
    copies.wait("grads")
    copies.start("out", grads.at[pos[3]], rest_out)
    copies.wait(0, 1, 2)
    gm[...] = sum(dot_t(grads[pos[r]], weights[r]) for r in range(3))
    copies.start("out", gm, gm_out)
    copies.wait("out")


def cotangent(pos, own, other, parts):
    tokens, (depth, width) = 4 * own[0].shape[0], parts[0].shape
    gm = shape_of((tokens, width), F32)
    return copy_call(
        cotangent_kernel,
        "cotangent",
        (pos,),
        (*own, *other, *parts),
        (gm, shape_of((tokens, depth))),
        (shape_of((4, tokens, depth)), shape_of((3, width, depth)), gm),
        3 * (depth // width) + 16 + 2,
    )


def late_kernel(core, idx, pos, *refs):
    gm_in, rest_in, part, mix_in, kv_in, att_in, parts, results = *refs[:6], refs[6:10], refs[10:16]
    gmf, rest, wo, mix, kv, att, wq, gm, gq, crossed, wide, narrow, sems = refs[16:]
    width, depth = wq.shape[1], wq.shape[0] // 4
    spans, sub = att.shape[0], depth // 2
    copies = Copies(sems)
    stage_output(copies, "in", part, wo)
    copies.start("in", rest_in, rest)
    copies.start("in", gm_in, gmf)
    copies.start("kv", kv_in, kv)
    copies.start("kv", att_in, att)
    copies.start("mix", mix_in, mix)
    for r, piece in enumerate(parts):
        place = pl.multiple_of(pos[r] * depth, depth)
        copies.start("query", rows_of(piece, parts[0].shape[0] - depth, depth), rows_of(wq, place, depth))
    copies.wait("in")
    gm[...] = (gmf[...] + dot_t(rest[...], wo[...])).astype(BF16)
    copies.wait("kv")
    todo = [(span_rows(n), n, h, *head_cols(width, h)) for n in range(spans) for h in range(width // HD)]
    grads = [dot_t(gm[rows, kc], take_blocks(idx, kv, n, vc)) for rows, n, _, kc, vc in todo]
    inner = [jnp.sum(att[n, h] * g, axis=-1, keepdims=True) for g, (_, n, h, _, _) in zip(grads, todo)]
    grads = [(att[n, h] * (g - a) * SCALE).astype(BF16) for g, a, (_, n, h, _, _) in zip(grads, inner, todo)]
    for g, (rows, n, _, kc, _) in zip(grads, todo):
        slot, within = divmod(n, spans // 4)
        value = dot(g, take_blocks(idx, kv, n, kc)).astype(BF16)
        gq[rows, kc] = value
        crossed[span_rows(CROSSED[slot] * (spans // 4) + within), kc] = value
    copies.wait("mix", "query")
    project(core[0], mix, wo, wide.at[0], wide.at[1], slice(0, sub))
    first = wide.shape[2] - sub
    for n, (source, chunk, side) in enumerate(((crossed, 0, 2), (crossed, 1, 2), (gq, 0, 0), (gq, 1, 0))):
        buffer = (narrow if chunk else wide).at[n // 2]
        start, place = side * depth + chunk * first, 0 if chunk else sub
        for at in range(0, buffer.shape[1] - place, 256):
            value = dot_t(source[...], wq[start + at : start + at + 256])
            buffer[:, place + at : place + at + 256] = value.astype(BF16)
        if n < 2:
            copies.start("out", buffer, results[n])
        else:
            rows = buffer.shape[0] // 2
            for half in range(2):
                copies.start("out", rows_of(buffer, half * rows, rows), results[2 * n - 2 + half])
    copies.wait("out")


def late_slices(core, idx, pos, gm, rest, part, mix, kv, att, parts):
    tokens, width = gm.shape
    depth = part.shape[0]
    wide = shape_of((tokens, depth // 2 + depth))
    narrow = shape_of((tokens, depth))
    heads = shape_of((tokens, width))
    return copy_call(
        late_kernel,
        "late_slices",
        (core.reshape(1), idx, pos),
        (gm, rest, part, mix, kv, att, *parts),
        (wide, narrow, *(shape_of((tokens // 2, a.shape[1])) for a in (wide, wide, narrow, narrow))),
        (
            gm,
            rest,
            shape_of((width, depth)),
            mix,
            kv,
            att,
            shape_of((4 * depth, width)),
            heads,
            heads,
            heads,
            shape_of((2, *wide.shape)),
            shape_of((2, *narrow.shape)),
        ),
        depth // width + 5 + 4 + 6,
        room=43,
        far=(0, 1),
    )


def add_kernel(firsts, *refs):
    n = len(firsts)
    arrays, out, held, sems = refs[:n], refs[n], refs[n + 1], refs[n + 2]
    rows = held.shape[1] // 2
    copies = Copies(sems)
    for part in range(2):
        for k, array in enumerate(arrays):
            copies.start(part, rows_of(array, firsts[k] + part * rows, rows), rows_of(held.at[k], part * rows, rows))
    for part in range(2):
        cut = slice(part * rows, (part + 1) * rows)
        copies.wait(part)
        held[0, cut] = sum(held[k, cut].astype(F32) for k in range(n)).astype(BF16)
        copies.start("out", rows_of(held.at[0], part * rows, rows), rows_of(out, part * rows, rows))
    copies.wait("out")


def add_rows(rows, *terms):
    arrays, firsts = zip(*terms)
    shape = (rows, arrays[0].shape[1])
    return copy_call(
        lambda *refs: add_kernel(firsts, *refs),
        "add_rows",
        (),
        arrays,
        (shape_of(shape),),
        (shape_of((len(arrays), *shape)),),
        2 * len(arrays) + 2,
        room=46,
        far=(0,),
        inputs=pltpu.HBM,
    )[0]


def flat(y, z, x, m):
    return ((y * 4 + z) * 2 + x) * 2 + m


def permutation(move):
    pairs = []
    for y in range(2):
        for z in range(4):
            for x in range(2):
                for m in range(2):
                    pairs.append((flat(y, z, x, m), flat(*move(y, z, x, m))))
    return pairs


RING = (0, 1, 3, 2)
NEXT = {RING[i]: RING[(i + 1) % 4] for i in range(4)}
PREV = {RING[i]: RING[(i + 3) % 4] for i in range(4)}
FIRST = permutation(lambda y, z, x, m: (y, z, 1 - x, m) if m == 0 else (1 - y, z, x, m))
SECOND = permutation(lambda y, z, x, m: (1 - y, z, x, m) if m == 0 else (y, z, 1 - x, m))
CORE = permutation(lambda y, z, x, m: (y, z, x, 1 - m))
UP = permutation(lambda y, z, x, m: (y, NEXT[z], x, m))
DOWN = permutation(lambda y, z, x, m: (y, PREV[z], x, m))


def move(array, pairs):
    return lax.ppermute(array, AXES, pairs)


def phase(*arrays):
    return lax.optimization_barrier(arrays)


def local_plane(
    hidden,
    grad_out,
    database,
    enc_gain,
    query_weight,
    key_weight,
    value_weight,
    out_weight,
    block_ids,
    owners,
):
    y, z, x, m = (lax.axis_index(a).astype(jnp.int32) for a in AXES)
    depth, width = query_weight.shape[0], query_weight.shape[1] // 4
    rank = key_weight.shape[0]
    blocks, e = database.shape[0] // 2, database.shape[2]
    rows, half = hidden.shape
    nxt = lax.rem(2 * z + 1 - z // 2, 4)
    sources = (z, 3 - nxt, nxt, 3 - z)

    def codes_of(array):
        start = array.shape[1] - half - 128 if array.shape[1] > 128 else 0
        return array[0, start : start + UNITS].astype(jnp.int32)

    both = projection_slices(y * 2 + x, query_weight, key_weight, value_weight, out_weight)
    early, late = both[: 2 * rank + depth], both[2 * rank + depth :]
    early_up, early_down = move(early, UP), move(both, DOWN)
    he, e_far = prepare(m, owners, block_ids, hidden, grad_out, database, enc_gain, both)
    he_first, he_second = move(he, FIRST), move(he, SECOND)
    places = [s ^ (2 * m) for s in sources]
    turn, zz = after(m, early_up, early_down), after(z, early_up, early_down)
    nxt = lax.rem(2 * zz + 1 - zz // 2, 4)
    sources = (zz, 3 - nxt, nxt, 3 - zz)
    pos, sources = jnp.stack([s ^ (2 * turn) for s in sources]), jnp.stack(sources)
    codes = codes_of(after(he, pos))
    he_first, he_second, codes = phase(he_first, he_second, codes)
    early_far = move(after(early_up, he_first, he_second), UP)
    he_last = move(he_first, SECOND)
    he_two, he_one = move(he_first, CORE), move(he_second, CORE)
    h_zero, g_zero = move(hidden, CORE), move(grad_out, CORE)
    codes = jnp.stack([codes] + [codes_of(a) for a in (he_second, he_first)])
    he_two, he_one, h_zero, g_zero, codes, sources, late = phase(
        he_two, he_one, h_zero, g_zero, codes, sources, late
    )
    early_far = after(early_far, he_two)
    he_last = after(he_last, early_far)
    he_three = move(he_last, CORE)
    late_up = move(after(late, early_far), UP)
    he_own = (he, he_second, he_first, he_last)
    he_other = (h_zero, he_two, he_one, he_three)

    per = rows // BLOCK
    codes = jnp.concatenate((codes, codes_of(he_last)[None]))
    own_of, id_of = codes // (2 * blocks), codes % (2 * blocks)
    slot = jnp.arange(4, dtype=jnp.int32)
    rel_x = own_of ^ x
    rel_y = jnp.where(m == 0, slot % 2, slot // 2)[:, None]
    bank = jnp.where(m == 0, rel_x * 2 + rel_y, rel_y * 2 + rel_x)
    holder, block = id_of // blocks, id_of % blocks
    idx = (block // per * 8 + (holder ^ m) * 4 + bank) * per + block % per
    idx = (idx * (BLOCK // TILE)).reshape(-1, UPC).astype(jnp.int32)

    earlies = (early, early_up, early_down, early_far)
    kv, mixture, attention = forward(sources, idx, pos, he_own, e_far, he_other, earlies, half, e, depth)
    late_up, mixture = phase(late_up, mixture)

    late_far = move(late_up, UP)
    lates = (late, late_up, early_down)
    o_theirs, o_mine = output_slices(m, mixture, lates)

    def slots(array):
        return array.reshape(-1, rows, array.shape[1])

    def begin(mine, theirs):
        return (mine.astype(F32) + theirs[2:].astype(F32)).astype(BF16)

    def carry_on(mine, theirs, first):
        return (mine[1].astype(F32) + theirs[1].astype(F32) + first[1].astype(F32)).astype(BF16)

    def finish(mine, theirs, first, second):
        return sum(a.astype(F32) for a in (mine[0], theirs[0], first[0], second))

    o_theirs, o_mine = slots(move(o_theirs, CORE)), slots(o_mine)
    g_other = (after(g_zero, o_mine), *he_other[1:])
    gm, rest = cotangent(pos, he_own, g_other, lates)
    o_theirs = after(o_theirs, gm)
    o_send = begin(o_mine[2:], o_theirs)
    o_first = move(o_send, FIRST)
    late_far = after(late_far, o_send)
    t0, t1, m0, n0, m1, n1 = late_slices(m, idx, pos, gm, rest, late_far, mixture, kv, attention, earlies)
    t0, t1, o_first = phase(t0, t1, o_first)
    t0 = move(t0, CORE)
    t1 = move(after(t1, t0), CORE)
    merged = (a.reshape(-1, a.shape[2]) for a in (o_mine, o_theirs, o_first))
    o_next = add_rows(rows, *((a, rows) for a in merged))
    o_second = move(o_next, SECOND)
    t0 = after(t0, o_next)
    send0 = add_rows(2 * rows, (n0, 0), (t0, 2 * rows))
    send1 = add_rows(2 * rows, (n1, 0), (after(t1, send0), 2 * rows))
    t0, t1, m0, m1, send0, send1 = (slots(a) for a in (t0, t1, m0, m1, send0, send1))
    first0, first1 = move(send0, FIRST), move(send1, FIRST)
    first0 = after(first0, o_next)
    next0 = carry_on(m0, t0, first0)
    second0 = move(next0, SECOND)
    o_sum = finish(o_mine, o_theirs, o_first, after(o_second, next0))
    first1 = after(first1, next0, o_sum)
    next1 = carry_on(m1, t1, first1)
    second1 = move(next1, SECOND)
    sub = depth // 2
    sum0 = finish(m0, t0, first0, after(second0, next1))

    pieces = [o_sum[:, i * sub : (i + 1) * sub] for i in range(3)] + [sum0[:, :sub]]
    whole = jnp.zeros((4,) + pieces[0].shape, F32)
    for piece, place in zip(pieces, places):
        whole = lax.dynamic_update_slice_in_dim(whole, piece[None], place, 0)
    swapped = move(whole[2:].astype(BF16), CORE).astype(F32)
    low = jnp.where(m == 0, whole[:2], swapped)
    high = jnp.where(m == 0, swapped, whole[:2])
    summed = jnp.concatenate((low[0], high[0], low[1], high[1]), axis=1)
    output = (hidden.astype(F32) + summed).astype(BF16)

    edge = sum0.shape[1] - sub
    rest1 = m1[0].astype(F32) + t1[0].astype(F32) + first1[0].astype(F32)
    base = grad_out.astype(F32) + jnp.concatenate((sum0[:, sub:], rest1), axis=1)
    second1 = after(second1, base, output)
    grad_hidden = (base + jnp.pad(second1.astype(F32), ((0, 0), (edge, 0)))).astype(BF16)
    return (output, grad_hidden)


def local_any(
    hidden,
    grad_out,
    database,
    enc_gain,
    query_weight,
    key_weight,
    value_weight,
    out_weight,
    block_ids,
    owners,
):
    tok_rows = hidden.shape[0]
    span_count = block_ids.shape[0]
    local_width = query_weight.shape[1]
    local_heads = local_width // HD
    owner_count = lax.axis_size("nbr")
    capacity = UNITS // owner_count
    score_scale = 1.0 / math.sqrt(HD)
    full_hidden, full_grad = (
        lax.all_gather(hidden, "mp", axis=1, tiled=True),
        lax.all_gather(grad_out, "mp", axis=1, tiled=True),
    )
    query_full, key_full, value_full, out_full = (
        lax.all_gather(query_weight, "dp", axis=0, tiled=True),
        lax.all_gather(key_weight, "dp", axis=0, tiled=True),
        lax.all_gather(value_weight, "dp", axis=0, tiled=True),
        lax.all_gather(out_weight, "dp", axis=1, tiled=True),
    )
    queries = jnp.dot(full_hidden, query_full, preferred_element_type=jnp.float32)
    queries = queries.astype(jnp.bfloat16).reshape(span_count, SPAN, local_heads, HD)
    owner_flat = owners.reshape(UNITS)
    id_flat = block_ids.reshape(UNITS)
    positions = jnp.arange(UNITS, dtype=jnp.int32)
    send_order = jnp.argsort(owner_flat * UNITS + positions)
    restore = jnp.argsort(send_order)
    requests = id_flat[send_order].reshape(owner_count, capacity)
    fetched = database[lax.all_to_all(requests, "nbr", split_axis=0, concat_axis=0, tiled=True)]
    encoded = encode_rows(fetched, enc_gain)
    key_part = jnp.einsum(
        "osbe,ef->osbf", encoded, key_full, preferred_element_type=jnp.float32
    ).astype(jnp.bfloat16)
    value_part = jnp.einsum(
        "osbe,ef->osbf", encoded, value_full, preferred_element_type=jnp.float32
    ).astype(jnp.bfloat16)
    stacked = jnp.concatenate((key_part, value_part), axis=-1)
    answers = lax.all_to_all(stacked, "nbr", split_axis=0, concat_axis=0, tiled=True)
    gathered = answers.reshape((UNITS,) + answers.shape[2:])[restore]
    kv_rows = gathered.reshape(span_count, UPC * BLOCK, 2 * local_width)
    key_rows = kv_rows[:, :, :local_width]
    value_rows = kv_rows[:, :, local_width:]
    key_rows = key_rows.reshape(span_count, UPC * BLOCK, local_heads, HD)
    value_rows = value_rows.reshape(span_count, UPC * BLOCK, local_heads, HD)
    scores = (
        jnp.einsum("cthd,cjhd->chtj", queries, key_rows, preferred_element_type=jnp.float32)
        * score_scale
    )
    attention = jax.nn.softmax(scores, axis=-1)
    attention_low = attention.astype(jnp.bfloat16)
    mixture = jnp.einsum(
        "chtj,cjhd->cthd", attention_low, value_rows, preferred_element_type=jnp.float32
    )
    mixture = mixture.astype(jnp.bfloat16).reshape(tok_rows, local_width)
    partial_out = jnp.dot(mixture, out_full, preferred_element_type=jnp.float32)
    summed = lax.psum_scatter(partial_out, "mp", scatter_dimension=1, tiled=True)
    output = (hidden.astype(jnp.float32) + summed).astype(jnp.bfloat16)
    grad_mixture = jnp.einsum("td,hd->th", full_grad, out_full, preferred_element_type=jnp.float32)
    grad_mixture = grad_mixture.astype(jnp.bfloat16).reshape(span_count, SPAN, local_heads, HD)
    grad_attention = jnp.einsum(
        "cthd,cjhd->chtj", grad_mixture, value_rows, preferred_element_type=jnp.float32
    )
    grad_scores = (
        attention
        * (grad_attention - jnp.sum(attention * grad_attention, axis=-1, keepdims=True))
        * score_scale
    )
    grad_scores = grad_scores.astype(jnp.bfloat16)
    grad_queries = jnp.einsum(
        "chtj,cjhd->cthd", grad_scores, key_rows, preferred_element_type=jnp.float32
    )
    grad_queries = grad_queries.astype(jnp.bfloat16).reshape(tok_rows, local_width)
    partial_grad = jnp.einsum(
        "th,dh->td", grad_queries, query_full, preferred_element_type=jnp.float32
    )
    grad_sum = lax.psum_scatter(partial_grad, "mp", scatter_dimension=1, tiled=True)
    grad_hidden = (grad_out.astype(jnp.float32) + grad_sum).astype(jnp.bfloat16)
    return (output, grad_hidden)


def solution(mesh):
    in_specs = (
        P(("groups", "dp", "nbr"), "mp"),
        P(("groups", "dp", "nbr"), "mp"),
        P(("groups", "dp", "nbr"), None, None),
        P(),
        P("dp", "mp"),
        P("dp", "mp"),
        P("dp", "mp"),
        P("mp", "dp"),
        P(("groups", "dp", "nbr"), None),
        P(("groups", "dp", "nbr"), None),
    )
    out_specs = (P(("groups", "dp", "nbr"), "mp"), P(("groups", "dp", "nbr"), "mp"))
    sizes = tuple(mesh.shape[a] for a in AXES)
    local = local_plane if sizes == (2, 4, 2, 2) else local_any
    return jax.shard_map(local, mesh=mesh, in_specs=in_specs, out_specs=out_specs, check_vma=False)
```
